32 devices in a mesh: tm: 8 (over y, x, core), chan: 4 (over z).
Axes of the slice: x: 2, y: 2, z: 4, core: 2. Of those that a mesh axis runs over, the one named last changes fastest.
Arguments:
- record: bfloat16 [8192, 10240], P('tm', 'chan'), may hold values from -6 to 6
- fir_taps: bfloat16 [64], replicated, may hold values from -0.75 to 0.75
- gauge_lag: int32 [10240], P('chan'), may hold values from 1 to 16
- projector: bfloat16 [8192, 128], P('tm'), may hold values from -0.1875 to 0.1875
- compress: float32 [256, 128], replicated, may hold values from -0.5 to 0.5
Outputs:
- sketch: float32 [128, 10240], P('tm', 'chan')
The draws below stay inside these ranges and needn't reach their ends.
Inputs may be any that keep to these rules, and one draw needn't show every extreme that they name: `gauge_lag`: some channel has lag 16.
All inputs are finite; a program needn't handle non-finite values.
Results may differ from the reference program's by a relative error of at most 0.0028.
Values may be sent and summed in bfloat16 or wider, within the bound.
No kernel may reach another device: no remote copies, remote signals or barrier semaphores. Data moves between devices by JAX's collectives and lax.ppermute only.
A program may use at most 64 MiB of HBM per device.

```python
import jax
import jax.numpy as jnp
from jax import lax

CHANNELS = 10240
RANK = 128
TAPS = 64
GAUGE_MAX = 16
K_ITERS = 8
S_DEV = 1024
TIME = 8192
LEVELS = 3
N_TM = 8


def plant(drawn, rng, least, high):
    longest = drawn.shape.index(max(drawn.shape))
    spots = []
    for shift in (0, 1):
        where = [jax.random.randint(jax.random.fold_in(rng, axis), (), 0, length) for axis, length in enumerate(drawn.shape)]
        where[longest] = (where[longest] + shift) % drawn.shape[longest]
        spots.append(tuple(where))
    return drawn.at[spots[0]].set(least).at[spots[1]].set(high)


def steps_of(stream_key, extent, shards, low, top_value):
    def one(dim, blocks):
        draws = jax.random.uniform(jax.random.fold_in(jax.random.fold_in(stream_key, 6), dim), (blocks,), jnp.float32, low / len(shards), top_value / len(shards))
        return jnp.repeat(jnp.exp(draws), extent[dim] // blocks).reshape((-1,) + (1,) * (len(extent) - dim - 1))

    level = one(*shards[0])
    for cut in shards[1:]:
        level = level * one(*cut)
    return level


def centred(stream_key, shape, scale, most, shards=(), kind=jnp.bfloat16):
    level = steps_of(stream_key, shape, shards, -0.22, 0.18) if shards else 1.0
    values = jax.random.normal(stream_key, shape, jnp.float32) * scale * level
    return jnp.minimum(jnp.maximum(values, -most), most).astype(kind)


def setup_inputs(seed: int = 0) -> dict:
    streams_of = jax.random.split(jax.random.key(seed), 6)
    return {
        "record": centred(streams_of[0], (TIME, CHANNELS), 1.0, 6.0, ((0, 8), (1, 4))),
        "fir_taps": centred(streams_of[1], (TAPS,), TAPS ** -0.5, 0.75),
        "gauge_lag": plant(jax.random.randint(streams_of[2], (CHANNELS,), 1, GAUGE_MAX + 1), jax.random.fold_in(streams_of[2], 1), 1, GAUGE_MAX).astype(jnp.int32),
        "projector": centred(streams_of[3], (TIME, RANK), S_DEV ** -0.5, 0.1875, ((0, 8),)),
        "compress": centred(streams_of[4], (2 * RANK, RANK), RANK ** -0.5, 0.5, (), jnp.float32),
    }


def merge_pair(stacked, compress):
    width = stacked.shape[0]
    eye = jnp.eye(width, dtype=jnp.float32)
    gram = jnp.dot(stacked, stacked.T, precision=lax.Precision.HIGHEST, preferred_element_type=jnp.float32)
    mean_level = jnp.trace(gram) / width
    shifted = gram - mean_level * eye
    signed = shifted / jnp.sqrt(jnp.sum(shifted * shifted) + 1e-06)
    for step_index in range(K_ITERS):
        square = jnp.dot(signed, signed, precision=lax.Precision.HIGHEST, preferred_element_type=jnp.float32)
        signed = jnp.dot(signed, 1.5 * eye - 0.5 * square, precision=lax.Precision.HIGHEST, preferred_element_type=jnp.float32)
    filter_mat = 0.5 * (eye + signed)
    mixing = jnp.dot(compress.T, filter_mat, precision=lax.Precision.HIGHEST, preferred_element_type=jnp.float32)
    return jnp.dot(mixing, stacked, precision=lax.Precision.HIGHEST, preferred_element_type=jnp.float32)

def reference(record, fir_taps, gauge_lag, projector, compress):
    halo_rows = TAPS - 1 + GAUGE_MAX
    padded = jnp.concatenate([jnp.zeros((halo_rows, CHANNELS), jnp.bfloat16), record], 0)
    taps_wide = fir_taps.astype(jnp.float32)

    def one_block(block_index):
        start = (block_index * S_DEV).astype(jnp.int32)
        extended = lax.dynamic_slice(padded, (start, jnp.int32(0)), (S_DEV + halo_rows, CHANNELS)).astype(jnp.float32)
        filtered = jnp.zeros((S_DEV + GAUGE_MAX, CHANNELS), jnp.float32)
        for tap_index in range(TAPS):
            first = TAPS - 1 - tap_index
            filtered = filtered + taps_wide[tap_index] * extended[first:first + S_DEV + GAUGE_MAX]
        current = filtered[GAUGE_MAX:]
        lagged = jnp.zeros((S_DEV, CHANNELS), jnp.float32)
        for lag_step in range(1, GAUGE_MAX + 1):
            chosen = (gauge_lag == lag_step).astype(jnp.float32)[None, :]
            lagged = lagged + chosen * filtered[GAUGE_MAX - lag_step:GAUGE_MAX - lag_step + S_DEV]
        strain = (current - lagged).astype(jnp.bfloat16)
        block_proj = lax.dynamic_slice(projector, (start, jnp.int32(0)), (S_DEV, RANK))
        return jnp.dot(block_proj.T, strain, preferred_element_type=jnp.float32)
    sketches = lax.map(one_block, jnp.arange(N_TM, dtype=jnp.int32))
    for depth_level in range(LEVELS):
        count_now = sketches.shape[0]
        pairs = sketches.reshape(count_now // 2, 2 * RANK, CHANNELS)
        sketches = lax.map(lambda stacked: merge_pair(stacked, compress), pairs)
    return sketches[0]
```

```python
import functools

import jax
import jax.numpy as jnp
from jax import lax
from jax.experimental import pallas as pl
from jax.experimental.pallas import tpu as pltpu
from jax.sharding import PartitionSpec as P

TAPS = 64
GAUGE_MAX = 16
K_ITERS = 8
HALO = TAPS + GAUGE_MAX
BLOCK = 128
F32 = jnp.float32
BF16 = jnp.bfloat16


def dot(a, b):
    return jnp.dot(a, b, preferred_element_type=F32)


def dot_nt(a, b):
    return lax.dot_general(a, b, (((1,), (1,)), ((), ())), preferred_element_type=F32)


def split(a):
    high = a.astype(BF16)
    return high, (a - high.astype(F32)).astype(BF16)


def dot3(a, b):
    ah, al = split(a)
    bh, bl = split(b)
    return dot(ah, bh) + (dot(ah, bl) + dot(al, bh))


def tap_matrix(fir_taps):
    row = jnp.arange(BLOCK, dtype=jnp.int32)[:, None]
    col = jnp.arange(BLOCK + TAPS, dtype=jnp.int32)[None, :]
    tap = row + TAPS - col
    padded = jnp.where((tap >= 0) & (tap < TAPS), fir_taps[jnp.clip(tap, 0, TAPS - 1)], 0)
    return padded.astype(BF16)


def front_kernel(record, halo, lag, taps, proj_t, out, filtered, strain):
    rows = record.shape[0]
    cols = record.shape[1]
    filtered[0:GAUGE_MAX, :] = dot(taps[0:GAUGE_MAX, 0:HALO], halo[...])
    for b in range(rows // BLOCK):
        if b == 0:
            seg = jnp.concatenate([halo[GAUGE_MAX:HALO, :], record[0:BLOCK, :]], 0)
        else:
            seg = record[b * BLOCK - TAPS : (b + 1) * BLOCK, :]
        first = GAUGE_MAX + b * BLOCK
        filtered[first : first + BLOCK, :] = dot(taps[...], seg)
    lane = min(128, cols)
    for c in range(0, cols, lane):
        span = slice(c, c + lane)
        shift = GAUGE_MAX - lag[:, span]

        def one(b, carry):
            first = pl.multiple_of(b * BLOCK, BLOCK)
            seg = filtered[pl.ds(first, BLOCK + GAUGE_MAX), span]
            current = seg[GAUGE_MAX:]
            picked = jnp.where((shift & 8) != 0, seg[8:], seg[:-8])
            for step in (4, 2, 1):
                moved = pltpu.roll(picked, picked.shape[0] - step, 0)
                picked = jnp.where((shift & step) != 0, moved, picked)
            strain[pl.ds(first, BLOCK), span] = (current - picked[:BLOCK]).astype(BF16)
            return carry

        lax.fori_loop(0, rows // BLOCK, one, 0)
    out[...] = dot(proj_t[...], strain[...]).astype(BF16)


def front(record, halo, lag, taps, proj_t):
    rows, cols = record.shape
    rank = proj_t.shape[0]
    tile = 256 if cols % 256 == 0 else 128 if cols % 128 == 0 else cols
    whole = lambda a: pl.BlockSpec(a.shape, lambda i: (0, 0))
    return pl.pallas_call(
        front_kernel,
        grid=(cols // tile,),
        in_specs=[
            pl.BlockSpec((rows, tile), lambda i: (0, i)),
            pl.BlockSpec((HALO, tile), lambda i: (0, i)),
            pl.BlockSpec((1, tile), lambda i: (0, i)),
            whole(taps),
            whole(proj_t),
        ],
        out_specs=pl.BlockSpec((rank, tile), lambda i: (0, i)),
        out_shape=jax.ShapeDtypeStruct((rank, cols), BF16),
        scratch_shapes=[
            pltpu.VMEM((rows + GAUGE_MAX, tile), F32),
            pltpu.VMEM((rows, tile), BF16),
        ],
        compiler_params=pltpu.CompilerParams(vmem_limit_bytes=32 * 2**20),
        name="front",
    )(record, halo, lag, taps, proj_t)


def eye_mask(n):
    row = lax.broadcasted_iota(jnp.int32, (n, n), 0)
    col = lax.broadcasted_iota(jnp.int32, (n, n), 1)
    return row == col


def pair_kernel(top, bottom, out):
    rank = top.shape[0]
    a, b = top[...], bottom[...]
    aa, ab, bb = dot_nt(a, a), dot_nt(a, b), dot_nt(b, b)
    diag = eye_mask(rank)
    trace = jnp.sum(jnp.where(diag, aa + bb, 0.0), axis=(0, 1), keepdims=True)
    mean = trace / (2 * rank)
    out[0:rank, :] = (aa - jnp.where(diag, mean, 0.0)).astype(BF16)
    out[rank : 2 * rank, :] = ab.astype(BF16)
    out[2 * rank : 3 * rank, :] = (bb - jnp.where(diag, mean, 0.0)).astype(BF16)
    full = jnp.broadcast_to(mean, (16, rank))
    row = lax.broadcasted_iota(jnp.int32, (16, rank), 0)
    high = full.astype(BF16)
    rest = full - high.astype(F32)
    mid = rest.astype(BF16)
    low = (rest - mid.astype(F32)).astype(BF16)
    zero = jnp.zeros_like(high)
    out[3 * rank :, :] = jnp.where(
        row == 0, high.astype(F32), jnp.where(row == 1, mid.astype(F32), low.astype(F32))
    ).astype(BF16) * jnp.where(row < 3, 1.0, 0.0).astype(BF16) + zero


def pair_gram(top, bottom):
    rank = top.shape[0]
    return pl.pallas_call(
        pair_kernel,
        out_shape=jax.ShapeDtypeStruct((3 * rank + 16, rank), BF16),
        compiler_params=pltpu.CompilerParams(vmem_limit_bytes=32 * 2**20),
        name="pair_gram",
    )(top, bottom)


def cross_kernel(top, bottom, out):
    out[...] = dot_nt(top[...], bottom[...]).astype(out.dtype)


def cross_gram(top, bottom, dtype):
    return pl.pallas_call(
        cross_kernel,
        out_shape=jax.ShapeDtypeStruct((top.shape[0], bottom.shape[0]), dtype),
        compiler_params=pltpu.CompilerParams(vmem_limit_bytes=32 * 2**20),
        name="cross_gram",
    )(top, bottom)


def sign_filter(gram, mean, compress_t, mixing, level):
    size = gram.shape[0]
    eye = jnp.where(eye_mask(size), 1.0, 0.0)
    norm = jnp.sum(gram * gram, axis=(0, 1), keepdims=True) + 1e-6
    z = gram * lax.rsqrt(norm)
    for _ in range(K_ITERS):
        zh, zl = split(z)
        square = dot(zh, zh) + (dot(zh, zl) + dot(zl, zh))
        ph, pl_ = split(1.5 * eye - 0.5 * square)
        z = dot(zh, ph) + (dot(zh, pl_) + dot(zl, ph))
    mix = dot3(compress_t, 0.5 * (eye + z))
    mixing[...] = mix
    if level is not None:
        mh, ml = split(mix)
        gh, gl = split(gram + mean * eye)
        half = dot(mh, gh) + (dot(mh, gl) + dot(ml, gh))
        hh, hl = split(half)
        level[...] = dot_nt(hh, mh) + (dot_nt(hh, ml) + dot_nt(hl, mh))


def first_filter_kernel(count, *refs):
    parts, compress_t, mixing, level = refs[:count], refs[count], refs[count + 1], refs[count + 2]
    total = parts[0][...].astype(F32)
    for part in parts[1:]:
        total = total + part[...].astype(F32)
    rank = total.shape[1]
    aa, ab, bb = total[0:rank], total[rank : 2 * rank], total[2 * rank : 3 * rank]
    mean = total[3 * rank : 3 * rank + 1, 0:1]
    mean = mean + total[3 * rank + 1 : 3 * rank + 2, 0:1] + total[3 * rank + 2 : 3 * rank + 3, 0:1]
    gram = jnp.concatenate(
        [jnp.concatenate([aa, ab], 1), jnp.concatenate([ab.T, bb], 1)], 0
    )
    sign_filter(gram, mean, compress_t[...], mixing, level)


def later_filter_kernel(count, last, *refs):
    parts, top, bottom, compress_t, mixing = refs[:count], *refs[count : count + 4]
    level = None if last else refs[count + 4]
    ab = parts[0][...].astype(F32)
    for part in parts[1:]:
        ab = ab + part[...].astype(F32)
    gram = jnp.concatenate(
        [jnp.concatenate([top[...], ab], 1), jnp.concatenate([ab.T, bottom[...]], 1)], 0
    )
    size = gram.shape[0]
    diag = eye_mask(size)
    mean = jnp.sum(jnp.where(diag, gram, 0.0), axis=(0, 1), keepdims=True) / size
    sign_filter(gram - jnp.where(diag, mean, 0.0), mean, compress_t[...], mixing, level)


def filter_call(kernel, args, rank, last):
    out = [jax.ShapeDtypeStruct((rank, 2 * rank), F32)]
    if not last:
        out.append(jax.ShapeDtypeStruct((rank, rank), F32))
    return pl.pallas_call(
        kernel,
        out_shape=out,
        compiler_params=pltpu.CompilerParams(vmem_limit_bytes=32 * 2**20),
        name="sign_filter",
    )(*args)


def mix_kernel(mixing, top, bottom, out):
    mh, ml = split(mixing[...])
    rank = top.shape[0]
    a, b = top[...], bottom[...]
    total = dot(mh[:, :rank], a) + dot(mh[:, rank:], b)
    total = total + (dot(ml[:, :rank], a) + dot(ml[:, rank:], b))
    out[...] = total.astype(out.dtype)


def mix(mixing, top, bottom, dtype):
    rows = mixing.shape[0]
    cols = top.shape[1]
    tile = next((t for t in (640, 512, 256, 128) if cols % t == 0), cols)
    rank = top.shape[0]
    return pl.pallas_call(
        mix_kernel,
        grid=(cols // tile,),
        in_specs=[
            pl.BlockSpec(mixing.shape, lambda i: (0, 0)),
            pl.BlockSpec((rank, tile), lambda i: (0, i)),
            pl.BlockSpec((rank, tile), lambda i: (0, i)),
        ],
        out_specs=pl.BlockSpec((rows, tile), lambda i: (0, i)),
        out_shape=jax.ShapeDtypeStruct((rows, cols), dtype),
        name="mix",
    )(mixing, top, bottom)


def swap(value, axis, mask):
    count = lax.axis_size(axis)
    return lax.ppermute(value, axis, [(source, source ^ mask) for source in range(count)])


def gather_parts(value, axis):
    count = lax.axis_size(axis)
    if count > 4 or count & (count - 1):
        return [lax.psum(value.astype(F32), axis)]
    return [value] + [swap(value, axis, mask) for mask in range(1, count)]


def on_device(record, fir_taps, gauge_lag, projector, compress):
    rows, cols = record.shape
    rank = projector.shape[1]
    count = lax.axis_size("tm")
    position = lax.axis_index("tm")
    tail = record[rows - HALO :]
    halo = lax.ppermute(tail, "tm", [(source, source + 1) for source in range(count - 1)])
    sketch = front(
        record, halo, gauge_lag[None, :], tap_matrix(fir_taps), projector.T
    )
    compress_t = compress.T
    depths = count.bit_length() - 1
    narrowed = []
    level = None
    for depth in range(depths):
        last = depth == depths - 1
        mask = 2**depth
        lower = position // mask % 2 == 0
        width = sketch.shape[1]
        if depth > 0 and width % 256 == 0:
            bit = position // 2 ** (depth - 1) % 2
            sketch = jnp.where(bit == 0, sketch[:, : width // 2], sketch[:, width // 2 :])
            narrowed.append(depth - 1)
        other = swap(sketch, "tm", mask)
        top = jnp.where(lower, sketch, other)
        bottom = jnp.where(lower, other, sketch)
        if depth == 0:
            parts = gather_parts(pair_gram(top, bottom), "chan")
            results = filter_call(
                functools.partial(first_filter_kernel, len(parts)), parts + [compress_t], rank, False
            )
        else:
            other_level = swap(level, "tm", mask)
            part = cross_gram(top, bottom, BF16)
            for bit in narrowed:
                part = (part.astype(F32) + swap(part, "tm", 2**bit).astype(F32)).astype(BF16)
            parts = gather_parts(part, "chan")
            args = parts + [
                jnp.where(lower, level, other_level),
                jnp.where(lower, other_level, level),
                compress_t,
            ]
            results = filter_call(
                functools.partial(later_filter_kernel, len(parts), last), args, rank, last
            )
        mixing = results[0]
        level = None if last else results[1]
        if not last:
            sketch = mix(mixing, top, bottom, BF16)
    share = rank // count
    span = 2 ** len(narrowed)
    assert narrowed == list(range(len(narrowed)))
    start = position // span * span * share
    chosen = lax.dynamic_slice_in_dim(mixing, start, span * share, 0)
    result = mix(chosen, top, bottom, F32)
    if span > 1:
        groups = [list(range(g, g + span)) for g in range(0, count, span)]
        pieces = lax.all_to_all(
            result.reshape(span, share, result.shape[1]), "tm", 0, 0, axis_index_groups=groups
        )
        order = [
            sum(((part >> (len(narrowed) - 1 - bit)) & 1) << bit for bit in range(len(narrowed)))
            for part in range(span)
        ]
        result = jnp.concatenate([pieces[piece] for piece in order], 1)
    return result


def solution(mesh):
    return jax.shard_map(
        on_device,
        mesh=mesh,
        in_specs=(P("tm", "chan"), P(), P("chan"), P("tm", None), P()),
        out_specs=P("tm", "chan"),
        check_vma=False,
    )
```

```python
import functools

import jax
import jax.numpy as jnp
from jax import lax
from jax.experimental import pallas as pl
from jax.experimental.pallas import tpu as pltpu
from jax.sharding import PartitionSpec as P

TAPS = 64
GAUGE_MAX = 16
K_ITERS = 8
HALO = TAPS + GAUGE_MAX
BLOCK = 128
EXTRA = 16
F32 = jnp.float32
BF16 = jnp.bfloat16
ANY = pl.BlockSpec(memory_space=pl.ANY)
SMEM = pl.BlockSpec(memory_space=pltpu.SMEM)
VMEM = pl.BlockSpec(memory_space=pltpu.VMEM)
PARAMS = pltpu.CompilerParams(vmem_limit_bytes=40 * 2**20)


def dot(a, b):
    return jnp.dot(a, b, preferred_element_type=F32)


def dot_nt(a, b):
    return lax.dot_general(a, b, (((1,), (1,)), ((), ())), preferred_element_type=F32)


def split(a):
    high = a.astype(BF16)
    return high, (a - high.astype(F32)).astype(BF16)


def dot3(a, b):
    ah, al = split(a)
    bh, bl = split(b)
    return dot(ah, bh) + (dot(ah, bl) + dot(al, bh))


def dot3_nt(a, b):
    ah, al = split(a)
    bh, bl = split(b)
    return dot_nt(ah, bh) + (dot_nt(ah, bl) + dot_nt(al, bh))


def eye_mask(n):
    row = lax.broadcasted_iota(jnp.int32, (n, n), 0)
    col = lax.broadcasted_iota(jnp.int32, (n, n), 1)
    return row == col


def front_kernel(record, halo, lag, taps, projector, out, band, proj_t):
    rows = record.shape[0]
    cols = record.shape[1]

    @pl.when(pl.program_id(0) == 0)
    def _():
        line = jnp.broadcast_to(taps[...], (BLOCK, taps.shape[1]))
        rolled = pltpu.roll(line, 0, 1, stride=1, stride_axis=0)
        band[...] = rolled[:, : BLOCK + TAPS].astype(BF16)
        proj_t[...] = projector[...].astype(F32).T.astype(BF16)

    lane = min(128, cols)
    before = dot(band[0:GAUGE_MAX, 0:HALO], halo[...])
    total = jnp.zeros(out.shape, F32)
    for b in range(rows // BLOCK):
        if b == 0:
            segment = jnp.concatenate([halo[GAUGE_MAX:HALO, :], record[0:BLOCK, :]], 0)
        else:
            segment = record[b * BLOCK - TAPS : (b + 1) * BLOCK, :]
        current = dot(band[...], segment)
        parts = []
        for c in range(0, cols, lane):
            span = slice(c, c + lane)
            shift = GAUGE_MAX - lag[:, span]
            here = current[:, span]
            wide = jnp.concatenate([before[:, span], here], 0)
            picked = jnp.where((shift & 8) != 0, wide[8:], wide[:-8])
            for step in (4, 2, 1):
                moved = pltpu.roll(picked, picked.shape[0] - step, 0)
                picked = jnp.where((shift & step) != 0, moved, picked)
            parts.append((here - picked[:BLOCK]).astype(BF16))
        strain = jnp.concatenate(parts, 1) if len(parts) > 1 else parts[0]
        total = total + dot(proj_t[:, b * BLOCK : (b + 1) * BLOCK], strain)
        before = current[BLOCK - GAUGE_MAX :]
    out[...] = total.astype(BF16)


def front(record, halo, lag, taps, projector):
    rows, cols = record.shape
    rank = projector.shape[1]
    tile = next((t for t in (512, 640, 256, 128) if cols % t == 0), cols)
    whole = lambda a: pl.BlockSpec(a.shape, lambda i: (0, 0))
    return pl.pallas_call(
        front_kernel,
        grid=(cols // tile,),
        in_specs=[
            pl.BlockSpec((rows, tile), lambda i: (0, i)),
            pl.BlockSpec((HALO, tile), lambda i: (0, i)),
            pl.BlockSpec((1, tile), lambda i: (0, i)),
            whole(taps),
            whole(projector),
        ],
        out_specs=pl.BlockSpec((rank, tile), lambda i: (0, i)),
        out_shape=jax.ShapeDtypeStruct((rank, cols), BF16),
        scratch_shapes=[
            pltpu.VMEM((BLOCK, BLOCK + TAPS), BF16),
            pltpu.VMEM((rank, rows), BF16),
        ],
        compiler_params=PARAMS,
        name="front",
    )(record, halo, lag, taps, projector)


def pair_kernel(own, other, out):
    rank = own.shape[0]
    a, b = own[...], other[...]
    aa, ab, bb = dot_nt(a, a), dot_nt(a, b), dot_nt(b, b)
    diag = eye_mask(rank)
    trace = jnp.sum(jnp.where(diag, aa + bb, 0.0), axis=(0, 1), keepdims=True)
    mean = trace / (2 * rank)
    aa = aa - jnp.where(diag, mean, 0.0)
    bb = bb - jnp.where(diag, mean, 0.0)
    row = lax.broadcasted_iota(jnp.int32, (rank, rank), 0)
    col = lax.broadcasted_iota(jnp.int32, (rank, rank), 1)
    out[0:rank, :] = jnp.where(row <= col, aa, bb).astype(BF16)
    out[rank : 2 * rank, :] = ab.astype(BF16)
    bottom = jnp.sum(jnp.where(diag, bb, 0.0), axis=0, keepdims=True)
    full = jnp.broadcast_to(mean, (EXTRA, rank))
    high = full.astype(BF16).astype(F32)
    mid = (full - high).astype(BF16).astype(F32)
    low = full - high - mid
    line = lax.broadcasted_iota(jnp.int32, (EXTRA, rank), 0)
    extra = jnp.where(line == 0, high, jnp.where(line == 1, mid, jnp.where(line == 2, low, 0.0)))
    out[2 * rank :, :] = jnp.where(line == 3, jnp.broadcast_to(bottom, (EXTRA, rank)), extra).astype(
        BF16
    )


def pair_gram(own, other):
    rank = own.shape[0]
    return pl.pallas_call(
        pair_kernel,
        out_shape=jax.ShapeDtypeStruct((2 * rank + EXTRA, rank), BF16),
        compiler_params=PARAMS,
        name="pair_gram",
    )(own, other)


def cross_kernel(own, other, out):
    out[...] = dot_nt(own[...], other[...]).astype(out.dtype)


def cross_gram(own, other):
    return pl.pallas_call(
        cross_kernel,
        out_shape=jax.ShapeDtypeStruct((own.shape[0], other.shape[0]), BF16),
        compiler_params=PARAMS,
        name="cross_gram",
    )(own, other)


def summed(parts):
    total = parts[0][...].astype(F32)
    for part in parts[1:]:
        total = total + part[...].astype(F32)
    return total


def square_of(aa, ab, bb):
    return jnp.concatenate(
        [jnp.concatenate([aa, ab], 1), jnp.concatenate([ab.T, bb], 1)], 0
    )


def first_gram(parts):
    total = summed(parts)
    rank = total.shape[1]
    both = total[0:rank]
    ab = total[rank : 2 * rank]
    extra = total[2 * rank :]
    mean = extra[0:1, 0:1] + extra[1:2, 0:1] + extra[2:3, 0:1]
    row = lax.broadcasted_iota(jnp.int32, (rank, rank), 0)
    col = lax.broadcasted_iota(jnp.int32, (rank, rank), 1)
    turned = both.T
    aa = jnp.where(row <= col, both, turned)
    bb = jnp.where(row > col, both, jnp.where(row < col, turned, extra[3:4, :]))
    return square_of(aa, ab, bb), mean


def later_gram(parts, own_level, other_level):
    gram = square_of(own_level[...], summed(parts), other_level[...])
    diag = eye_mask(gram.shape[0])
    mean = jnp.sum(jnp.where(diag, gram, 0.0), axis=(0, 1), keepdims=True) / gram.shape[0]
    return gram - jnp.where(diag, mean, 0.0), mean


def filter_kernel(count, first, last, *refs):
    parts, refs = refs[:count], refs[count:]
    if first:
        levels = ()
    else:
        levels, refs = refs[:2], refs[2:]
    compress_t, offset, own, other, refs = *refs[:4], refs[4:]
    if last:
        sketch, pair, sems = refs
    else:
        sketch, level, pair, sems = refs
    rank, width = own.shape[0], pair.shape[1]
    start = pl.multiple_of(offset[0], 128) if width % 128 == 0 else 0
    copies = [
        pltpu.make_async_copy(
            source.at[:, pl.ds(start, width)] if width < own.shape[1] else source,
            pair.at[slice(i * rank, (i + 1) * rank)],
            sems.at[i],
        )
        for i, source in enumerate((own, other))
    ]
    for copy in copies:
        copy.start()
    gram, mean = first_gram(parts) if first else later_gram(parts, *levels)
    size = gram.shape[0]
    eye = jnp.where(eye_mask(size), 1.0, 0.0)
    z = gram * lax.rsqrt(jnp.sum(gram * gram, axis=(0, 1), keepdims=True) + 1e-6)
    for _ in range(K_ITERS):
        zh, zl = split(z)
        square = dot(zh, zh) + (dot(zh, zl) + dot(zl, zh))
        ph, low = split(1.5 * eye - 0.5 * square)
        z = dot(zh, ph) + (dot(zh, low) + dot(zl, ph))
    mixing = dot3(compress_t[...], 0.5 * (eye + z))
    for copy in copies:
        copy.wait()
    high, low = split(mixing)
    both = jnp.concatenate([high, low], 0)
    rows = mixing.shape[0]
    tile = next((t for t in (640, 512, 256, 128) if width % t == 0), width)
    for c in range(0, width, tile):
        wide = dot(both, pair[:, c : c + tile])
        sketch[:, c : c + tile] = (wide[:rows] + wide[rows:]).astype(sketch.dtype)
    if not last:
        level[...] = dot3_nt(dot3(mixing, gram + mean * eye), mixing)


def filter_call(parts, levels, compress_t, offset, own, other, width, first, last):
    rank = own.shape[0]
    rows = compress_t.shape[0]
    out = [jax.ShapeDtypeStruct((rows, width), F32 if last else BF16)]
    if not last:
        out.append(jax.ShapeDtypeStruct((rank, rank), F32))
    args = [*parts, *levels, compress_t]
    return pl.pallas_call(
        functools.partial(filter_kernel, len(parts), first, last),
        in_specs=[VMEM] * len(args) + [SMEM, ANY, ANY],
        out_shape=out,
        scratch_shapes=[pltpu.VMEM((2 * rank, width), BF16), pltpu.SemaphoreType.DMA((2,))],
        compiler_params=PARAMS,
        name="sign_filter",
    )(*args, offset, own, other)


def swap(value, axis, mask):
    count = lax.axis_size(axis)
    return lax.ppermute(value, axis, [(source, source ^ mask) for source in range(count)])


def gather_parts(value, axis):
    count = lax.axis_size(axis)
    if count > 4 or count & (count - 1):
        return [lax.psum(value.astype(F32), axis)]
    return [value] + [swap(value, axis, mask) for mask in range(1, count)]


def join_kernel(offsets, *refs):
    out = refs[-1]
    width = refs[0].shape[1]
    for i, piece in enumerate(refs[:-1]):
        out[:, pl.ds(pl.multiple_of(offsets[i], 128), width)] = piece[...]


def join(offsets, pieces):
    share, width = pieces[0].shape
    return pl.pallas_call(
        join_kernel,
        in_specs=[SMEM] + [VMEM] * len(pieces),
        out_shape=jax.ShapeDtypeStruct((share, width * len(pieces)), F32),
        name="join",
    )(offsets, *pieces)


def on_device(record, fir_taps, gauge_lag, projector, compress):
    rows, cols = record.shape
    rank = projector.shape[1]
    count = lax.axis_size("tm")
    position = lax.axis_index("tm")
    depths = count.bit_length() - 1
    share = rank // count
    halo = lax.ppermute(
        record[rows - HALO :], "tm", [(source, source + 1) for source in range(count - 1)]
    )
    taps = jnp.pad(fir_taps.astype(F32)[::-1], (1, 2 * BLOCK - TAPS - 1))[None, :]
    sketch = front(record, halo, gauge_lag[None, :], taps, projector)

    widths = []
    width = cols
    for depth in range(1, depths):
        if width % 256 == 0:
            width //= 2
        widths.append(width)
    narrowed = [depth for depth in range(depths - 1) if widths[depth] < ([cols] + widths)[depth]]
    assert narrowed == list(range(len(narrowed)))
    span = 2 ** len(narrowed)

    def bit_of(where, bit):
        return where // 2**bit % 2

    compress_t = compress.T
    flipped = jnp.concatenate([compress_t[:, rank:], compress_t[:, :rank]], 1)

    level = None
    for depth in range(depths):
        first, last = depth == 0, depth == depths - 1
        mask = 2**depth
        weights = jnp.where(bit_of(position, depth) == 0, compress_t, flipped)
        if last:
            weights = jnp.concatenate(
                [
                    lax.dynamic_slice_in_dim(weights, (position ^ part) * share, share, 0)
                    for part in range(span)
                ],
                0,
            )
        here = sketch.shape[1]
        narrow = not last and widths[depth] < here
        offset = bit_of(position, depth) * (here // 2) if narrow else jnp.int32(0)
        offset = jnp.reshape(offset, (1,)).astype(jnp.int32)
        other = swap(sketch, "tm", mask)
        if first:
            parts = gather_parts(pair_gram(sketch, other), "chan")
            levels = []
        else:
            levels = [level, swap(level, "tm", mask)]
            part = cross_gram(sketch, other)
            for bit in [b for b in narrowed if b < depth]:
                part = (part.astype(F32) + swap(part, "tm", 2**bit).astype(F32)).astype(BF16)
            parts = gather_parts(part, "chan")
        results = filter_call(
            parts, levels, weights, offset, sketch, other, here if last else widths[depth], first, last
        )
        sketch = results[0]
        level = None if last else results[1]
    if span == 1:
        return sketch
    width = sketch.shape[1]
    pieces = [sketch[:share]] + [
        swap(sketch[part * share : (part + 1) * share], "tm", part) for part in range(1, span)
    ]
    offsets = []
    for part in range(span):
        source = position ^ part
        offsets.append(sum(bit_of(source, bit) * (cols >> (bit + 1)) for bit in narrowed))
    return join(jnp.stack(offsets).astype(jnp.int32), pieces)


def solution(mesh):
    return jax.shard_map(
        on_device,
        mesh=mesh,
        in_specs=(P("tm", "chan"), P(), P("chan"), P("tm", None), P()),
        out_specs=P("tm", "chan"),
        check_vma=False,
    )
```

```python
import functools

import jax
import jax.numpy as jnp
from jax import lax
from jax.experimental import pallas as pl
from jax.experimental.pallas import tpu as pltpu
from jax.sharding import PartitionSpec as P

TAPS = 64
GAUGE_MAX = 16
K_ITERS = 8
HALO = TAPS + GAUGE_MAX
BLOCK = 192
CHUNK = 256
EXTRA = 16
F32 = jnp.float32
BF16 = jnp.bfloat16
ANY = pl.BlockSpec(memory_space=pl.ANY)
SMEM = pl.BlockSpec(memory_space=pltpu.SMEM)
VMEM = pl.BlockSpec(memory_space=pltpu.VMEM)
PARAMS = pltpu.CompilerParams(vmem_limit_bytes=40 * 2**20)


def dot(a, b):
    return jnp.dot(a, b, preferred_element_type=F32)


def dot_nt(a, b):
    return lax.dot_general(a, b, (((1,), (1,)), ((), ())), preferred_element_type=F32)


def split(a):
    high = a.astype(BF16)
    return high, (a - high.astype(F32)).astype(BF16)


def dot3(a, b):
    ah, al = split(a)
    bh, bl = split(b)
    return dot(ah, bh) + (dot(ah, bl) + dot(al, bh))


def dot3_nt(a, b):
    ah, al = split(a)
    bh, bl = split(b)
    return dot_nt(ah, bh) + (dot_nt(ah, bl) + dot_nt(al, bh))


def eye_mask(n):
    row = lax.broadcasted_iota(jnp.int32, (n, n), 0)
    col = lax.broadcasted_iota(jnp.int32, (n, n), 1)
    return row == col


def front_kernel(record, halo, lag, taps, projector, out, band, proj_t, strain):
    rows = record.shape[0]
    cols = record.shape[1]

    @pl.when(pl.program_id(0) == 0)
    def _():
        line = jnp.broadcast_to(taps[...], (BLOCK, taps.shape[1]))
        band[...] = pltpu.roll(line, 0, 1, stride=1, stride_axis=0).astype(BF16)
        proj_t[...] = projector[...].astype(F32).T.astype(BF16)

    lane = min(128, cols)
    before = dot(band[0:GAUGE_MAX, 0:HALO], halo[...])
    total = jnp.zeros(out.shape, F32)
    used = 0
    for first in range(0, rows, BLOCK):
        size = min(BLOCK, rows - first)
        if first == 0:
            segment = jnp.concatenate([halo[GAUGE_MAX:HALO, :], record[0:size, :]], 0)
        else:
            segment = record[first - TAPS : first + size, :]
        current = dot(band[:size, : size + TAPS], segment)
        for c in range(0, cols, lane):
            span = slice(c, c + lane)
            shift = GAUGE_MAX - lag[:, span]
            here = current[:, span]
            wide = jnp.concatenate([before[:, span], here], 0)
            picked = jnp.where((shift & 8) != 0, wide[8:], wide[:-8])
            for step in (4, 2, 1):
                moved = pltpu.roll(picked, picked.shape[0] - step, 0)
                picked = jnp.where((shift & step) != 0, moved, picked)
            strain[first : first + size, span] = (here - picked[:size]).astype(BF16)
        before = current[size - GAUGE_MAX :]
        while used < rows and min(used + CHUNK, rows) <= first + size:
            part = slice(used, min(used + CHUNK, rows))
            total = total + dot(proj_t[:, part], strain[part, :])
            used = part.stop
    out[...] = total.astype(BF16)


def front(record, halo, lag, taps, projector):
    rows, cols = record.shape
    rank = projector.shape[1]
    tile = next((t for t in (512, 640, 256, 128) if cols % t == 0), cols)
    whole = lambda a: pl.BlockSpec(a.shape, lambda i: (0, 0))
    return pl.pallas_call(
        front_kernel,
        grid=(cols // tile,),
        in_specs=[
            pl.BlockSpec((rows, tile), lambda i: (0, i)),
            pl.BlockSpec((HALO, tile), lambda i: (0, i)),
            pl.BlockSpec((1, tile), lambda i: (0, i)),
            whole(taps),
            whole(projector),
        ],
        out_specs=pl.BlockSpec((rank, tile), lambda i: (0, i)),
        out_shape=jax.ShapeDtypeStruct((rank, cols), BF16),
        scratch_shapes=[
            pltpu.VMEM((BLOCK, BLOCK + TAPS), BF16),
            pltpu.VMEM((rank, rows), BF16),
            pltpu.VMEM((rows, tile), BF16),
        ],
        compiler_params=pltpu.CompilerParams(vmem_limit_bytes=58 * 2**20),
        name="front",
    )(record, halo, lag, taps, projector)


def pair_kernel(own, other, out):
    rank = own.shape[0]
    a, b = own[...], other[...]
    aa, ab, bb = dot_nt(a, a), dot_nt(a, b), dot_nt(b, b)
    diag = eye_mask(rank)
    trace = jnp.sum(jnp.where(diag, aa + bb, 0.0), axis=(0, 1), keepdims=True)
    mean = trace / (2 * rank)
    aa = aa - jnp.where(diag, mean, 0.0)
    bb = bb - jnp.where(diag, mean, 0.0)
    row = lax.broadcasted_iota(jnp.int32, (rank, rank), 0)
    col = lax.broadcasted_iota(jnp.int32, (rank, rank), 1)
    out[0:rank, :] = jnp.where(row <= col, aa, bb).astype(BF16)
    out[rank : 2 * rank, :] = ab.astype(BF16)
    bottom = jnp.sum(jnp.where(diag, bb, 0.0), axis=0, keepdims=True)
    full = jnp.broadcast_to(mean, (EXTRA, rank))
    high = full.astype(BF16).astype(F32)
    mid = (full - high).astype(BF16).astype(F32)
    low = full - high - mid
    line = lax.broadcasted_iota(jnp.int32, (EXTRA, rank), 0)
    extra = jnp.where(line == 0, high, jnp.where(line == 1, mid, jnp.where(line == 2, low, 0.0)))
    out[2 * rank :, :] = jnp.where(line == 3, jnp.broadcast_to(bottom, (EXTRA, rank)), extra).astype(
        BF16
    )


def pair_gram(own, other):
    rank = own.shape[0]
    return pl.pallas_call(
        pair_kernel,
        out_shape=jax.ShapeDtypeStruct((2 * rank + EXTRA, rank), BF16),
        compiler_params=PARAMS,
        name="pair_gram",
    )(own, other)


def ahead_kernel(own, sibling, partner, out):
    rank = own.shape[0]
    there = partner[...]
    out[0:rank, :] = dot_nt(own[...], there).astype(out.dtype)
    out[rank:, :] = dot_nt(sibling[...], there).astype(out.dtype)


def ahead_gram(own, sibling, partner):
    rank = own.shape[0]
    return pl.pallas_call(
        ahead_kernel,
        out_shape=jax.ShapeDtypeStruct((2 * rank, rank), BF16),
        compiler_params=PARAMS,
        name="ahead_gram",
    )(own, sibling, partner)


def summed(parts):
    total = parts[0][...].astype(F32)
    for part in parts[1:]:
        total = total + part[...].astype(F32)
    return total


def square_of(aa, ab, bb):
    return jnp.concatenate(
        [jnp.concatenate([aa, ab], 1), jnp.concatenate([ab.T, bb], 1)], 0
    )


def first_gram(parts):
    total = summed(parts)
    rank = total.shape[1]
    both = total[0:rank]
    ab = total[rank : 2 * rank]
    extra = total[2 * rank :]
    mean = extra[0:1, 0:1] + extra[1:2, 0:1] + extra[2:3, 0:1]
    row = lax.broadcasted_iota(jnp.int32, (rank, rank), 0)
    col = lax.broadcasted_iota(jnp.int32, (rank, rank), 1)
    turned = both.T
    aa = jnp.where(row <= col, both, turned)
    bb = jnp.where(row > col, both, jnp.where(row < col, turned, extra[3:4, :]))
    return square_of(aa, ab, bb), mean


def later_gram(own_mix, own_level, packed, ahead, sibling_ahead):
    rank = own_mix.shape[0]
    mine, theirs = ahead[...], sibling_ahead[...]
    cross = jnp.concatenate(
        [
            jnp.concatenate([mine[:rank], theirs[rank:]], 1),
            jnp.concatenate([mine[rank:], theirs[:rank]], 1),
        ],
        0,
    )
    high, low = split(own_mix[...])
    half = dot(high, cross) + dot(low, cross)
    high, low = split(half)
    other_mix = packed[:, : 2 * rank]
    ab = dot_nt(high, other_mix) + dot_nt(low, other_mix)
    other_level = packed[:, 2 * rank : 3 * rank].astype(F32) + packed[:, 3 * rank :].astype(F32)
    gram = square_of(own_level[...], ab, other_level)
    diag = eye_mask(gram.shape[0])
    mean = jnp.sum(jnp.where(diag, gram, 0.0), axis=(0, 1), keepdims=True) / gram.shape[0]
    return gram - jnp.where(diag, mean, 0.0), mean


def filter_kernel(count, first, last, *refs):
    grams, refs = refs[:count], refs[count:]
    compress_t, offset, own, other, refs = *refs[:4], refs[4:]
    if last:
        sketch, pair, sems = refs
    else:
        sketch, mix_out, level, packed, pair, sems = refs
    rank, width = own.shape[0], pair.shape[1]
    start = pl.multiple_of(offset[0], 128) if width % 128 == 0 else 0
    copies = [
        pltpu.make_async_copy(
            source.at[:, pl.ds(start, width)] if width < own.shape[1] else source,
            pair.at[slice(i * rank, (i + 1) * rank)],
            sems.at[i],
        )
        for i, source in enumerate((own, other))
    ]
    for copy in copies:
        copy.start()
    gram, mean = first_gram(grams) if first else later_gram(*grams)
    size = gram.shape[0]
    eye = jnp.where(eye_mask(size), 1.0, 0.0)
    z = gram * lax.rsqrt(jnp.sum(gram * gram, axis=(0, 1), keepdims=True) + 1e-6)
    for _ in range(K_ITERS):
        zh, zl = split(z)
        square = dot(zh, zh) + (dot(zh, zl) + dot(zl, zh))
        ph, low = split(1.5 * eye - 0.5 * square)
        z = dot(zh, ph) + (dot(zh, low) + dot(zl, ph))
    mixing = dot3(compress_t[...], 0.5 * (eye + z))
    for copy in copies:
        copy.wait()
    high, low = split(mixing)
    both = jnp.concatenate([high, low], 0)
    rows = mixing.shape[0]
    tile = next((t for t in (640, 512, 256, 128) if width % t == 0), width)
    for c in range(0, width, tile):
        wide = dot(both, pair[:, c : c + tile])
        sketch[:, c : c + tile] = (wide[:rows] + wide[rows:]).astype(sketch.dtype)
    if not last:
        block = dot3_nt(dot3(mixing, gram + mean * eye), mixing)
        mix_out[...] = mixing
        level[...] = block
        packed[:, : 2 * rank] = high
        high, low = split(block)
        packed[:, 2 * rank : 3 * rank] = high
        packed[:, 3 * rank :] = low


def filter_call(grams, compress_t, offset, own, other, width, first, last):
    rank = own.shape[0]
    rows = compress_t.shape[0]
    out = [jax.ShapeDtypeStruct((rows, width), F32 if last else BF16)]
    if not last:
        out.append(jax.ShapeDtypeStruct((rank, 2 * rank), F32))
        out.append(jax.ShapeDtypeStruct((rank, rank), F32))
        out.append(jax.ShapeDtypeStruct((rank, 4 * rank), BF16))
    args = [*grams, compress_t]
    return pl.pallas_call(
        functools.partial(filter_kernel, len(grams), first, last),
        in_specs=[VMEM] * len(args) + [SMEM, ANY, ANY],
        out_shape=out,
        scratch_shapes=[pltpu.VMEM((2 * rank, width), BF16), pltpu.SemaphoreType.DMA((2,))],
        compiler_params=PARAMS,
        name="sign_filter",
    )(*args, offset, own, other)


def swap(value, axis, mask):
    count = lax.axis_size(axis)
    return lax.ppermute(value, axis, [(source, source ^ mask) for source in range(count)])


def gather_parts(value, axis):
    count = lax.axis_size(axis)
    if count > 4 or count & (count - 1):
        return [lax.psum(value.astype(F32), axis)]
    return [value] + [swap(value, axis, mask) for mask in range(1, count)]


def join_kernel(offsets, *refs):
    out = refs[-1]
    width = refs[0].shape[1]
    for i, piece in enumerate(refs[:-1]):
        out[:, pl.ds(pl.multiple_of(offsets[i], 128), width)] = piece[...]


def join(offsets, pieces):
    share, width = pieces[0].shape
    return pl.pallas_call(
        join_kernel,
        in_specs=[SMEM] + [VMEM] * len(pieces),
        out_shape=jax.ShapeDtypeStruct((share, width * len(pieces)), F32),
        name="join",
    )(offsets, *pieces)


def on_device(record, fir_taps, gauge_lag, projector, compress):
    rows, cols = record.shape
    rank = projector.shape[1]
    count = lax.axis_size("tm")
    position = lax.axis_index("tm")
    depths = count.bit_length() - 1
    share = rank // count
    halo = lax.ppermute(
        record[rows - HALO :], "tm", [(source, source + 1) for source in range(count - 1)]
    )
    taps = jnp.pad(fir_taps.astype(F32)[::-1], (1, BLOCK - 1))[None, :]
    sketch = front(record, halo, gauge_lag[None, :], taps, projector)

    widths = []
    width = cols
    for depth in range(1, depths):
        if width % 256 == 0:
            width //= 2
        widths.append(width)
    narrowed = [depth for depth in range(depths - 1) if widths[depth] < ([cols] + widths)[depth]]
    assert narrowed == list(range(len(narrowed)))
    span = 2 ** len(narrowed)

    def bit_of(where, bit):
        return where // 2**bit % 2

    compress_t = compress.T
    flipped = jnp.concatenate([compress_t[:, rank:], compress_t[:, :rank]], 1)

    kept = ahead = None
    for depth in range(depths):
        first, last = depth == 0, depth == depths - 1
        mask = 2**depth
        weights = jnp.where(bit_of(position, depth) == 0, compress_t, flipped)
        if last:
            weights = jnp.concatenate(
                [
                    lax.dynamic_slice_in_dim(weights, (position ^ part) * share, share, 0)
                    for part in range(span)
                ],
                0,
            )
        here = sketch.shape[1]
        narrow = not last and widths[depth] < here
        offset = bit_of(position, depth) * (here // 2) if narrow else jnp.int32(0)
        offset = jnp.reshape(offset, (1,)).astype(jnp.int32)
        other = swap(sketch, "tm", mask)
        if first:
            grams = gather_parts(pair_gram(sketch, other), "chan")
        else:
            mixing, level, packed = kept
            grams = [mixing, level, swap(packed, "tm", mask), *ahead]
        if not last:
            part = ahead_gram(sketch, other, swap(sketch, "tm", 2 * mask))
            for bit in [b for b in narrowed if b < depth]:
                part = (part.astype(F32) + swap(part, "tm", 2**bit).astype(F32)).astype(BF16)
            parts = gather_parts(part, "chan")
            total = sum(piece.astype(F32) for piece in parts).astype(BF16)
            ahead = total, swap(total, "tm", mask)
        sketch, *kept = filter_call(
            grams, weights, offset, sketch, other, here if last else widths[depth], first, last
        )
    if span == 1:
        return sketch
    width = sketch.shape[1]
    pieces = [sketch[:share]] + [
        swap(sketch[part * share : (part + 1) * share], "tm", part) for part in range(1, span)
    ]
    offsets = []
    for part in range(span):
        source = position ^ part
        offsets.append(sum(bit_of(source, bit) * (cols >> (bit + 1)) for bit in narrowed))
    return join(jnp.stack(offsets).astype(jnp.int32), pieces)


def solution(mesh):
    return jax.shard_map(
        on_device,
        mesh=mesh,
        in_specs=(P("tm", "chan"), P(), P("chan"), P("tm", None), P()),
        out_specs=P("tm", "chan"),
        check_vma=False,
    )
```

```python
import functools

import jax
import jax.numpy as jnp
from jax import lax
from jax.experimental import pallas as pl
from jax.experimental.pallas import tpu as pltpu
from jax.sharding import PartitionSpec as P

TAPS = 64
GAUGE_MAX = 16
K_ITERS = 8
HALO = TAPS + GAUGE_MAX
BLOCK = 128
STEP = 16
CHUNK = 256
EXTRA = 16
F32 = jnp.float32
BF16 = jnp.bfloat16
ANY = pl.BlockSpec(memory_space=pl.ANY)
SMEM = pl.BlockSpec(memory_space=pltpu.SMEM)
VMEM = pl.BlockSpec(memory_space=pltpu.VMEM)
PARAMS = pltpu.CompilerParams(vmem_limit_bytes=40 * 2**20)


def dot(a, b):
    return jnp.dot(a, b, preferred_element_type=F32)


def dot_nt(a, b):
    return lax.dot_general(a, b, (((1,), (1,)), ((), ())), preferred_element_type=F32)


def split(a):
    high = a.astype(BF16)
    return high, (a - high.astype(F32)).astype(BF16)


def dot3(a, b):
    ah, al = split(a)
    bh, bl = split(b)
    return dot(ah, bh) + (dot(ah, bl) + dot(al, bh))


def dot3_nt(a, b):
    ah, al = split(a)
    bh, bl = split(b)
    return dot_nt(ah, bh) + (dot_nt(ah, bl) + dot_nt(al, bh))


def eye_mask(n):
    row = lax.broadcasted_iota(jnp.int32, (n, n), 0)
    col = lax.broadcasted_iota(jnp.int32, (n, n), 1)
    return row == col


def one_hot(shape, place):
    row = lax.broadcasted_iota(jnp.int32, shape, 0)
    col = lax.broadcasted_iota(jnp.int32, shape, 1)
    return jnp.where(place(row) == col, 1.0, 0.0).astype(BF16)


def front_kernel(first, last, *refs):
    if first == 0:
        record, halo, lag, band, proj_t, begun, out, strain = refs
    else:
        record, lag, taps, projector, out, band, proj_t, strain = refs
        halo = begun = None

        @pl.when(pl.program_id(0) == 0)
        def _():
            turn = one_hot((TAPS, 256), lambda tap: TAPS - tap)
            line = dot(jnp.broadcast_to(taps[...], (8, TAPS)), turn)[0:1]
            line = jnp.broadcast_to(line, (BLOCK + GAUGE_MAX, 256))
            rolled = pltpu.roll(line, 0, 1, stride=1, stride_axis=0)[:, : BLOCK + HALO]
            order = one_hot((2 * BLOCK, BLOCK + GAUGE_MAX), lambda row: row // 8 + STEP * (row % 8))
            band[...] = dot(order, rolled.astype(BF16)).astype(BF16)
            order = one_hot((BLOCK, BLOCK), lambda row: row // 8 + STEP * (row % 8))
            for block in range(projector.shape[0] // BLOCK):
                part = slice(block * BLOCK, (block + 1) * BLOCK)
                moved = dot(order, projector[part, :])
                proj_t[:, part] = moved.T.astype(BF16)

    cols = record.shape[1]
    lane = min(128, cols)
    lanes = cols // lane
    total = jnp.zeros(out.shape, F32) if begun is None else begun[...]
    used = first * BLOCK
    for block in range(first, last):
        start = block * BLOCK
        if block == 0:
            segment = jnp.concatenate([halo[...], record[0:BLOCK, :]], 0)
        else:
            segment = record[start - HALO : start + BLOCK, :]
        result = dot(band[...], segment)
        for c in range(lanes):
            span = slice(c * lane, (c + 1) * lane)
            shift = GAUGE_MAX - lag[pl.ds(pl.program_id(0) * lanes + c, 1), :]
            wide = result[:, span]
            picked = wide
            length = 2 * BLOCK
            for step in (8, 4, 2, 1):
                length = BLOCK + 8 * (step - 1)
                picked = jnp.where(
                    (shift & step) != 0, picked[8 * step : 8 * step + length], picked[:length]
                )
            strain[start : start + BLOCK, span] = (wide[BLOCK:] - picked).astype(BF16)
        done = start + BLOCK
        if done % CHUNK == 0 or block == last - 1:
            total = total + dot(proj_t[:, used:done], strain[used:done, :])
            used = done
    out[...] = total.astype(out.dtype)


def front_call(blocks, tile, args, in_specs, shape, more, scratch_rows):
    cols = shape.shape[1]
    specs = [pl.BlockSpec((shape.shape[0], tile), lambda i: (0, i))]
    specs += [pl.BlockSpec(a.shape, lambda i: (0, 0)) for a in more]
    return pl.pallas_call(
        functools.partial(front_kernel, *blocks),
        grid=(cols // tile,),
        in_specs=in_specs,
        out_specs=specs,
        out_shape=[shape, *more],
        scratch_shapes=[pltpu.VMEM((scratch_rows, tile), BF16)],
        compiler_params=pltpu.CompilerParams(vmem_limit_bytes=58 * 2**20),
        name="front",
    )(*args)


def front(record, halo, lag, taps, projector):
    rows, cols = record.shape
    rank = projector.shape[1]
    lag = lag.reshape(cols // 128, 128) if cols % 128 == 0 else lag[None, :]
    whole = lambda a: pl.BlockSpec(a.shape, lambda i: (0, 0))
    columns = lambda count, tile: pl.BlockSpec((count, tile), lambda i: (0, i))
    tile = next((t for t in (512, 640, 256, 128) if cols % t == 0), cols)
    begun, band, proj_t = front_call(
        (1, rows // BLOCK),
        tile,
        (record, lag, taps, projector),
        [columns(rows, tile), whole(lag), whole(taps), whole(projector)],
        jax.ShapeDtypeStruct((rank, cols), F32),
        [
            jax.ShapeDtypeStruct((2 * BLOCK, BLOCK + HALO), BF16),
            jax.ShapeDtypeStruct((rank, rows), BF16),
        ],
        rows,
    )
    tile = next((t for t in (1280, 640, 512, 256, 128) if cols % t == 0), cols)
    return front_call(
        (0, 1),
        tile,
        (record, halo, lag, band, proj_t, begun),
        [
            columns(BLOCK, tile),
            columns(HALO, tile),
            whole(lag),
            whole(band),
            pl.BlockSpec((rank, BLOCK), lambda i: (0, 0)),
            columns(rank, tile),
        ],
        jax.ShapeDtypeStruct((rank, cols), BF16),
        [],
        BLOCK,
    )[0]


def fetch(sources, targets, sems):
    copies = [
        pltpu.make_async_copy(source, target, sems.at[i])
        for i, (source, target) in enumerate(zip(sources, targets))
    ]
    for copy in copies:
        copy.start()
    for copy in copies:
        copy.wait()


def pair_kernel(own_ref, other_ref, out, own, other, sems):
    rank = own.shape[0]
    fetch((own_ref, other_ref), (own, other), sems)
    a, b = own[...], other[...]
    aa, ab, bb = dot_nt(a, a), dot_nt(a, b), dot_nt(b, b)
    diag = eye_mask(rank)
    trace = jnp.sum(jnp.where(diag, aa + bb, 0.0), axis=(0, 1), keepdims=True)
    mean = trace / (2 * rank)
    aa = aa - jnp.where(diag, mean, 0.0)
    bb = bb - jnp.where(diag, mean, 0.0)
    row = lax.broadcasted_iota(jnp.int32, (rank, rank), 0)
    col = lax.broadcasted_iota(jnp.int32, (rank, rank), 1)
    out[0:rank, :] = jnp.where(row <= col, aa, bb).astype(BF16)
    out[rank : 2 * rank, :] = ab.astype(BF16)
    bottom = jnp.sum(jnp.where(diag, bb, 0.0), axis=0, keepdims=True)
    full = jnp.broadcast_to(mean, (EXTRA, rank))
    high = full.astype(BF16).astype(F32)
    mid = (full - high).astype(BF16).astype(F32)
    low = full - high - mid
    line = lax.broadcasted_iota(jnp.int32, (EXTRA, rank), 0)
    extra = jnp.where(line == 0, high, jnp.where(line == 1, mid, jnp.where(line == 2, low, 0.0)))
    out[2 * rank :, :] = jnp.where(line == 3, jnp.broadcast_to(bottom, (EXTRA, rank)), extra).astype(
        BF16
    )


def pair_gram(own, other):
    rank = own.shape[0]
    return pl.pallas_call(
        pair_kernel,
        in_specs=[ANY, ANY],
        scratch_shapes=[pltpu.VMEM(own.shape, BF16)] * 2 + [pltpu.SemaphoreType.DMA((2,))],
        out_shape=jax.ShapeDtypeStruct((2 * rank + EXTRA, rank), BF16),
        compiler_params=PARAMS,
        name="pair_gram",
    )(own, other)


def ahead_kernel(own_ref, sibling_ref, partner_ref, out, own, sibling, partner, sems):
    rank = own.shape[0]
    fetch((own_ref, sibling_ref, partner_ref), (own, sibling, partner), sems)
    there = partner[...]
    out[0:rank, :] = dot_nt(own[...], there).astype(out.dtype)
    out[rank:, :] = dot_nt(sibling[...], there).astype(out.dtype)


def ahead_gram(own, sibling, partner):
    rank = own.shape[0]
    return pl.pallas_call(
        ahead_kernel,
        in_specs=[ANY] * 3,
        scratch_shapes=[pltpu.VMEM(own.shape, BF16)] * 3 + [pltpu.SemaphoreType.DMA((3,))],
        out_shape=jax.ShapeDtypeStruct((2 * rank, rank), BF16),
        compiler_params=PARAMS,
        name="ahead_gram",
    )(own, sibling, partner)


def summed(parts):
    total = parts[0][...].astype(F32)
    for part in parts[1:]:
        total = total + part[...].astype(F32)
    return total


def square_of(aa, ab, bb):
    return jnp.concatenate(
        [jnp.concatenate([aa, ab], 1), jnp.concatenate([ab.T, bb], 1)], 0
    )


def first_gram(parts):
    total = summed(parts)
    rank = total.shape[1]
    both = total[0:rank]
    ab = total[rank : 2 * rank]
    extra = total[2 * rank :]
    mean = extra[0:1, 0:1] + extra[1:2, 0:1] + extra[2:3, 0:1]
    row = lax.broadcasted_iota(jnp.int32, (rank, rank), 0)
    col = lax.broadcasted_iota(jnp.int32, (rank, rank), 1)
    turned = both.T
    aa = jnp.where(row <= col, both, turned)
    bb = jnp.where(row > col, both, jnp.where(row < col, turned, extra[3:4, :]))
    return square_of(aa, ab, bb), mean


def later_gram(own_mix, own_level, packed, ahead, sibling_ahead):
    rank = own_mix.shape[0]
    mine, theirs = ahead[...], sibling_ahead[...]
    cross = jnp.concatenate(
        [
            jnp.concatenate([mine[:rank], theirs[rank:]], 1),
            jnp.concatenate([mine[rank:], theirs[:rank]], 1),
        ],
        0,
    )
    high, low = split(own_mix[...])
    half = dot(high, cross) + dot(low, cross)
    high, low = split(half)
    other_mix = packed[:, : 2 * rank]
    ab = dot_nt(high, other_mix) + dot_nt(low, other_mix)
    other_level = packed[:, 2 * rank : 3 * rank].astype(F32) + packed[:, 3 * rank :].astype(F32)
    gram = square_of(own_level[...], ab, other_level)
    diag = eye_mask(gram.shape[0])
    mean = jnp.sum(jnp.where(diag, gram, 0.0), axis=(0, 1), keepdims=True) / gram.shape[0]
    return gram - jnp.where(diag, mean, 0.0), mean


def filter_kernel(count, first, last, *refs):
    grams, refs = refs[:count], refs[count:]
    compress_t, offset, own, other, refs = *refs[:4], refs[4:]
    if last:
        *sketch, pair, sems = refs
    else:
        sketch, mix_out, level, packed, pair, sems = refs
    rank, width = own.shape[0], pair.shape[1]
    start = pl.multiple_of(offset[0], 128) if width % 128 == 0 else 0
    copies = [
        pltpu.make_async_copy(
            source.at[:, pl.ds(start, width)] if width < own.shape[1] else source,
            pair.at[slice(i * rank, (i + 1) * rank)],
            sems.at[i],
        )
        for i, source in enumerate((own, other))
    ]
    for copy in copies:
        copy.start()
    gram, mean = first_gram(grams) if first else later_gram(*grams)
    size = gram.shape[0]
    eye = jnp.where(eye_mask(size), 1.0, 0.0)
    z = gram * lax.rsqrt(jnp.sum(gram * gram, axis=(0, 1), keepdims=True) + 1e-6)
    for _ in range(K_ITERS):
        zh, zl = split(z)
        square = dot(zh, zh) + (dot(zh, zl) + dot(zl, zh))
        ph, low = split(1.5 * eye - 0.5 * square)
        z = dot(zh, ph) + (dot(zh, low) + dot(zl, ph))
    mixing = dot3(compress_t[...], 0.5 * (eye + z))
    for copy in copies:
        copy.wait()
    high, low = split(mixing)
    both = jnp.concatenate([high, low], 0)
    rows = mixing.shape[0]
    tile = next((t for t in (640, 512, 256, 128) if width % t == 0), width)
    for c in range(0, width, tile):
        wide = dot(both, pair[:, c : c + tile])
        wide = wide[:rows] + wide[rows:]
        if last:
            share = rows // len(sketch)
            for i, piece in enumerate(sketch):
                piece[:, c : c + tile] = wide[i * share : (i + 1) * share]
        else:
            sketch[:, c : c + tile] = wide.astype(BF16)
    if not last:
        block = dot3_nt(dot3(mixing, gram + mean * eye), mixing)
        mix_out[...] = mixing
        level[...] = block
        packed[:, : 2 * rank] = high
        high, low = split(block)
        packed[:, 2 * rank : 3 * rank] = high
        packed[:, 3 * rank :] = low


def filter_call(grams, compress_t, offset, own, other, width, first, last, pieces):
    rank = own.shape[0]
    rows = compress_t.shape[0]
    if last:
        out = [jax.ShapeDtypeStruct((rows // pieces, width), F32)] * pieces
    else:
        out = [jax.ShapeDtypeStruct((rows, width), BF16)]
        out.append(jax.ShapeDtypeStruct((rank, 2 * rank), F32))
        out.append(jax.ShapeDtypeStruct((rank, rank), F32))
        out.append(jax.ShapeDtypeStruct((rank, 4 * rank), BF16))
    args = [*grams, compress_t]
    return pl.pallas_call(
        functools.partial(filter_kernel, len(grams), first, last),
        in_specs=[VMEM] * len(args) + [SMEM, ANY, ANY],
        out_shape=out,
        scratch_shapes=[pltpu.VMEM((2 * rank, width), BF16), pltpu.SemaphoreType.DMA((2,))],
        compiler_params=PARAMS,
        name="sign_filter",
    )(*args, offset, own, other)


def swap(value, axis, mask):
    count = lax.axis_size(axis)
    return lax.ppermute(value, axis, [(source, source ^ mask) for source in range(count)])


def gather_parts(value, axis):
    count = lax.axis_size(axis)
    if count > 4 or count & (count - 1):
        return [lax.psum(value.astype(F32), axis)]
    return [value] + [swap(value, axis, mask) for mask in range(1, count)]


def join_kernel(offsets, *refs):
    pieces, out, sems = refs[:-2], refs[-2], refs[-1]
    width = pieces[0].shape[1]
    targets = [
        out.at[:, pl.ds(pl.multiple_of(offsets[i], 128), width)] for i in range(len(pieces))
    ]
    fetch(pieces, targets, sems)


def join(offsets, pieces):
    share, width = pieces[0].shape
    count = len(pieces)
    return pl.pallas_call(
        join_kernel,
        in_specs=[SMEM] + [ANY] * count,
        out_specs=ANY,
        scratch_shapes=[pltpu.SemaphoreType.DMA((count,))],
        out_shape=jax.ShapeDtypeStruct((share, width * count), F32),
        name="join",
    )(offsets, *pieces)


def on_device(record, fir_taps, gauge_lag, projector, compress):
    rows, cols = record.shape
    rank = projector.shape[1]
    count = lax.axis_size("tm")
    position = lax.axis_index("tm")
    depths = count.bit_length() - 1
    share = rank // count
    halo = lax.ppermute(
        record[rows - HALO :], "tm", [(source, source + 1) for source in range(count - 1)]
    )
    sketch = front(record, halo, gauge_lag, fir_taps[None, :], projector)

    widths = []
    width = cols
    for depth in range(1, depths):
        if width % 256 == 0:
            width //= 2
        widths.append(width)
    narrowed = [depth for depth in range(depths - 1) if widths[depth] < ([cols] + widths)[depth]]
    assert narrowed == list(range(len(narrowed)))
    span = 2 ** len(narrowed)

    def bit_of(where, bit):
        return where // 2**bit % 2

    compress_t = compress.T
    flipped = jnp.concatenate([compress_t[:, rank:], compress_t[:, :rank]], 1)

    kept = ahead = None
    for depth in range(depths):
        first, last = depth == 0, depth == depths - 1
        mask = 2**depth
        weights = jnp.where(bit_of(position, depth) == 0, compress_t, flipped)
        if last:
            weights = jnp.concatenate(
                [
                    lax.dynamic_slice_in_dim(weights, (position ^ part) * share, share, 0)
                    for part in range(span)
                ],
                0,
            )
        here = sketch.shape[1]
        narrow = not last and widths[depth] < here
        offset = bit_of(position, depth) * (here // 2) if narrow else jnp.int32(0)
        offset = jnp.reshape(offset, (1,)).astype(jnp.int32)
        other = swap(sketch, "tm", mask)
        if first:
            grams = gather_parts(pair_gram(sketch, other), "chan")
        else:
            mixing, level, packed = kept
            grams = [mixing, level, swap(packed, "tm", mask), *ahead]
        if not last:
            part = ahead_gram(sketch, other, swap(sketch, "tm", 2 * mask))
            for bit in [b for b in narrowed if b < depth]:
                part = (part.astype(F32) + swap(part, "tm", 2**bit).astype(F32)).astype(BF16)
            parts = gather_parts(part, "chan")
            total = sum(piece.astype(F32) for piece in parts).astype(BF16)
            ahead = total, swap(total, "tm", mask)
        width = here if last else widths[depth]
        sketch, *kept = filter_call(
            grams, weights, offset, sketch, other, width, first, last, span
        )
    if span == 1:
        return sketch
    pieces = [sketch] + [
        swap(piece, "tm", part) for part, piece in enumerate(kept, 1)
    ]
    offsets = []
    for part in range(span):
        source = position ^ part
        offsets.append(sum(bit_of(source, bit) * (cols >> (bit + 1)) for bit in narrowed))
    return join(jnp.stack(offsets).astype(jnp.int32), pieces)


def solution(mesh):
    return jax.shard_map(
        on_device,
        mesh=mesh,
        in_specs=(P("tm", "chan"), P(), P("chan"), P("tm", None), P()),
        out_specs=P("tm", "chan"),
        check_vma=False,
    )
```

```python
import functools

import jax
import jax.numpy as jnp
from jax import lax
from jax.experimental import pallas as pl
from jax.experimental.pallas import tpu as pltpu
from jax.sharding import PartitionSpec as P

TAPS = 64
GAUGE_MAX = 16
K_ITERS = 8
HALO = TAPS + GAUGE_MAX
BLOCK = 128
STEP = 16
CHUNK = 256
EXTRA = 16
F32 = jnp.float32
BF16 = jnp.bfloat16
ANY = pl.BlockSpec(memory_space=pl.ANY)
SMEM = pl.BlockSpec(memory_space=pltpu.SMEM)
VMEM = pl.BlockSpec(memory_space=pltpu.VMEM)
PARAMS = pltpu.CompilerParams(vmem_limit_bytes=40 * 2**20)


def dot(a, b):
    return jnp.dot(a, b, preferred_element_type=F32)


def dot_nt(a, b):
    return lax.dot_general(a, b, (((1,), (1,)), ((), ())), preferred_element_type=F32)


def split(a):
    high = a.astype(BF16)
    return high, (a - high.astype(F32)).astype(BF16)


def dot3_split(ah, al, bh, bl):
    rows = ah.shape[0]
    wide = dot(jnp.concatenate([ah, al], 0), bh)
    return wide[:rows] + (wide[rows:] + dot(ah, bl))


def dot3(a, b):
    return dot3_split(*split(a), *split(b))


def dot3_nt(a, b):
    ah, al = split(a)
    bh, bl = split(b)
    return dot_nt(ah, bh) + (dot_nt(ah, bl) + dot_nt(al, bh))


def eye_mask(n):
    row = lax.broadcasted_iota(jnp.int32, (n, n), 0)
    col = lax.broadcasted_iota(jnp.int32, (n, n), 1)
    return row == col


def one_hot(shape, place):
    row = lax.broadcasted_iota(jnp.int32, shape, 0)
    col = lax.broadcasted_iota(jnp.int32, shape, 1)
    return jnp.where(place(row) == col, 1.0, 0.0).astype(BF16)


def front_kernel(first, last, *refs):
    if first == 0:
        record, halo, lag, band, weights, begun, out, strain = refs
    else:
        record, lag, taps, projector, out, band, head_weights, head, strain, weights = refs
        halo = begun = None

        @pl.when(pl.program_id(0) == 0)
        def _():
            turn = one_hot((TAPS, 256), lambda tap: TAPS - tap)
            line = dot(jnp.broadcast_to(taps[...], (8, TAPS)), turn)[0:1]
            line = jnp.broadcast_to(line, (BLOCK + GAUGE_MAX, 256))
            rolled = pltpu.roll(line, 0, 1, stride=1, stride_axis=0)[:, : BLOCK + HALO]
            order = one_hot((2 * BLOCK, BLOCK + GAUGE_MAX), lambda row: row // 8 + STEP * (row % 8))
            band[...] = dot(order, rolled.astype(BF16)).astype(BF16)
            order = one_hot((BLOCK, BLOCK), lambda row: row // 8 + STEP * (row % 8))
            for block in range(projector.shape[0] // BLOCK):
                part = slice(block * BLOCK, (block + 1) * BLOCK)
                weights[part, :] = dot(order, projector[part, :]).astype(BF16)
            head_weights[...] = weights[0:BLOCK, :]

    cols = record.shape[1]
    lane = min(128, cols)
    lanes = cols // lane
    total = None
    used = first * BLOCK
    if first > 0:
        head[...] = record[0:BLOCK, :]
    for block in range(first, last):
        start = block * BLOCK
        if block == 0:
            segment = jnp.concatenate([halo[...], record[0:BLOCK, :]], 0)
        else:
            segment = record[start - HALO : start + BLOCK, :]
        result = dot(band[...], segment)
        for c in range(lanes):
            span = slice(c * lane, (c + 1) * lane)
            shift = GAUGE_MAX - lag[pl.ds(pl.program_id(0) * lanes + c, 1), :]
            wide = result[:, span]
            picked = wide
            length = 2 * BLOCK
            for step in (8, 4, 2, 1):
                length = BLOCK + 8 * (step - 1)
                picked = jnp.where(
                    (shift & step) != 0, picked[8 * step : 8 * step + length], picked[:length]
                )
            strain[span, start : start + BLOCK] = (wide[BLOCK:] - picked).T.astype(BF16)
        done = start + BLOCK
        if done % CHUNK == 0 or block == last - 1:
            part = dot(strain[:, used:done], weights[used:done, :])
            total = part if total is None else total + part
            used = done
    total = total.T
    if begun is not None:
        total = total + begun[...]
    out[...] = total.astype(out.dtype)


def front_call(blocks, args, in_specs, out_specs, out_shape, scratch, steps, grant):
    return pl.pallas_call(
        functools.partial(front_kernel, *blocks),
        grid=(steps,),
        in_specs=in_specs,
        out_specs=out_specs,
        out_shape=out_shape,
        scratch_shapes=[pltpu.VMEM(shape, BF16) for shape in scratch],
        compiler_params=pltpu.CompilerParams(vmem_limit_bytes=grant * 2**20),
        name="front",
    )(*args)


def front(record, halo, lag, taps, projector):
    rows, cols = record.shape
    rank = projector.shape[1]
    lag = lag.reshape(cols // 128, 128) if cols % 128 == 0 else lag[None, :]
    whole = lambda a: pl.BlockSpec(a.shape, lambda i: (0, 0))
    columns = lambda count, tile: pl.BlockSpec((count, tile), lambda i: (0, i))
    tile = next((t for t in (512, 640, 256, 128) if cols % t == 0), cols)
    shapes = [
        jax.ShapeDtypeStruct((rank, cols), F32),
        jax.ShapeDtypeStruct((2 * BLOCK, BLOCK + HALO), BF16),
        jax.ShapeDtypeStruct((BLOCK, rank), BF16),
        jax.ShapeDtypeStruct((BLOCK, cols), BF16),
    ]
    begun, band, weights, head = front_call(
        (1, rows // BLOCK),
        (record, lag, taps, projector),
        [columns(rows, tile), whole(lag), whole(taps), whole(projector)],
        [columns(rank, tile), whole(shapes[1]), whole(shapes[2]), columns(BLOCK, tile)],
        shapes,
        [(tile, rows), (rows, rank)],
        cols // tile,
        58,
    )
    tile = next((t for t in (1280, 640, 512, 256, 128) if cols % t == 0), cols)
    return front_call(
        (0, 1),
        (head, halo, lag, band, weights, begun),
        [
            columns(BLOCK, tile),
            columns(HALO, tile),
            whole(lag),
            whole(band),
            whole(weights),
            columns(rank, tile),
        ],
        columns(rank, tile),
        jax.ShapeDtypeStruct((rank, cols), BF16),
        [(tile, BLOCK)],
        cols // tile,
        32,
    )


def pair_kernel(own, other, out):
    rank = own.shape[0]
    a, b = own[...], other[...]
    aa, ab, bb = dot_nt(a, a), dot_nt(a, b), dot_nt(b, b)
    diag = eye_mask(rank)
    trace = jnp.sum(jnp.where(diag, aa + bb, 0.0), axis=(0, 1), keepdims=True)
    mean = trace / (2 * rank)
    aa = aa - jnp.where(diag, mean, 0.0)
    bb = bb - jnp.where(diag, mean, 0.0)
    row = lax.broadcasted_iota(jnp.int32, (rank, rank), 0)
    col = lax.broadcasted_iota(jnp.int32, (rank, rank), 1)
    out[0:rank, :] = jnp.where(row <= col, aa, bb).astype(BF16)
    out[rank : 2 * rank, :] = ab.astype(BF16)
    bottom = jnp.sum(jnp.where(diag, bb, 0.0), axis=0, keepdims=True)
    full = jnp.broadcast_to(mean, (EXTRA, rank))
    high = full.astype(BF16).astype(F32)
    mid = (full - high).astype(BF16).astype(F32)
    low = full - high - mid
    line = lax.broadcasted_iota(jnp.int32, (EXTRA, rank), 0)
    extra = jnp.where(line == 0, high, jnp.where(line == 1, mid, jnp.where(line == 2, low, 0.0)))
    out[2 * rank :, :] = jnp.where(line == 3, jnp.broadcast_to(bottom, (EXTRA, rank)), extra).astype(
        BF16
    )


def pair_gram(own, other):
    rank = own.shape[0]
    return pl.pallas_call(
        pair_kernel,
        out_shape=jax.ShapeDtypeStruct((2 * rank + EXTRA, rank), BF16),
        compiler_params=PARAMS,
        name="pair_gram",
    )(own, other)


def ahead_kernel(own, sibling, partner, out):
    rank = own.shape[0]
    there = partner[...]
    out[0:rank, :] = dot_nt(own[...], there).astype(out.dtype)
    out[rank:, :] = dot_nt(sibling[...], there).astype(out.dtype)


def ahead_gram(own, sibling, partner):
    rank = own.shape[0]
    return pl.pallas_call(
        ahead_kernel,
        out_shape=jax.ShapeDtypeStruct((2 * rank, rank), BF16),
        compiler_params=PARAMS,
        name="ahead_gram",
    )(own, sibling, partner)


def summed(parts):
    total = parts[0][...].astype(F32)
    for part in parts[1:]:
        total = total + part[...].astype(F32)
    return total


def square_of(aa, ab, bb):
    return jnp.concatenate(
        [jnp.concatenate([aa, ab], 1), jnp.concatenate([ab.T, bb], 1)], 0
    )


def first_gram(parts):
    total = summed(parts)
    rank = total.shape[1]
    both = total[0:rank]
    ab = total[rank : 2 * rank]
    extra = total[2 * rank :]
    mean = extra[0:1, 0:1] + extra[1:2, 0:1] + extra[2:3, 0:1]
    row = lax.broadcasted_iota(jnp.int32, (rank, rank), 0)
    col = lax.broadcasted_iota(jnp.int32, (rank, rank), 1)
    turned = both.T
    aa = jnp.where(row <= col, both, turned)
    bb = jnp.where(row > col, both, jnp.where(row < col, turned, extra[3:4, :]))
    return square_of(aa, ab, bb), mean


def later_gram(own_mix, own_level, packed, ahead, sibling_ahead):
    rank = own_mix.shape[0]
    mine, theirs = ahead[...], sibling_ahead[...]
    cross = jnp.concatenate(
        [
            jnp.concatenate([mine[:rank], theirs[rank:]], 1),
            jnp.concatenate([mine[rank:], theirs[:rank]], 1),
        ],
        0,
    )
    high, low = split(own_mix[...])
    half = dot(high, cross) + dot(low, cross)
    high, low = split(half)
    other_mix = packed[:, : 2 * rank]
    ab = dot_nt(high, other_mix) + dot_nt(low, other_mix)
    other_level = packed[:, 2 * rank : 3 * rank].astype(F32) + packed[:, 3 * rank :].astype(F32)
    gram = square_of(own_level[...], ab, other_level)
    diag = eye_mask(gram.shape[0])
    mean = jnp.sum(jnp.where(diag, gram, 0.0), axis=(0, 1), keepdims=True) / gram.shape[0]
    return gram - jnp.where(diag, mean, 0.0), mean


def filter_kernel(count, first, last, *refs):
    grams, refs = refs[:count], refs[count:]
    compress_t, offset, own, other, refs = *refs[:4], refs[4:]
    if last:
        *sketch, pair, sems = refs
    else:
        sketch, mix_out, level, packed, pair, sems = refs
    rank, width = own.shape[0], pair.shape[1]
    start = pl.multiple_of(offset[0], 128) if width % 128 == 0 else 0
    copies = [
        pltpu.make_async_copy(
            source.at[:, pl.ds(start, width)] if width < own.shape[1] else source,
            pair.at[slice(i * rank, (i + 1) * rank)],
            sems.at[i],
        )
        for i, source in enumerate((own, other))
    ]
    for copy in copies:
        copy.start()
    gram, mean = first_gram(grams) if first else later_gram(*grams)
    size = gram.shape[0]
    eye = jnp.where(eye_mask(size), 1.0, 0.0)
    z = gram * lax.rsqrt(jnp.sum(gram * gram, axis=(0, 1), keepdims=True) + 1e-6)
    for _ in range(K_ITERS):
        zh, zl = split(z)
        square = dot3_split(zh, zl, zh, zl)
        z = dot3_split(zh, zl, *split(1.5 * eye - 0.5 * square))
    mixing = dot3(compress_t[...], 0.5 * (eye + z))
    for copy in copies:
        copy.wait()
    high, low = split(mixing)
    both = jnp.concatenate([high, low], 0)
    rows = mixing.shape[0]
    tile = next((t for t in (640, 512, 256, 128) if width % t == 0), width)
    for c in range(0, width, tile):
        wide = dot(both, pair[:, c : c + tile])
        wide = wide[:rows] + wide[rows:]
        if last:
            share = rows // len(sketch)
            for i, piece in enumerate(sketch):
                piece[:, c : c + tile] = wide[i * share : (i + 1) * share]
        else:
            sketch[:, c : c + tile] = wide.astype(BF16)
    if not last:
        block = dot3_nt(dot3(mixing, gram + mean * eye), mixing)
        mix_out[...] = mixing
        level[...] = block
        packed[:, : 2 * rank] = high
        high, low = split(block)
        packed[:, 2 * rank : 3 * rank] = high
        packed[:, 3 * rank :] = low


def filter_call(grams, compress_t, offset, own, other, width, first, last, pieces):
    rank = own.shape[0]
    rows = compress_t.shape[0]
    if last:
        out = [jax.ShapeDtypeStruct((rows // pieces, width), F32)] * pieces
    else:
        out = [jax.ShapeDtypeStruct((rows, width), BF16)]
        out.append(jax.ShapeDtypeStruct((rank, 2 * rank), F32))
        out.append(jax.ShapeDtypeStruct((rank, rank), F32))
        out.append(jax.ShapeDtypeStruct((rank, 4 * rank), BF16))
    args = [*grams, compress_t]
    return pl.pallas_call(
        functools.partial(filter_kernel, len(grams), first, last),
        in_specs=[VMEM] * len(args) + [SMEM, ANY, ANY],
        out_shape=out,
        scratch_shapes=[pltpu.VMEM((2 * rank, width), BF16), pltpu.SemaphoreType.DMA((2,))],
        compiler_params=PARAMS,
        name="sign_filter",
    )(*args, offset, own, other)


def swap(value, axis, mask):
    count = lax.axis_size(axis)
    return lax.ppermute(value, axis, [(source, source ^ mask) for source in range(count)])


def gather_parts(value, axis):
    count = lax.axis_size(axis)
    if count > 4 or count & (count - 1):
        return [lax.psum(value.astype(F32), axis)]
    return [value] + [swap(value, axis, mask) for mask in range(1, count)]


def join_kernel(offsets, *refs):
    out = refs[-1]
    width = refs[0].shape[1]
    for i, piece in enumerate(refs[:-1], 1):
        out[:, pl.ds(pl.multiple_of(offsets[i], 128), width)] = piece[...]


def join(offsets, pieces):
    share, width = pieces[0].shape
    return pl.pallas_call(
        join_kernel,
        in_specs=[SMEM] + [VMEM] * len(pieces),
        out_shape=jax.ShapeDtypeStruct((share, width * len(pieces)), F32),
        name="join",
    )(offsets, *pieces)


def on_device(record, fir_taps, gauge_lag, projector, compress):
    rows, cols = record.shape
    rank = projector.shape[1]
    count = lax.axis_size("tm")
    position = lax.axis_index("tm")
    depths = count.bit_length() - 1
    share = rank // count
    halo = lax.ppermute(
        record[rows - HALO :], "tm", [(source, source + 1) for source in range(count - 1)]
    )
    sketch = front(record, halo, gauge_lag, fir_taps[None, :], projector)

    widths = []
    width = cols
    for depth in range(1, depths):
        if width % 256 == 0:
            width //= 2
        widths.append(width)
    narrowed = [depth for depth in range(depths - 1) if widths[depth] < ([cols] + widths)[depth]]
    assert narrowed == list(range(len(narrowed)))
    span = 2 ** len(narrowed)

    def bit_of(where, bit):
        return where // 2**bit % 2

    compress_t = compress.T
    flipped = jnp.concatenate([compress_t[:, rank:], compress_t[:, :rank]], 1)

    places = [position * 0]
    for part in range(span):
        source = position ^ part
        places.append(sum([bit_of(source, bit) * (cols >> (bit + 1)) for bit in narrowed], position * 0))
    places = jnp.stack(places).astype(jnp.int32)
    kept = ahead = None
    for depth in range(depths):
        first, last = depth == 0, depth == depths - 1
        mask = 2**depth
        weights = jnp.where(bit_of(position, depth) == 0, compress_t, flipped)
        if last:
            weights = jnp.concatenate(
                [
                    lax.dynamic_slice_in_dim(weights, (position ^ part) * share, share, 0)
                    for part in range(span)
                ],
                0,
            )
        here = sketch.shape[1]
        narrow = not last and widths[depth] < here
        offset = bit_of(position, depth) * (here // 2) if narrow else jnp.int32(0)
        offset = places if last else jnp.reshape(offset, (1,)).astype(jnp.int32)
        other = swap(sketch, "tm", mask)
        if first:
            grams = gather_parts(pair_gram(sketch, other), "chan")
        else:
            mixing, level, packed = kept
            grams = [mixing, level, swap(packed, "tm", mask), *ahead]
        if not last:
            part = ahead_gram(sketch, other, swap(sketch, "tm", 2 * mask))
            for bit in [b for b in narrowed if b < depth]:
                part = (part.astype(F32) + swap(part, "tm", 2**bit).astype(F32)).astype(BF16)
            parts = gather_parts(part, "chan")
            total = sum(piece.astype(F32) for piece in parts).astype(BF16)
            ahead = total, swap(total, "tm", mask)
        width = here if last else widths[depth]
        sketch, *kept = filter_call(
            grams, weights, offset, sketch, other, width, first, last, span
        )
    if span == 1:
        return sketch
    pieces = [sketch] + [
        swap(piece, "tm", part) for part, piece in enumerate(kept, 1)
    ]
    return join(places, pieces)


def solution(mesh):
    return jax.shard_map(
        on_device,
        mesh=mesh,
        in_specs=(P("tm", "chan"), P(), P("chan"), P("tm", None), P()),
        out_specs=P("tm", "chan"),
        check_vma=False,
    )
```

```python
import functools

import jax
import jax.numpy as jnp
from jax import lax
from jax.experimental import pallas as pl
from jax.experimental.pallas import tpu as pltpu
from jax.sharding import PartitionSpec as P

TAPS = 64
GAUGE_MAX = 16
K_ITERS = 8
HALO = TAPS + GAUGE_MAX
BLOCK = 128
STEP = 16
CHUNK = 256
EXTRA = 16
F32 = jnp.float32
BF16 = jnp.bfloat16
ANY = pl.BlockSpec(memory_space=pl.ANY)
HBM = pl.BlockSpec(memory_space=pltpu.HBM)
SMEM = pl.BlockSpec(memory_space=pltpu.SMEM)
VMEM = pl.BlockSpec(memory_space=pltpu.VMEM)
PARAMS = pltpu.CompilerParams(vmem_limit_bytes=40 * 2**20)


def dot(a, b):
    return jnp.dot(a, b, preferred_element_type=F32)


def dot_nt(a, b):
    return lax.dot_general(a, b, (((1,), (1,)), ((), ())), preferred_element_type=F32)


def split(a):
    high = a.astype(BF16)
    return high, (a - high.astype(F32)).astype(BF16)


def dot3_split(ah, al, bh, bl):
    rows = ah.shape[0]
    wide = dot(jnp.concatenate([ah, al], 0), bh)
    return wide[:rows] + (wide[rows:] + dot(ah, bl))


def dot3(a, b):
    return dot3_split(*split(a), *split(b))


def dot3_nt(a, b):
    ah, al = split(a)
    bh, bl = split(b)
    return dot_nt(ah, bh) + (dot_nt(ah, bl) + dot_nt(al, bh))


def eye_mask(n):
    row = lax.broadcasted_iota(jnp.int32, (n, n), 0)
    col = lax.broadcasted_iota(jnp.int32, (n, n), 1)
    return row == col


def one_hot(shape, place):
    row = lax.broadcasted_iota(jnp.int32, shape, 0)
    col = lax.broadcasted_iota(jnp.int32, shape, 1)
    return jnp.where(place(row) == col, 1.0, 0.0).astype(BF16)


def front_kernel(first, last, *refs):
    if first == 0:
        record, halo, lag, band, weights, begun, side, out, send, strain = refs
    else:
        record, lag_ref, taps_ref, projector_ref, out, band, head_weights, head = refs[:8]
        strain, weights, lag, taps, projector, sems = refs[8:]
        halo = begun = None

        @pl.when(pl.program_id(0) == 0)
        def _():
            sources, targets = (lag_ref, taps_ref, projector_ref), (lag, taps, projector)
            copies = [
                pltpu.make_async_copy(source, target, sems.at[i])
                for i, (source, target) in enumerate(zip(sources, targets))
            ]
            for copy in copies:
                copy.start()
            for copy in copies:
                copy.wait()
            turn = one_hot((TAPS, 256), lambda tap: TAPS - tap)
            line = dot(jnp.broadcast_to(taps[...], (8, TAPS)), turn)[0:1]
            line = jnp.broadcast_to(line, (BLOCK + GAUGE_MAX, 256))
            rolled = pltpu.roll(line, 0, 1, stride=1, stride_axis=0)[:, : BLOCK + HALO]
            order = one_hot((2 * BLOCK, BLOCK + GAUGE_MAX), lambda row: row // 8 + STEP * (row % 8))
            band[...] = dot(order, rolled.astype(BF16)).astype(BF16)
            order = one_hot((BLOCK, BLOCK), lambda row: row // 8 + STEP * (row % 8))
            for block in range(projector.shape[0] // BLOCK):
                part = slice(block * BLOCK, (block + 1) * BLOCK)
                weights[:, part] = dot(order, projector[part, :]).T.astype(BF16)
            head_weights[...] = weights[:, 0:BLOCK]

    cols = record.shape[1]
    lane = min(128, cols)
    lanes = cols // lane
    group = 256 if cols % 256 == 0 else lane
    total = None
    used = first * BLOCK
    if first > 0:
        head[...] = record[0:BLOCK, :]
    for block in range(first, last):
        start = block * BLOCK
        for g in range(0, cols, group):
            if block == 0:
                segment = jnp.concatenate([halo[:, g : g + group], record[0:BLOCK, g : g + group]], 0)
            else:
                segment = record[start - HALO : start + BLOCK, g : g + group]
            result = dot(band[...], segment)
            for c in range(0, group, lane):
                line = pl.program_id(0) * lanes + (g + c) // lane
                shift = GAUGE_MAX - lag[pl.ds(line, 1), :]
                wide = result[:, c : c + lane]
                picked = wide
                for step in (8, 4, 2, 1):
                    length = BLOCK + 8 * (step - 1)
                    picked = jnp.where(
                        (shift & step) != 0, picked[8 * step : 8 * step + length], picked[:length]
                    )
                strain[start : start + BLOCK, g + c : g + c + lane] = (wide[BLOCK:] - picked).astype(
                    BF16
                )
        done = start + BLOCK
        if done % CHUNK == 0 or block == last - 1:
            part = dot(weights[:, used:done], strain[used:done, :])
            total = part if total is None else total + part
            used = done
    if begun is None:
        out[...] = total
    else:
        total = (total + begun[...]).astype(BF16)
        out[...] = total
        if send.shape[1] == cols:

            @pl.when(pl.program_id(0) == side[0])
            def _():
                send[...] = total


def front_call(blocks, args, in_specs, out_specs, out_shape, scratch, steps, grant):
    return pl.pallas_call(
        functools.partial(front_kernel, *blocks),
        grid=(steps,),
        in_specs=in_specs,
        out_specs=out_specs,
        out_shape=out_shape,
        scratch_shapes=scratch,
        compiler_params=pltpu.CompilerParams(vmem_limit_bytes=grant * 2**20),
        cost_estimate=cost(100 * (blocks[1] - blocks[0]) * BLOCK * BLOCK * args[0].shape[1] * 2),
        name="front",
    )(*args)


def front(record, halo, lag, taps, projector, side):
    rows, cols = record.shape
    rank = projector.shape[1]
    lag = lag.reshape(cols // 128, 128) if cols % 128 == 0 else lag[None, :]
    whole = lambda a: pl.BlockSpec(a.shape, lambda i: (0, 0))
    columns = lambda count, tile: pl.BlockSpec((count, tile), lambda i: (0, i))
    tile = next((t for t in (512, 640, 256, 128) if cols % t == 0), cols)
    shapes = [
        jax.ShapeDtypeStruct((rank, cols), F32),
        jax.ShapeDtypeStruct((2 * BLOCK, BLOCK + HALO), BF16),
        jax.ShapeDtypeStruct((rank, BLOCK), BF16),
        jax.ShapeDtypeStruct((BLOCK, cols), BF16),
    ]
    begun, band, weights, head = front_call(
        (1, rows // BLOCK),
        (record, lag, taps, projector),
        [columns(rows, tile), HBM, HBM, HBM],
        [columns(rank, tile), whole(shapes[1]), whole(shapes[2]), columns(BLOCK, tile)],
        shapes,
        [
            pltpu.VMEM((rows, tile), BF16),
            pltpu.VMEM((rank, rows), BF16),
            pltpu.VMEM(lag.shape, lag.dtype),
            pltpu.VMEM(taps.shape, BF16),
            pltpu.VMEM(projector.shape, BF16),
            pltpu.SemaphoreType.DMA((3,)),
        ],
        cols // tile,
        50,
    )
    halves = cols % 256 == 0
    tile = cols // 2 if halves else cols
    return front_call(
        (0, 1),
        (head, halo, lag, band, weights, begun, side),
        [
            columns(BLOCK, tile),
            columns(HALO, tile),
            whole(lag),
            whole(band),
            whole(weights),
            columns(rank, tile),
            SMEM,
        ],
        [columns(rank, tile), pl.BlockSpec((rank, tile if halves else 128), lambda i: (0, 0))],
        [
            jax.ShapeDtypeStruct((rank, cols), BF16),
            jax.ShapeDtypeStruct((rank, tile if halves else 128), BF16),
        ],
        [pltpu.VMEM((BLOCK, tile), BF16)],
        cols // tile,
        32,
    )


def pair_kernel(own, other, out):
    rank = own.shape[0]
    a, b = own[...], other[...]
    aa, ab, bb = dot_nt(a, a), dot_nt(a, b), dot_nt(b, b)
    diag = eye_mask(rank)
    trace = jnp.sum(jnp.where(diag, aa + bb, 0.0), axis=(0, 1), keepdims=True)
    mean = trace / (2 * rank)
    aa = aa - jnp.where(diag, mean, 0.0)
    bb = bb - jnp.where(diag, mean, 0.0)
    row = lax.broadcasted_iota(jnp.int32, (rank, rank), 0)
    col = lax.broadcasted_iota(jnp.int32, (rank, rank), 1)
    out[0:rank, :] = jnp.where(row <= col, aa, bb).astype(BF16)
    out[rank : 2 * rank, :] = ab.astype(BF16)
    bottom = jnp.sum(jnp.where(diag, bb, 0.0), axis=0, keepdims=True)
    full = jnp.broadcast_to(mean, (EXTRA, rank))
    high = full.astype(BF16).astype(F32)
    mid = (full - high).astype(BF16).astype(F32)
    low = full - high - mid
    line = lax.broadcasted_iota(jnp.int32, (EXTRA, rank), 0)
    extra = jnp.where(line == 0, high, jnp.where(line == 1, mid, jnp.where(line == 2, low, 0.0)))
    out[2 * rank :, :] = jnp.where(line == 3, jnp.broadcast_to(bottom, (EXTRA, rank)), extra).astype(
        BF16
    )


def pair_gram(own, other):
    rank = own.shape[0]
    return pl.pallas_call(
        pair_kernel,
        out_shape=jax.ShapeDtypeStruct((2 * rank + EXTRA, rank), BF16),
        compiler_params=PARAMS,
        name="pair_gram",
    )(own, other)


def ahead_kernel(own, sibling, partner, start, _, out):
    rank = own.shape[0]
    there = partner[...]
    width = there.shape[1]
    span = slice(None) if width == own.shape[1] else pl.ds(pl.multiple_of(start[0], 128), width)
    out[0:rank, :] = dot_nt(own[:, span], there).astype(out.dtype)
    out[rank:, :] = dot_nt(sibling[:, span], there).astype(out.dtype)


def ahead_gram(own, sibling, partner, start, after):
    rank = own.shape[0]
    return pl.pallas_call(
        ahead_kernel,
        in_specs=[VMEM, VMEM, VMEM, SMEM, ANY],
        out_shape=jax.ShapeDtypeStruct((2 * rank, rank), BF16),
        compiler_params=PARAMS,
        name="ahead_gram",
    )(own, sibling, partner, start, after)


def summed(parts):
    total = parts[0][...].astype(F32)
    for part in parts[1:]:
        total = total + part[...].astype(F32)
    return total


def square_of(aa, ab, bb):
    return jnp.concatenate(
        [jnp.concatenate([aa, ab], 1), jnp.concatenate([ab.T, bb], 1)], 0
    )


def first_gram(parts):
    total = summed(parts)
    rank = total.shape[1]
    both = total[0:rank]
    ab = total[rank : 2 * rank]
    extra = total[2 * rank :]
    mean = extra[0:1, 0:1] + extra[1:2, 0:1] + extra[2:3, 0:1]
    row = lax.broadcasted_iota(jnp.int32, (rank, rank), 0)
    col = lax.broadcasted_iota(jnp.int32, (rank, rank), 1)
    turned = both.T
    aa = jnp.where(row <= col, both, turned)
    bb = jnp.where(row > col, both, jnp.where(row < col, turned, extra[3:4, :]))
    return square_of(aa, ab, bb), mean


def later_gram(own_mix, own_level, packed, ahead, sibling_ahead, *other_half):
    rank = own_mix.shape[0]
    mine, theirs = ahead[...], sibling_ahead[...]
    cross = jnp.concatenate(
        [
            jnp.concatenate([mine[:rank], theirs[rank:]], 1),
            jnp.concatenate([mine[rank:], theirs[:rank]], 1),
        ],
        0,
    )
    if other_half:
        first, second = (ref[...].astype(F32) for ref in other_half)
        blocks = ((first[:rank], first[rank:]), (second[rank:], second[:rank]))
        turned = [jnp.concatenate([block.T for block in row], 1) for row in blocks]
        cross = (cross.astype(F32) + jnp.concatenate(turned, 0)).astype(BF16)
    high, low = split(own_mix[...])
    half = dot(high, cross) + dot(low, cross)
    high, low = split(half)
    other_mix = packed[:, : 2 * rank]
    ab = dot_nt(high, other_mix) + dot_nt(low, other_mix)
    other_level = packed[:, 2 * rank : 3 * rank].astype(F32) + packed[:, 3 * rank :].astype(F32)
    gram = square_of(own_level[...], ab, other_level)
    diag = eye_mask(gram.shape[0])
    mean = jnp.sum(jnp.where(diag, gram, 0.0), axis=(0, 1), keepdims=True) / gram.shape[0]
    return gram - jnp.where(diag, mean, 0.0), mean


def filter_kernel(count, first, last, *refs):
    grams, refs = refs[:count], refs[count:]
    compress_t, offset, own, other, _, refs = *refs[:5], refs[5:]
    if last:
        *sketch, pair, sems = refs
    else:
        sketch, mix_out, level, packed, pair, sems = refs
    rank, width = own.shape[0], pair.shape[1]
    start = pl.multiple_of(offset[0], 128) if width % 128 == 0 else 0
    copies = [
        pltpu.make_async_copy(
            source.at[:, pl.ds(start, width)] if width < own.shape[1] else source,
            pair.at[slice(i * rank, (i + 1) * rank)],
            sems.at[i],
        )
        for i, source in enumerate((own, other))
    ]
    for copy in copies:
        copy.start()
    gram, mean = first_gram(grams) if first else later_gram(*grams)
    size = gram.shape[0]
    eye = jnp.where(eye_mask(size), 1.0, 0.0)
    z = gram * lax.rsqrt(jnp.sum(gram * gram, axis=(0, 1), keepdims=True) + 1e-6)
    for _ in range(K_ITERS):
        zh, zl = split(z)
        square = dot3_split(zh, zl, zh, zl)
        z = dot3_split(zh, zl, *split(1.5 * eye - 0.5 * square))
    mixing = dot3(compress_t[...], 0.5 * (eye + z))
    for copy in copies:
        copy.wait()
    high, low = split(mixing)
    both = jnp.concatenate([high, low], 0)
    rows = mixing.shape[0]
    tile = next((t for t in (640, 512, 256, 128) if width % t == 0), width)
    for c in range(0, width, tile):
        wide = dot(both, pair[:, c : c + tile])
        wide = wide[:rows] + wide[rows:]
        if last:
            share = rows // len(sketch)
            for i, piece in enumerate(sketch):
                piece[:, c : c + tile] = wide[i * share : (i + 1) * share]
        else:
            sketch[:, c : c + tile] = wide.astype(BF16)
    if not last:
        block = dot3_nt(dot3(mixing, gram + mean * eye), mixing)
        mix_out[...] = mixing
        level[...] = block
        packed[:, : 2 * rank] = high
        high, low = split(block)
        packed[:, 2 * rank : 3 * rank] = high
        packed[:, 3 * rank :] = low


def cost(flops, bytes_accessed=0):
    return pl.CostEstimate(flops=int(flops), bytes_accessed=int(bytes_accessed), transcendentals=0)


def filter_call(grams, compress_t, offset, own, other, before, width, first, last, pieces):
    rank = own.shape[0]
    rows = compress_t.shape[0]
    if last:
        out = [jax.ShapeDtypeStruct((rows // pieces, width), F32)] * pieces
    else:
        out = [jax.ShapeDtypeStruct((rows, width), BF16)]
        out.append(jax.ShapeDtypeStruct((rank, 2 * rank), F32))
        out.append(jax.ShapeDtypeStruct((rank, rank), F32))
        out.append(jax.ShapeDtypeStruct((rank, 4 * rank), BF16))
    args = [*grams, compress_t]
    return pl.pallas_call(
        functools.partial(filter_kernel, len(grams), first, last),
        in_specs=[VMEM] * len(args) + [SMEM, ANY, ANY, ANY],
        out_shape=out,
        scratch_shapes=[pltpu.VMEM((2 * rank, width), BF16), pltpu.SemaphoreType.DMA((2,))],
        compiler_params=PARAMS,
        cost_estimate=cost(50 * K_ITERS * (2 * rank) ** 3),
        name="sign_filter",
    )(*args, offset, own, other, before)


def swap(value, axis, mask):
    count = lax.axis_size(axis)
    return lax.ppermute(value, axis, [(source, source ^ mask) for source in range(count)])


def gather_parts(value, axis):
    count = lax.axis_size(axis)
    if count > 4 or count & (count - 1):
        return [lax.psum(value.astype(F32), axis)]
    return [value] + [swap(value, axis, mask) for mask in range(1, count)]


def join_kernel(offsets, *refs):
    out = refs[-1]
    width = refs[0].shape[1]
    for i, piece in enumerate(refs[:-1], 1):
        out[:, pl.ds(pl.multiple_of(offsets[i], 128), width)] = piece[...]


def join(offsets, pieces):
    share, width = pieces[0].shape
    return pl.pallas_call(
        join_kernel,
        in_specs=[SMEM] + [VMEM] * len(pieces),
        out_shape=jax.ShapeDtypeStruct((share, width * len(pieces)), F32),
        name="join",
    )(offsets, *pieces)


def on_device(record, fir_taps, gauge_lag, projector, compress):
    rows, cols = record.shape
    rank = projector.shape[1]
    count = lax.axis_size("tm")
    position = lax.axis_index("tm")
    depths = count.bit_length() - 1
    share = rank // count
    halo = lax.ppermute(
        record[rows - HALO :], "tm", [(source, source + 1) for source in range(count - 1)]
    )
    side = position // 2 % 2
    sketch, half = front(
        record, halo, gauge_lag, fir_taps[None, :], projector, jnp.reshape(1 - side, (1,)).astype(jnp.int32)
    )

    widths = []
    width = cols
    for depth in range(1, depths):
        if width % 256 == 0:
            width //= 2
        widths.append(width)
    narrowed = [depth for depth in range(depths - 1) if widths[depth] < ([cols] + widths)[depth]]
    assert narrowed == list(range(len(narrowed)))
    span = 2 ** len(narrowed)

    def bit_of(where, bit):
        return where // 2**bit % 2

    compress_t = compress.T
    flipped = jnp.concatenate([compress_t[:, rank:], compress_t[:, :rank]], 1)

    places = [position * 0]
    for part in range(span):
        source = position ^ part
        places.append(sum([bit_of(source, bit) * (cols >> (bit + 1)) for bit in narrowed], position * 0))
    places = jnp.stack(places).astype(jnp.int32)
    kept = ahead = None
    for depth in range(depths):
        first, last = depth == 0, depth == depths - 1
        mask = 2**depth
        weights = jnp.where(bit_of(position, depth) == 0, compress_t, flipped)
        if last:
            weights = jnp.concatenate(
                [
                    lax.dynamic_slice_in_dim(weights, (position ^ part) * share, share, 0)
                    for part in range(span)
                ],
                0,
            )
        here = sketch.shape[1]
        narrow = not last and widths[depth] < here
        offset = bit_of(position, depth) * (here // 2) if narrow else jnp.int32(0)
        offset = places if last else jnp.reshape(offset, (1,)).astype(jnp.int32)
        other = swap(sketch, "tm", mask)
        if first:
            grams = gather_parts(pair_gram(sketch, other), "chan")
        else:
            mixing, level, packed = kept
            grams = [mixing, level, swap(packed, "tm", mask), *ahead]
        width = here if last else widths[depth]
        merge = lambda before: filter_call(
            grams, weights, offset, sketch, other, before, width, first, last, span
        )
        if last:
            sketch, *kept = merge(grams[0])
            continue
        halves = first and cols % 256 == 0
        partner = swap(half if halves else sketch, "tm", 2 * mask)
        start = jnp.reshape(side * (here // 2), (1,)).astype(jnp.int32)
        if first:
            part = ahead_gram(sketch, other, partner, start, start)
            merged, *kept = merge(part)
        else:
            merged, *kept = merge(grams[0])
            part = ahead_gram(sketch, other, partner, start, kept[1])
        for bit in [b for b in narrowed if b < depth]:
            part = (part.astype(F32) + swap(part, "tm", 2**bit).astype(F32)).astype(BF16)
        parts = gather_parts(part, "chan")
        total = sum(piece.astype(F32) for piece in parts).astype(BF16)
        ahead = [total, swap(total, "tm", mask)]
        if halves:
            ahead += [swap(total, "tm", 2 * mask), swap(total, "tm", 3 * mask)]
        sketch = merged
    if span == 1:
        return sketch
    pieces = [sketch] + [
        swap(piece, "tm", part) for part, piece in enumerate(kept, 1)
    ]
    return join(places, pieces)


def solution(mesh):
    return jax.shard_map(
        on_device,
        mesh=mesh,
        in_specs=(P("tm", "chan"), P(), P("chan"), P("tm", None), P()),
        out_specs=P("tm", "chan"),
        check_vma=False,
    )
```

```python
import functools

import jax
import jax.numpy as jnp
from jax import lax
from jax.experimental import pallas as pl
from jax.experimental.pallas import tpu as pltpu
from jax.sharding import PartitionSpec as P

TAPS = 64
GAUGE_MAX = 16
K_ITERS = 8
HALO = TAPS + GAUGE_MAX
BLOCK = 128
STEP = 16
CHUNK = 256
EXTRA = 16
F32 = jnp.float32
BF16 = jnp.bfloat16
ANY = pl.BlockSpec(memory_space=pl.ANY)
HBM = pl.BlockSpec(memory_space=pltpu.HBM)
SMEM = pl.BlockSpec(memory_space=pltpu.SMEM)
VMEM = pl.BlockSpec(memory_space=pltpu.VMEM)
PARAMS = pltpu.CompilerParams(vmem_limit_bytes=40 * 2**20)


def dot(a, b):
    return jnp.dot(a, b, preferred_element_type=F32)


def dot_nt(a, b):
    return lax.dot_general(a, b, (((1,), (1,)), ((), ())), preferred_element_type=F32)


def split(a):
    high = a.astype(BF16)
    return high, (a - high.astype(F32)).astype(BF16)


def dot3_split(ah, al, bh, bl):
    rows = ah.shape[0]
    wide = dot(jnp.concatenate([ah, al], 0), bh)
    return wide[:rows] + (wide[rows:] + dot(ah, bl))


def dot3(a, b):
    return dot3_split(*split(a), *split(b))


def dot3_nt(a, b):
    ah, al = split(a)
    bh, bl = split(b)
    return dot_nt(ah, bh) + (dot_nt(ah, bl) + dot_nt(al, bh))


def eye_mask(n):
    row = lax.broadcasted_iota(jnp.int32, (n, n), 0)
    col = lax.broadcasted_iota(jnp.int32, (n, n), 1)
    return row == col


def one_hot(shape, place):
    row = lax.broadcasted_iota(jnp.int32, shape, 0)
    col = lax.broadcasted_iota(jnp.int32, shape, 1)
    return jnp.where(place(row) == col, 1.0, 0.0).astype(BF16)


def front_kernel(first, last, *refs):
    if first == 0:
        record, halo, lag, band, weights, begun, side, out, send, strain = refs
    else:
        record, lag_ref, taps_ref, projector_ref, out, band, head_weights, head = refs[:8]
        strain, weights, lag, taps, projector, sems = refs[8:]
        halo = begun = None

        @pl.when(pl.program_id(0) == 0)
        def _():
            sources, targets = (lag_ref, taps_ref, projector_ref), (lag, taps, projector)
            copies = [
                pltpu.make_async_copy(source, target, sems.at[i])
                for i, (source, target) in enumerate(zip(sources, targets))
            ]
            for copy in copies:
                copy.start()
            for copy in copies:
                copy.wait()
            turn = one_hot((TAPS, 256), lambda tap: TAPS - tap)
            line = dot(jnp.broadcast_to(taps[...], (8, TAPS)), turn)[0:1]
            line = jnp.broadcast_to(line, (BLOCK + GAUGE_MAX, 256))
            rolled = pltpu.roll(line, 0, 1, stride=1, stride_axis=0)[:, : BLOCK + HALO]
            order = one_hot((2 * BLOCK, BLOCK + GAUGE_MAX), lambda row: row // 8 + STEP * (row % 8))
            band[...] = dot(order, rolled.astype(BF16)).astype(BF16)
            order = one_hot((BLOCK, BLOCK), lambda row: row // 8 + STEP * (row % 8))
            for block in range(projector.shape[0] // BLOCK):
                part = slice(block * BLOCK, (block + 1) * BLOCK)
                weights[:, part] = dot(order, projector[part, :]).T.astype(BF16)
            head_weights[...] = weights[:, 0:BLOCK]

    cols = record.shape[1]
    lane = min(128, cols)
    lanes = cols // lane
    group = 256 if cols % 256 == 0 else lane
    total = None
    used = first * BLOCK
    if first > 0:
        head[...] = record[0:BLOCK, :]
    for block in range(first, last):
        start = block * BLOCK
        for g in range(0, cols, group):
            if block == 0:
                segment = jnp.concatenate([halo[:, g : g + group], record[0:BLOCK, g : g + group]], 0)
            else:
                segment = record[start - HALO : start + BLOCK, g : g + group]
            result = dot(band[...], segment)
            for c in range(0, group, lane):
                line = pl.program_id(0) * lanes + (g + c) // lane
                shift = GAUGE_MAX - lag[pl.ds(line, 1), :]
                wide = result[:, c : c + lane]
                picked = wide
                for step in (8, 4, 2, 1):
                    length = BLOCK + 8 * (step - 1)
                    picked = jnp.where(
                        (shift & step) != 0, picked[8 * step : 8 * step + length], picked[:length]
                    )
                strain[start : start + BLOCK, g + c : g + c + lane] = (wide[BLOCK:] - picked).astype(
                    BF16
                )
        done = start + BLOCK
        if done % CHUNK == 0 or block == last - 1:
            part = dot(weights[:, used:done], strain[used:done, :])
            total = part if total is None else total + part
            used = done
    if begun is None:
        out[...] = total
    else:
        total = (total + begun[...]).astype(BF16)
        out[...] = total
        if send.shape[1] == cols:

            @pl.when(pl.program_id(0) == side[0])
            def _():
                send[...] = total


def front_call(blocks, args, in_specs, out_specs, out_shape, scratch, steps, grant):
    return pl.pallas_call(
        functools.partial(front_kernel, *blocks),
        grid=(steps,),
        in_specs=in_specs,
        out_specs=out_specs,
        out_shape=out_shape,
        scratch_shapes=scratch,
        compiler_params=pltpu.CompilerParams(vmem_limit_bytes=grant * 2**20),
        cost_estimate=cost(100 * (blocks[1] - blocks[0]) * BLOCK * BLOCK * args[0].shape[1] * 2),
        name="front",
    )(*args)


def front(record, halo, lag, taps, projector, side):
    rows, cols = record.shape
    rank = projector.shape[1]
    lag = lag.reshape(cols // 128, 128) if cols % 128 == 0 else lag[None, :]
    whole = lambda a: pl.BlockSpec(a.shape, lambda i: (0, 0))
    columns = lambda count, tile: pl.BlockSpec((count, tile), lambda i: (0, i))
    tile = next((t for t in (512, 640, 256, 128) if cols % t == 0), cols)
    shapes = [
        jax.ShapeDtypeStruct((rank, cols), F32),
        jax.ShapeDtypeStruct((2 * BLOCK, BLOCK + HALO), BF16),
        jax.ShapeDtypeStruct((rank, BLOCK), BF16),
        jax.ShapeDtypeStruct((BLOCK, cols), BF16),
    ]
    begun, band, weights, head = front_call(
        (1, rows // BLOCK),
        (record, lag, taps, projector),
        [columns(rows, tile), HBM, HBM, HBM],
        [columns(rank, tile), whole(shapes[1]), whole(shapes[2]), columns(BLOCK, tile)],
        shapes,
        [
            pltpu.VMEM((rows, tile), BF16),
            pltpu.VMEM((rank, rows), BF16),
            pltpu.VMEM(lag.shape, lag.dtype),
            pltpu.VMEM(taps.shape, BF16),
            pltpu.VMEM(projector.shape, BF16),
            pltpu.SemaphoreType.DMA((3,)),
        ],
        cols // tile,
        48,
    )
    halves = cols % 256 == 0
    tile = cols // 2 if halves else cols
    return front_call(
        (0, 1),
        (head, halo, lag, band, weights, begun, side),
        [
            columns(BLOCK, tile),
            columns(HALO, tile),
            whole(lag),
            whole(band),
            whole(weights),
            columns(rank, tile),
            SMEM,
        ],
        [columns(rank, tile), pl.BlockSpec((rank, tile if halves else 128), lambda i: (0, 0))],
        [
            jax.ShapeDtypeStruct((rank, cols), BF16),
            jax.ShapeDtypeStruct((rank, tile if halves else 128), BF16),
        ],
        [pltpu.VMEM((BLOCK, tile), BF16)],
        cols // tile,
        32,
    )


def pair_kernel(own, other, out):
    rank = own.shape[0]
    a, b = own[...], other[...]
    aa, ab, bb = dot_nt(a, a), dot_nt(a, b), dot_nt(b, b)
    diag = eye_mask(rank)
    trace = jnp.sum(jnp.where(diag, aa + bb, 0.0), axis=(0, 1), keepdims=True)
    mean = trace / (2 * rank)
    aa = aa - jnp.where(diag, mean, 0.0)
    bb = bb - jnp.where(diag, mean, 0.0)
    row = lax.broadcasted_iota(jnp.int32, (rank, rank), 0)
    col = lax.broadcasted_iota(jnp.int32, (rank, rank), 1)
    out[0:rank, :] = jnp.where(row <= col, aa, bb).astype(BF16)
    out[rank : 2 * rank, :] = ab.astype(BF16)
    bottom = jnp.sum(jnp.where(diag, bb, 0.0), axis=0, keepdims=True)
    full = jnp.broadcast_to(mean, (EXTRA, rank))
    high = full.astype(BF16).astype(F32)
    mid = (full - high).astype(BF16).astype(F32)
    low = full - high - mid
    line = lax.broadcasted_iota(jnp.int32, (EXTRA, rank), 0)
    extra = jnp.where(line == 0, high, jnp.where(line == 1, mid, jnp.where(line == 2, low, 0.0)))
    out[2 * rank :, :] = jnp.where(line == 3, jnp.broadcast_to(bottom, (EXTRA, rank)), extra).astype(
        BF16
    )


def pair_gram(own, other):
    rank = own.shape[0]
    return pl.pallas_call(
        pair_kernel,
        out_shape=jax.ShapeDtypeStruct((2 * rank + EXTRA, rank), BF16),
        compiler_params=PARAMS,
        name="pair_gram",
    )(own, other)


def ahead_kernel(own, sibling, partner, start, _, out):
    rank = own.shape[0]
    there = partner[...]
    width = there.shape[1]
    span = slice(None) if width == own.shape[1] else pl.ds(pl.multiple_of(start[0], 128), width)
    out[0:rank, :] = dot_nt(own[:, span], there).astype(out.dtype)
    out[rank:, :] = dot_nt(sibling[:, span], there).astype(out.dtype)


def ahead_gram(own, sibling, partner, start, after):
    rank = own.shape[0]
    return pl.pallas_call(
        ahead_kernel,
        in_specs=[VMEM, VMEM, VMEM, SMEM, ANY],
        out_shape=jax.ShapeDtypeStruct((2 * rank, rank), BF16),
        compiler_params=PARAMS,
        name="ahead_gram",
    )(own, sibling, partner, start, after)


def summed(parts):
    total = parts[0][...].astype(F32)
    for part in parts[1:]:
        total = total + part[...].astype(F32)
    return total


def square_of(aa, ab, bb):
    return jnp.concatenate(
        [jnp.concatenate([aa, ab], 1), jnp.concatenate([ab.T, bb], 1)], 0
    )


def first_gram(parts):
    total = summed(parts)
    rank = total.shape[1]
    both = total[0:rank]
    ab = total[rank : 2 * rank]
    extra = total[2 * rank :]
    mean = extra[0:1, 0:1] + extra[1:2, 0:1] + extra[2:3, 0:1]
    row = lax.broadcasted_iota(jnp.int32, (rank, rank), 0)
    col = lax.broadcasted_iota(jnp.int32, (rank, rank), 1)
    turned = both.T
    aa = jnp.where(row <= col, both, turned)
    bb = jnp.where(row > col, both, jnp.where(row < col, turned, extra[3:4, :]))
    return square_of(aa, ab, bb), mean


def later_gram(own_mix, own_level, packed, ahead, sibling_ahead, *other_half):
    rank = own_mix.shape[0]
    mine, theirs = ahead[...], sibling_ahead[...]
    cross = jnp.concatenate(
        [
            jnp.concatenate([mine[:rank], theirs[rank:]], 1),
            jnp.concatenate([mine[rank:], theirs[:rank]], 1),
        ],
        0,
    )
    if other_half:
        first, second = (ref[...].astype(F32) for ref in other_half)
        blocks = ((first[:rank], first[rank:]), (second[rank:], second[:rank]))
        turned = [jnp.concatenate([block.T for block in row], 1) for row in blocks]
        cross = (cross.astype(F32) + jnp.concatenate(turned, 0)).astype(BF16)
    high, low = split(own_mix[...])
    half = dot(high, cross) + dot(low, cross)
    high, low = split(half)
    other_mix = packed[:, : 2 * rank]
    ab = dot_nt(high, other_mix) + dot_nt(low, other_mix)
    other_level = packed[:, 2 * rank : 3 * rank].astype(F32) + packed[:, 3 * rank :].astype(F32)
    gram = square_of(own_level[...], ab, other_level)
    diag = eye_mask(gram.shape[0])
    mean = jnp.sum(jnp.where(diag, gram, 0.0), axis=(0, 1), keepdims=True) / gram.shape[0]
    return gram - jnp.where(diag, mean, 0.0), mean


def filter_kernel(count, first, last, quarters, *refs):
    grams, refs = refs[:count], refs[count:]
    compress_t, places, own, other, _, refs = *refs[:5], refs[5:]
    *out, pair, sems = refs
    if not last:
        *out, mix_out, level, packed = out
    rank, width = own.shape[0], pair.shape[1]
    start = pl.multiple_of(places[0], 128) if width < own.shape[1] else 0
    copies = [
        pltpu.make_async_copy(
            source.at[:, pl.ds(start, width)] if width < own.shape[1] else source,
            pair.at[slice(i * rank, (i + 1) * rank)],
            sems.at[i],
        )
        for i, source in enumerate((own, other))
    ]
    for copy in copies:
        copy.start()
    gram, mean = first_gram(grams) if first else later_gram(*grams)
    size = gram.shape[0]
    eye = jnp.where(eye_mask(size), 1.0, 0.0)
    z = gram * lax.rsqrt(jnp.sum(gram * gram, axis=(0, 1), keepdims=True) + 1e-6)
    for _ in range(K_ITERS):
        zh, zl = split(z)
        square = dot3_split(zh, zl, zh, zl)
        z = dot3_split(zh, zl, *split(1.5 * eye - 0.5 * square))
    mixing = dot3(compress_t[...], 0.5 * (eye + z))
    for copy in copies:
        copy.wait()
    high, low = split(mixing)
    both = jnp.concatenate([high, low], 0)
    rows = mixing.shape[0]

    def mixed(span):
        wide = dot(both, pair[:, span])
        return wide[:rows] + wide[rows:]

    if quarters:
        for half in range(2):
            part = mixed(slice(half * width // 2, (half + 1) * width // 2)).astype(BF16)
            for i, place in enumerate((1, 2)):
                mine, theirs = out[2 * i], out[2 * i + 1]

                @pl.when(places[place] == half)
                def _():
                    mine[...] = part

                @pl.when(places[place] != half)
                def _():
                    theirs[...] = part
    else:
        tile = next((t for t in (640, 512, 256, 128) if width % t == 0), width)
        for c in range(0, width, tile):
            part = mixed(slice(c, c + tile))
            share = rows // len(out)
            for i, piece in enumerate(out):
                piece[:, c : c + tile] = part[i * share : (i + 1) * share].astype(piece.dtype)
    if not last:
        block = dot3_nt(dot3(mixing, gram + mean * eye), mixing)
        mix_out[...] = mixing
        level[...] = block
        packed[:, : 2 * rank] = high
        high, low = split(block)
        packed[:, 2 * rank : 3 * rank] = high
        packed[:, 3 * rank :] = low


def cost(flops, bytes_accessed=0):
    return pl.CostEstimate(flops=int(flops), bytes_accessed=int(bytes_accessed), transcendentals=0)


def filter_call(grams, compress_t, places, own, other, before, width, first, last, pieces, quarters):
    rank = own.shape[0]
    rows = compress_t.shape[0]
    if last:
        out = [jax.ShapeDtypeStruct((rows // pieces, width), F32)] * pieces
    else:
        out = [jax.ShapeDtypeStruct((rank, width // 2), BF16)] * 4
        if not quarters:
            out = [jax.ShapeDtypeStruct((rank, width), BF16)]
        out.append(jax.ShapeDtypeStruct((rank, 2 * rank), F32))
        out.append(jax.ShapeDtypeStruct((rank, rank), F32))
        out.append(jax.ShapeDtypeStruct((rank, 4 * rank), BF16))
    args = [*grams, compress_t]
    return pl.pallas_call(
        functools.partial(filter_kernel, len(grams), first, last, quarters),
        in_specs=[VMEM] * len(args) + [SMEM, ANY, ANY, ANY],
        out_shape=out,
        scratch_shapes=[pltpu.VMEM((2 * rank, width), BF16), pltpu.SemaphoreType.DMA((2,))],
        compiler_params=PARAMS,
        cost_estimate=cost(50 * K_ITERS * (2 * rank) ** 3),
        name="sign_filter",
    )(*args, places, own, other, before)


def swap(value, axis, mask):
    count = lax.axis_size(axis)
    return lax.ppermute(value, axis, [(source, source ^ mask) for source in range(count)])


def gather_parts(value, axis):
    count = lax.axis_size(axis)
    if count > 4 or count & (count - 1):
        return [lax.psum(value.astype(F32), axis)]
    return [value] + [swap(value, axis, mask) for mask in range(1, count)]


def join_kernel(offsets, *refs):
    out = refs[-1]
    width = refs[0].shape[1]
    for i, piece in enumerate(refs[:-1], 1):
        out[:, pl.ds(pl.multiple_of(offsets[i], 128), width)] = piece[...]


def join(offsets, pieces):
    share, width = pieces[0].shape
    return pl.pallas_call(
        join_kernel,
        in_specs=[SMEM] + [VMEM] * len(pieces),
        out_shape=jax.ShapeDtypeStruct((share, width * len(pieces)), F32),
        name="join",
    )(offsets, *pieces)


def on_device(record, fir_taps, gauge_lag, projector, compress):
    rows, cols = record.shape
    rank = projector.shape[1]
    count = lax.axis_size("tm")
    position = lax.axis_index("tm")
    depths = count.bit_length() - 1
    share = rank // count
    halo = lax.ppermute(
        record[rows - HALO :], "tm", [(source, source + 1) for source in range(count - 1)]
    )
    side = position // 2 % 2
    sketch, half = front(
        record, halo, gauge_lag, fir_taps[None, :], projector, jnp.reshape(1 - side, (1,)).astype(jnp.int32)
    )

    widths = [cols]
    for depth in range(1, depths):
        widths.append(widths[-1] // 2 if widths[-1] % 256 == 0 else widths[-1])
    narrowed = [depth for depth in range(depths - 1) if widths[depth + 1] < widths[depth]]
    assert narrowed == list(range(len(narrowed)))
    span = 2 ** len(narrowed)

    def bit_of(where, bit):
        return where // 2**bit % 2

    compress_t = compress.T
    flipped = jnp.concatenate([compress_t[:, rank:], compress_t[:, :rank]], 1)

    def scalars(*values):
        return jnp.stack([position * 0 + value for value in values]).astype(jnp.int32)

    joined = [0]
    for part in range(span):
        source = position ^ part
        joined.append(sum([bit_of(source, bit) * (cols >> (bit + 1)) for bit in narrowed], 0))
    joined = scalars(*joined)
    kept = ahead = None
    keep, send, given = sketch, half if 0 in narrowed else sketch, sketch
    for depth in range(depths):
        first, last = depth == 0, depth == depths - 1
        mask = 2**depth
        weights = jnp.where(bit_of(position, depth) == 0, compress_t, flipped)
        if last:
            weights = jnp.concatenate(
                [
                    lax.dynamic_slice_in_dim(weights, (position ^ part) * share, share, 0)
                    for part in range(span)
                ],
                0,
            )
        other = swap(given, "tm", mask)
        if first:
            grams = gather_parts(pair_gram(sketch, other), "chan")
        else:
            mixing, level, packed = kept
            grams = [mixing, level, swap(packed, "tm", mask), *ahead]
        here = widths[depth]
        if last:
            out = filter_call(
                grams, weights, joined, sketch, other, grams[0], here, first, last, span, False
            )
            sketch, *kept = out
            continue
        ahead_bit = bit_of(position, depth + 1)
        halved = depth in narrowed
        sibling = other if first else swap(keep, "tm", mask)
        start = scalars(ahead_bit * (here // 2))
        if first:
            part = ahead_gram(sketch, sibling, swap(send, "tm", 2 * mask), start, start)
        else:
            part = ahead_gram(keep, sibling, swap(send, "tm", 2 * mask), start, ahead[0])
        for bit in [b for b in narrowed if b < depth]:
            part = (part.astype(F32) + swap(part, "tm", 2**bit).astype(F32)).astype(BF16)
        quarters = depth + 1 in narrowed
        places = scalars(
            bit_of(position, depth) * (here // 2) if halved and first else 0,
            bit_of(position, depth + 1),
            bit_of(position, min(depth + 2, depths - 1)),
        )
        width = widths[depth + 1]
        out = filter_call(
            grams, weights, places, sketch, other, part, width, first, last, span, quarters
        )
        parts = gather_parts(part, "chan")
        total = sum(piece.astype(F32) for piece in parts).astype(BF16)
        ahead = [total, swap(total, "tm", mask)]
        if halved:
            ahead += [swap(total, "tm", 2 * mask), swap(total, "tm", 3 * mask)]
        *out, mixing, level, packed = out
        kept = mixing, level, packed
        if quarters:
            sketch, given, keep, send = out
        else:
            sketch = given = keep = send = out[0]
    if span == 1:
        return sketch
    pieces = [sketch] + [
        swap(piece, "tm", part) for part, piece in enumerate(kept, 1)
    ]
    return join(joined, pieces)


def solution(mesh):
    return jax.shard_map(
        on_device,
        mesh=mesh,
        in_specs=(P("tm", "chan"), P(), P("chan"), P("tm", None), P()),
        out_specs=P("tm", "chan"),
        check_vma=False,
    )
```

```python
import functools

import jax
import jax.numpy as jnp
from jax import lax
from jax.experimental import pallas as pl
from jax.experimental.pallas import tpu as pltpu
from jax.sharding import PartitionSpec as P

TAPS = 64
GAUGE_MAX = 16
K_ITERS = 8
HALO = TAPS + GAUGE_MAX
BLOCK = 128
STEP = 16
CHUNK = 256
EXTRA = 16
F32 = jnp.float32
BF16 = jnp.bfloat16
ANY = pl.BlockSpec(memory_space=pl.ANY)
HBM = pl.BlockSpec(memory_space=pltpu.HBM)
SMEM = pl.BlockSpec(memory_space=pltpu.SMEM)
VMEM = pl.BlockSpec(memory_space=pltpu.VMEM)
PARAMS = pltpu.CompilerParams(vmem_limit_bytes=40 * 2**20)


def dot(a, b):
    return jnp.dot(a, b, preferred_element_type=F32)


def dot_nt(a, b):
    return lax.dot_general(a, b, (((1,), (1,)), ((), ())), preferred_element_type=F32)


def split(a):
    high = a.astype(BF16)
    return high, (a - high.astype(F32)).astype(BF16)


def dot3_split(ah, al, bh, bl):
    rows = ah.shape[0]
    wide = dot(jnp.concatenate([ah, al], 0), bh)
    return wide[:rows] + (wide[rows:] + dot(ah, bl))


def dot3(a, b):
    return dot3_split(*split(a), *split(b))


def dot3_nt(a, b):
    ah, al = split(a)
    bh, bl = split(b)
    return dot_nt(ah, bh) + (dot_nt(ah, bl) + dot_nt(al, bh))


def eye_mask(n):
    row = lax.broadcasted_iota(jnp.int32, (n, n), 0)
    col = lax.broadcasted_iota(jnp.int32, (n, n), 1)
    return row == col


def one_hot(shape, place):
    row = lax.broadcasted_iota(jnp.int32, shape, 0)
    col = lax.broadcasted_iota(jnp.int32, shape, 1)
    return jnp.where(place(row) == col, 1.0, 0.0).astype(BF16)


def front_kernel(first, last, *refs):
    if first == 0:
        record, halo, lag, band, weights, begun, out, strain = refs
    else:
        record, lag_ref, taps_ref, projector_ref, out, band, head_weights, head = refs[:8]
        strain, weights, lag, taps, projector, sems = refs[8:]
        halo = begun = None

        @pl.when(pl.program_id(0) == 0)
        def _():
            sources, targets = (lag_ref, taps_ref, projector_ref), (lag, taps, projector)
            copies = [
                pltpu.make_async_copy(source, target, sems.at[i])
                for i, (source, target) in enumerate(zip(sources, targets))
            ]
            for copy in copies:
                copy.start()
            for copy in copies:
                copy.wait()
            turn = one_hot((TAPS, 256), lambda tap: TAPS - tap)
            line = dot(jnp.broadcast_to(taps[...], (8, TAPS)), turn)[0:1]
            line = jnp.broadcast_to(line, (BLOCK + GAUGE_MAX, 256))
            rolled = pltpu.roll(line, 0, 1, stride=1, stride_axis=0)[:, : BLOCK + HALO]
            order = one_hot((2 * BLOCK, BLOCK + GAUGE_MAX), lambda row: row // 8 + STEP * (row % 8))
            band[...] = dot(order, rolled.astype(BF16)).astype(BF16)
            order = one_hot((BLOCK, BLOCK), lambda row: row // 8 + STEP * (row % 8))
            for block in range(projector.shape[0] // BLOCK):
                part = slice(block * BLOCK, (block + 1) * BLOCK)
                weights[:, part] = dot(order, projector[part, :]).T.astype(BF16)
            head_weights[...] = weights[:, 0:BLOCK]

    cols = record.shape[1]
    lane = min(128, cols)
    lanes = cols // lane
    group = 256 if cols % 256 == 0 else lane
    total = None
    used = first * BLOCK
    if first > 0:
        head[...] = record[0:BLOCK, :]
    for block in range(first, last):
        start = block * BLOCK
        for g in range(0, cols, group):
            if block == 0:
                segment = jnp.concatenate([halo[:, g : g + group], record[0:BLOCK, g : g + group]], 0)
            else:
                segment = record[start - HALO : start + BLOCK, g : g + group]
            result = dot(band[...], segment)
            for c in range(0, group, lane):
                line = pl.program_id(0) * lanes + (g + c) // lane
                shift = GAUGE_MAX - lag[pl.ds(line, 1), :]
                wide = result[:, c : c + lane]
                picked = wide
                for step in (8, 4, 2, 1):
                    length = BLOCK + 8 * (step - 1)
                    picked = jnp.where(
                        (shift & step) != 0, picked[8 * step : 8 * step + length], picked[:length]
                    )
                strain[start : start + BLOCK, g + c : g + c + lane] = (wide[BLOCK:] - picked).astype(
                    BF16
                )
        done = start + BLOCK
        if done % CHUNK == 0 or block == last - 1:
            part = dot(weights[:, used:done], strain[used:done, :])
            total = part if total is None else total + part
            used = done
    if begun is None:
        out[...] = total
    else:
        out[...] = (total + begun[...]).astype(BF16)


def front_call(blocks, args, in_specs, out_specs, out_shape, scratch, steps, grant):
    return pl.pallas_call(
        functools.partial(front_kernel, *blocks),
        grid=(steps,),
        in_specs=in_specs,
        out_specs=out_specs,
        out_shape=out_shape,
        scratch_shapes=scratch,
        compiler_params=pltpu.CompilerParams(vmem_limit_bytes=grant * 2**20),
        name="front",
    )(*args)


def front(record, halo, lag, taps, projector):
    rows, cols = record.shape
    rank = projector.shape[1]
    lag = lag.reshape(cols // 128, 128) if cols % 128 == 0 else lag[None, :]
    whole = lambda a: pl.BlockSpec(a.shape, lambda i: (0, 0))
    columns = lambda count, tile: pl.BlockSpec((count, tile), lambda i: (0, i))
    tile = next((t for t in (512, 640, 256, 128) if cols % t == 0), cols)
    shapes = [
        jax.ShapeDtypeStruct((rank, cols), F32),
        jax.ShapeDtypeStruct((2 * BLOCK, BLOCK + HALO), BF16),
        jax.ShapeDtypeStruct((rank, BLOCK), BF16),
        jax.ShapeDtypeStruct((BLOCK, cols), BF16),
    ]
    begun, band, weights, head = front_call(
        (1, rows // BLOCK),
        (record, lag, taps, projector),
        [columns(rows, tile), HBM, HBM, HBM],
        [columns(rank, tile), whole(shapes[1]), whole(shapes[2]), columns(BLOCK, tile)],
        shapes,
        [
            pltpu.VMEM((rows, tile), BF16),
            pltpu.VMEM((rank, rows), BF16),
            pltpu.VMEM(lag.shape, lag.dtype),
            pltpu.VMEM(taps.shape, BF16),
            pltpu.VMEM(projector.shape, BF16),
            pltpu.SemaphoreType.DMA((3,)),
        ],
        cols // tile,
        48,
    )
    tile = cols // 2 if cols % 256 == 0 else cols
    return front_call(
        (0, 1),
        (head, halo, lag, band, weights, begun),
        [
            columns(BLOCK, tile),
            columns(HALO, tile),
            whole(lag),
            whole(band),
            whole(weights),
            columns(rank, tile),
        ],
        columns(rank, tile),
        jax.ShapeDtypeStruct((rank, cols), BF16),
        [pltpu.VMEM((BLOCK, tile), BF16)],
        cols // tile,
        32,
    )


def pair_kernel(own, other, out):
    rank = own.shape[0]
    a, b = own[...], other[...]
    aa, ab, bb = dot_nt(a, a), dot_nt(a, b), dot_nt(b, b)
    diag = eye_mask(rank)
    trace = jnp.sum(jnp.where(diag, aa + bb, 0.0), axis=(0, 1), keepdims=True)
    mean = trace / (2 * rank)
    aa = aa - jnp.where(diag, mean, 0.0)
    bb = bb - jnp.where(diag, mean, 0.0)
    row = lax.broadcasted_iota(jnp.int32, (rank, rank), 0)
    col = lax.broadcasted_iota(jnp.int32, (rank, rank), 1)
    out[0:rank, :] = jnp.where(row <= col, aa, bb).astype(BF16)
    out[rank : 2 * rank, :] = ab.astype(BF16)
    bottom = jnp.sum(jnp.where(diag, bb, 0.0), axis=0, keepdims=True)
    full = jnp.broadcast_to(mean, (EXTRA, rank))
    high = full.astype(BF16).astype(F32)
    mid = (full - high).astype(BF16).astype(F32)
    low = full - high - mid
    line = lax.broadcasted_iota(jnp.int32, (EXTRA, rank), 0)
    extra = jnp.where(line == 0, high, jnp.where(line == 1, mid, jnp.where(line == 2, low, 0.0)))
    out[2 * rank :, :] = jnp.where(line == 3, jnp.broadcast_to(bottom, (EXTRA, rank)), extra).astype(
        BF16
    )


def pair_gram(own, other):
    rank = own.shape[0]
    return pl.pallas_call(
        pair_kernel,
        out_shape=jax.ShapeDtypeStruct((2 * rank + EXTRA, rank), BF16),
        compiler_params=PARAMS,
        name="pair_gram",
    )(own, other)


def ahead_kernel(width, own, sibling, partner, out):
    rank = own.shape[0]
    there = partner[:, :width]
    out[0:rank, :] = dot_nt(own[:, :width], there).astype(out.dtype)
    out[rank:, :] = dot_nt(sibling[:, :width], there).astype(out.dtype)


def ahead_gram(own, sibling, partner, width):
    rank = own.shape[0]
    return pl.pallas_call(
        functools.partial(ahead_kernel, width),
        out_shape=jax.ShapeDtypeStruct((2 * rank, rank), BF16),
        compiler_params=PARAMS,
        name="ahead_gram",
    )(own, sibling, partner)


def summed(parts):
    total = parts[0][...].astype(F32)
    for part in parts[1:]:
        total = total + part[...].astype(F32)
    return total


def square_of(aa, ab, bb):
    return jnp.concatenate(
        [jnp.concatenate([aa, ab], 1), jnp.concatenate([ab.T, bb], 1)], 0
    )


def first_gram(parts):
    total = summed(parts)
    rank = total.shape[1]
    both = total[0:rank]
    ab = total[rank : 2 * rank]
    extra = total[2 * rank :]
    mean = extra[0:1, 0:1] + extra[1:2, 0:1] + extra[2:3, 0:1]
    row = lax.broadcasted_iota(jnp.int32, (rank, rank), 0)
    col = lax.broadcasted_iota(jnp.int32, (rank, rank), 1)
    turned = both.T
    aa = jnp.where(row <= col, both, turned)
    bb = jnp.where(row > col, both, jnp.where(row < col, turned, extra[3:4, :]))
    return square_of(aa, ab, bb), mean


def later_gram(own_mix, own_level, ahead, sibling_ahead, other):
    rank = own_mix.shape[0]
    mine, theirs = ahead[...], sibling_ahead[...]
    cross = jnp.concatenate(
        [
            jnp.concatenate([mine[:rank], theirs[rank:]], 1),
            jnp.concatenate([mine[rank:], theirs[:rank]], 1),
        ],
        0,
    )
    high, low = split(own_mix[...])
    half = dot(high, cross) + dot(low, cross)
    high, low = split(half)
    place = other.shape[1] - 4 * rank
    other_mix = other[:, place : place + 2 * rank]
    ab = dot_nt(high, other_mix) + dot_nt(low, other_mix)
    place += 2 * rank
    other_level = other[:, place : place + rank].astype(F32) + other[:, place + rank :].astype(F32)
    gram = square_of(own_level[...], ab, other_level)
    diag = eye_mask(gram.shape[0])
    mean = jnp.sum(jnp.where(diag, gram, 0.0), axis=(0, 1), keepdims=True) / gram.shape[0]
    return gram - jnp.where(diag, mean, 0.0), mean


def filter_kernel(count, first, last, used, *refs):
    grams, refs = refs[:count], refs[count:]
    compress, places, own, other, refs = *refs[:4], refs[4:]
    *out, pair, turned, sems = refs
    if not last:
        *sketch, packed, mix_out, level = out
        place = packed.shape[1] - 4 * own.shape[0]
        sketch = sketch[0] if sketch else packed
    rank, width = own.shape[0], pair.shape[1]
    if width < used:
        span = pl.ds(pl.multiple_of(places[0], 128), width)
    else:
        span = slice(0, width)
    copies = [
        pltpu.make_async_copy(source.at[:, span], pair.at[slice(i * rank, (i + 1) * rank)], sems.at[i])
        for i, source in enumerate((own, other))
    ]
    for copy in copies:
        copy.start()
    flip = places[1]
    for i in range(2):
        half = compress[pl.ds(pl.multiple_of((flip + i) % 2 * rank, 128), rank), :]
        turned[:, i * rank : (i + 1) * rank] = half.T
    if last:
        share = out[0].shape[0]
        compress_t = jnp.concatenate(
            [
                turned[pl.ds(pl.multiple_of(places[2 + i] * share, 8), share), :]
                for i in range(len(out))
            ],
            0,
        )
    else:
        compress_t = turned[...]
    gram, mean = first_gram(grams) if first else later_gram(*grams)
    size = gram.shape[0]
    eye = jnp.where(eye_mask(size), 1.0, 0.0)
    z = gram * lax.rsqrt(jnp.sum(gram * gram, axis=(0, 1), keepdims=True) + 1e-6)
    for step in range(K_ITERS):
        zh, zl = split(z)
        square = dot3_split(zh, zl, zh, zl)
        factor = split(1.5 * eye - 0.5 * square)
        if step < K_ITERS - 1:
            z = dot3_split(zh, zl, *factor)
        else:
            turn = dot3_split(*split(compress_t), zh, zl)
            mixing = 0.5 * (compress_t + dot3_split(*split(turn), *factor))
    for copy in copies:
        copy.wait()
    high, low = split(mixing)
    both = jnp.concatenate([high, low], 0)
    rows = mixing.shape[0]
    tile = next((t for t in (640, 512, 256, 128) if width % t == 0), width)
    for c in range(0, width, tile):
        part = dot(both, pair[:, c : c + tile])
        part = part[:rows] + part[rows:]
        if last:
            for i, piece in enumerate(out):
                piece[:, c : c + tile] = part[i * share : (i + 1) * share]
        else:
            sketch[:, c : c + tile] = part.astype(BF16)
    if not last:
        block = dot3_nt(dot3(mixing, gram + mean * eye), mixing)
        mix_out[...] = mixing
        level[...] = block
        packed[:, place : place + 2 * rank] = high
        high, low = split(block)
        packed[:, place + 2 * rank : place + 3 * rank] = high
        packed[:, place + 3 * rank :] = low


def filter_call(grams, compress, places, own, other, used, width, first, last, pieces, joint):
    rank = own.shape[0]
    if last:
        share = rank // lax.axis_size("tm")
        out = [jax.ShapeDtypeStruct((share, width), F32)] * pieces
    else:
        out = [] if joint else [jax.ShapeDtypeStruct((rank, width), BF16)]
        out += [
            jax.ShapeDtypeStruct((rank, width * joint + 4 * rank), BF16),
            jax.ShapeDtypeStruct((rank, 2 * rank), F32),
            jax.ShapeDtypeStruct((rank, rank), F32),
        ]
    args = [*grams, compress]
    return pl.pallas_call(
        functools.partial(filter_kernel, len(grams), first, last, used),
        in_specs=[VMEM] * len(args) + [SMEM, ANY, ANY],
        out_shape=out,
        scratch_shapes=[
            pltpu.VMEM((2 * rank, width), BF16),
            pltpu.VMEM((rank, 2 * rank), F32),
            pltpu.SemaphoreType.DMA((2,)),
        ],
        compiler_params=PARAMS,
        name="sign_filter",
    )(*args, places, own, other)


def swap(value, axis, mask):
    count = lax.axis_size(axis)
    return lax.ppermute(value, axis, [(source, source ^ mask) for source in range(count)])


def gather_parts(value, axis):
    count = lax.axis_size(axis)
    if count > 4 or count & (count - 1):
        return [lax.psum(value.astype(F32), axis)]
    return [value] + [swap(value, axis, mask) for mask in range(1, count)]


def join_kernel(offsets, *refs):
    out = refs[-1]
    width = refs[0].shape[1]
    for i, piece in enumerate(refs[:-1], 1):
        out[:, pl.ds(pl.multiple_of(offsets[i], 128), width)] = piece[...]


def join(offsets, pieces):
    share, width = pieces[0].shape
    return pl.pallas_call(
        join_kernel,
        in_specs=[SMEM] + [VMEM] * len(pieces),
        out_shape=jax.ShapeDtypeStruct((share, width * len(pieces)), F32),
        name="join",
    )(offsets, *pieces)


def on_device(record, fir_taps, gauge_lag, projector, compress):
    rows, cols = record.shape
    rank = projector.shape[1]
    count = lax.axis_size("tm")
    position = lax.axis_index("tm")
    depths = count.bit_length() - 1
    share = rank // count
    halo = lax.ppermute(
        record[rows - HALO :], "tm", [(source, source + 1) for source in range(count - 1)]
    )
    sketch = front(record, halo, gauge_lag, fir_taps[None, :], projector)

    widths = [cols]
    for depth in range(1, depths):
        widths.append(widths[-1] // 2 if widths[-1] % 256 == 0 else widths[-1])
    narrowed = [depth for depth in range(depths - 1) if widths[depth + 1] < widths[depth]]
    assert narrowed == list(range(len(narrowed)))
    span = 2 ** len(narrowed)

    def bit_of(where, bit):
        return where // 2**bit % 2

    def scalars(*values):
        return jnp.stack([position * 0 + value for value in values]).astype(jnp.int32)

    joined = [0]
    for part in range(span):
        source = position ^ part
        joined.append(sum([bit_of(source, bit) * (cols >> (bit + 1)) for bit in narrowed], 0))
    joined = scalars(*joined)
    kept = ahead = None
    for depth in range(depths):
        first, last = depth == 0, depth == depths - 1
        mask = 2**depth
        here = widths[depth]
        other = swap(sketch, "tm", mask)
        if first:
            grams = gather_parts(pair_gram(sketch, other), "chan")
        else:
            grams = [*kept, *ahead, other if packed is None else swap(packed, "tm", mask)]
        flip = bit_of(position, depth)
        if last:
            order = [position ^ part for part in range(span)]
            places = scalars(0, flip, *order)
            sketch, *kept = filter_call(
                grams, compress, places, sketch, other, here, here, first, last, span, False
            )
            continue
        width = widths[depth + 1]
        places = scalars(flip * (here // 2) if width < here else 0, flip)
        joint = depth + 1 == depths - 1
        sent = sketch if sketch.shape[1] == here else sketch[:, :here]
        part = ahead_gram(sketch, other, swap(sent, "tm", 2 * mask), here)
        out = filter_call(
            grams, compress, places, sketch, other, here, width, first, last, span, joint
        )
        for bit in [b for b in narrowed if b < depth]:
            part = (part.astype(F32) + swap(part, "tm", 2**bit).astype(F32)).astype(BF16)
        parts = gather_parts(part, "chan")
        total = sum(piece.astype(F32) for piece in parts).astype(BF16)
        ahead = [total, swap(total, "tm", mask)]
        sketch, *kept = out
        packed = None if joint else kept.pop(0)
    if span == 1:
        return sketch
    pieces = [sketch] + [
        swap(piece, "tm", part) for part, piece in enumerate(kept, 1)
    ]
    return join(joined, pieces)


def solution(mesh):
    return jax.shard_map(
        on_device,
        mesh=mesh,
        in_specs=(P("tm", "chan"), P(), P("chan"), P("tm", None), P()),
        out_specs=P("tm", "chan"),
        check_vma=False,
    )
```

```python
import functools

import jax
import jax.numpy as jnp
from jax import lax
from jax.experimental import pallas as pl
from jax.experimental.pallas import tpu as pltpu
from jax.sharding import PartitionSpec as P

TAPS = 64
GAUGE_MAX = 16
K_ITERS = 8
HALO = TAPS + GAUGE_MAX
BLOCK = 128
STEP = 16
CHUNK = 256
EXTRA = 16
F32 = jnp.float32
BF16 = jnp.bfloat16
ANY = pl.BlockSpec(memory_space=pl.ANY)
HBM = pl.BlockSpec(memory_space=pltpu.HBM)
SMEM = pl.BlockSpec(memory_space=pltpu.SMEM)
VMEM = pl.BlockSpec(memory_space=pltpu.VMEM)
PARAMS = pltpu.CompilerParams(vmem_limit_bytes=40 * 2**20)


def dot(a, b):
    return jnp.dot(a, b, preferred_element_type=F32)


def dot_nt(a, b):
    return lax.dot_general(a, b, (((1,), (1,)), ((), ())), preferred_element_type=F32)


def split(a):
    high = a.astype(BF16)
    return high, (a - high.astype(F32)).astype(BF16)


def dot3_split(ah, al, bh, bl):
    rows = ah.shape[0]
    wide = dot(jnp.concatenate([ah, al], 0), bh)
    return wide[:rows] + (wide[rows:] + dot(ah, bl))


def dot3(a, b):
    return dot3_split(*split(a), *split(b))


def dot3_nt(a, b):
    ah, al = split(a)
    bh, bl = split(b)
    return dot_nt(ah, bh) + (dot_nt(ah, bl) + dot_nt(al, bh))


def eye_mask(n):
    row = lax.broadcasted_iota(jnp.int32, (n, n), 0)
    col = lax.broadcasted_iota(jnp.int32, (n, n), 1)
    return row == col


def one_hot(shape, place):
    row = lax.broadcasted_iota(jnp.int32, shape, 0)
    col = lax.broadcasted_iota(jnp.int32, shape, 1)
    return jnp.where(place(row) == col, 1.0, 0.0).astype(BF16)


def front_kernel(first, last, *refs):
    if first == 0:
        record, halo, lag, band, weights, begun, out, strain = refs
    else:
        record, lag_ref, taps_ref, projector_ref, out, band, head_weights, head = refs[:8]
        strain, weights, lag, taps, projector, sems = refs[8:]
        halo = begun = None

        @pl.when(pl.program_id(0) == 0)
        def _():
            sources, targets = (lag_ref, taps_ref, projector_ref), (lag, taps, projector)
            copies = [
                pltpu.make_async_copy(source, target, sems.at[i])
                for i, (source, target) in enumerate(zip(sources, targets))
            ]
            for copy in copies:
                copy.start()
            for copy in copies:
                copy.wait()
            turn = one_hot((TAPS, 256), lambda tap: TAPS - tap)
            line = dot(jnp.broadcast_to(taps[...], (8, TAPS)), turn)[0:1]
            line = jnp.broadcast_to(line, (BLOCK, 256))
            rolled = pltpu.roll(line, 0, 1, stride=1, stride_axis=0)[:, : BLOCK + TAPS]
            order = one_hot((BLOCK, BLOCK), lambda row: row // 8 + STEP * (row % 8))
            band[...] = dot(order, rolled.astype(BF16)).astype(BF16)
            for block in range(projector.shape[0] // BLOCK):
                part = slice(block * BLOCK, (block + 1) * BLOCK)
                weights[:, part] = dot(order, projector[part, :]).T.astype(BF16)
            head_weights[...] = weights[:, 0:BLOCK]

    cols = record.shape[1]
    lane = min(128, cols)
    lanes = cols // lane
    group = 256 if cols % 256 == 0 else lane
    total = None
    used = first * BLOCK
    if first > 0:
        head[...] = record[0:BLOCK, :]
    top = lax.broadcasted_iota(jnp.int32, (STEP, 8, lane), 1) == 0

    def later(rows):
        return pltpu.roll(rows.reshape(STEP, 8, lane), 1, 1)

    before = {}
    for g in range(0, cols, group):
        if first == 0:
            result = dot(band[:, BLOCK + TAPS - HALO :], halo[:, g : g + group])
        else:
            result = dot(band[:, TAPS:], record[(first - 1) * BLOCK : first * BLOCK, g : g + group])
        for c in range(0, group, lane):
            before[g + c] = later(result[:, c : c + lane])
    for block in range(first, last):
        start = block * BLOCK
        for g in range(0, cols, group):
            if block == 0:
                segment = jnp.concatenate(
                    [halo[HALO - TAPS :, g : g + group], record[0:BLOCK, g : g + group]], 0
                )
            else:
                segment = record[start - TAPS : start + BLOCK, g : g + group]
            result = dot(band[...], segment)
            for c in range(0, group, lane):
                line = pl.program_id(0) * lanes + (g + c) // lane
                shift = GAUGE_MAX - lag[pl.ds(line, 1), :]
                here = result[:, c : c + lane]
                moved = later(here)
                early = jnp.where(top, before[g + c], moved).reshape(BLOCK, lane)
                before[g + c] = moved
                picked = jnp.concatenate([early, here], 0)
                for step in (8, 4, 2, 1):
                    length = BLOCK + 8 * (step - 1)
                    picked = jnp.where(
                        (shift & step) != 0, picked[8 * step : 8 * step + length], picked[:length]
                    )
                strain[start : start + BLOCK, g + c : g + c + lane] = (here - picked).astype(BF16)
        done = start + BLOCK
        if done % CHUNK == 0 or block == last - 1:
            part = dot(weights[:, used:done], strain[used:done, :])
            total = part if total is None else total + part
            used = done
    if begun is None:
        out[...] = total
    else:
        out[...] = (total + begun[...]).astype(BF16)


def front_call(blocks, args, in_specs, out_specs, out_shape, scratch, steps, grant):
    return pl.pallas_call(
        functools.partial(front_kernel, *blocks),
        grid=(steps,),
        in_specs=in_specs,
        out_specs=out_specs,
        out_shape=out_shape,
        scratch_shapes=scratch,
        compiler_params=pltpu.CompilerParams(vmem_limit_bytes=grant * 2**20),
        name="front",
    )(*args)


def front(record, halo, lag, taps, projector):
    rows, cols = record.shape
    rank = projector.shape[1]
    lag = lag.reshape(cols // 128, 128) if cols % 128 == 0 else lag[None, :]
    whole = lambda a: pl.BlockSpec(a.shape, lambda i: (0, 0))
    columns = lambda count, tile: pl.BlockSpec((count, tile), lambda i: (0, i))
    tile = next((t for t in (512, 640, 256, 128) if cols % t == 0), cols)
    shapes = [
        jax.ShapeDtypeStruct((rank, cols), F32),
        jax.ShapeDtypeStruct((BLOCK, BLOCK + TAPS), BF16),
        jax.ShapeDtypeStruct((rank, BLOCK), BF16),
        jax.ShapeDtypeStruct((BLOCK, cols), BF16),
    ]
    begun, band, weights, head = front_call(
        (1, rows // BLOCK),
        (record, lag, taps, projector),
        [columns(rows, tile), HBM, HBM, HBM],
        [columns(rank, tile), whole(shapes[1]), whole(shapes[2]), columns(BLOCK, tile)],
        shapes,
        [
            pltpu.VMEM((rows, tile), BF16),
            pltpu.VMEM((rank, rows), BF16),
            pltpu.VMEM(lag.shape, lag.dtype),
            pltpu.VMEM(taps.shape, BF16),
            pltpu.VMEM(projector.shape, BF16),
            pltpu.SemaphoreType.DMA((3,)),
        ],
        cols // tile,
        48,
    )
    tile = cols // 2 if cols % 256 == 0 else cols
    return front_call(
        (0, 1),
        (head, halo, lag, band, weights, begun),
        [
            columns(BLOCK, tile),
            columns(HALO, tile),
            whole(lag),
            whole(band),
            whole(weights),
            columns(rank, tile),
        ],
        columns(rank, tile),
        jax.ShapeDtypeStruct((rank, cols), BF16),
        [pltpu.VMEM((BLOCK, tile), BF16)],
        cols // tile,
        32,
    )


def pair_kernel(own, other, out):
    rank = own.shape[0]
    a, b = own[...], other[...]
    aa, ab, bb = dot_nt(a, a), dot_nt(a, b), dot_nt(b, b)
    diag = eye_mask(rank)
    trace = jnp.sum(jnp.where(diag, aa + bb, 0.0), axis=(0, 1), keepdims=True)
    mean = trace / (2 * rank)
    aa = aa - jnp.where(diag, mean, 0.0)
    bb = bb - jnp.where(diag, mean, 0.0)
    row = lax.broadcasted_iota(jnp.int32, (rank, rank), 0)
    col = lax.broadcasted_iota(jnp.int32, (rank, rank), 1)
    out[0:rank, :] = jnp.where(row <= col, aa, bb).astype(BF16)
    out[rank : 2 * rank, :] = ab.astype(BF16)
    bottom = jnp.sum(jnp.where(diag, bb, 0.0), axis=0, keepdims=True)
    full = jnp.broadcast_to(mean, (EXTRA, rank))
    high = full.astype(BF16).astype(F32)
    mid = (full - high).astype(BF16).astype(F32)
    low = full - high - mid
    line = lax.broadcasted_iota(jnp.int32, (EXTRA, rank), 0)
    extra = jnp.where(line == 0, high, jnp.where(line == 1, mid, jnp.where(line == 2, low, 0.0)))
    out[2 * rank :, :] = jnp.where(line == 3, jnp.broadcast_to(bottom, (EXTRA, rank)), extra).astype(
        BF16
    )


def pair_gram(own, other):
    rank = own.shape[0]
    return pl.pallas_call(
        pair_kernel,
        out_shape=jax.ShapeDtypeStruct((2 * rank + EXTRA, rank), BF16),
        compiler_params=PARAMS,
        name="pair_gram",
    )(own, other)


def ahead_kernel(width, own, sibling, partner, out):
    rank = own.shape[0]
    there = partner[:, :width]
    out[0:rank, :] = dot_nt(own[:, :width], there).astype(out.dtype)
    out[rank:, :] = dot_nt(sibling[:, :width], there).astype(out.dtype)


def ahead_gram(own, sibling, partner, width):
    rank = own.shape[0]
    return pl.pallas_call(
        functools.partial(ahead_kernel, width),
        out_shape=jax.ShapeDtypeStruct((2 * rank, rank), BF16),
        compiler_params=PARAMS,
        name="ahead_gram",
    )(own, sibling, partner)


def summed(parts):
    total = parts[0][...].astype(F32)
    for part in parts[1:]:
        total = total + part[...].astype(F32)
    return total


def square_of(aa, ab, bb):
    return jnp.concatenate(
        [jnp.concatenate([aa, ab], 1), jnp.concatenate([ab.T, bb], 1)], 0
    )


def first_gram(parts):
    total = summed(parts)
    rank = total.shape[1]
    both = total[0:rank]
    ab = total[rank : 2 * rank]
    extra = total[2 * rank :]
    mean = extra[0:1, 0:1] + extra[1:2, 0:1] + extra[2:3, 0:1]
    row = lax.broadcasted_iota(jnp.int32, (rank, rank), 0)
    col = lax.broadcasted_iota(jnp.int32, (rank, rank), 1)
    turned = both.T
    aa = jnp.where(row <= col, both, turned)
    bb = jnp.where(row > col, both, jnp.where(row < col, turned, extra[3:4, :]))
    return square_of(aa, ab, bb), mean


def later_gram(own_mix, own_level, ahead, sibling_ahead, other):
    rank = own_mix.shape[0]
    mine, theirs = ahead[...], sibling_ahead[...]
    cross = jnp.concatenate(
        [
            jnp.concatenate([mine[:rank], theirs[rank:]], 1),
            jnp.concatenate([mine[rank:], theirs[:rank]], 1),
        ],
        0,
    )
    high, low = split(own_mix[...])
    half = dot(high, cross) + dot(low, cross)
    high, low = split(half)
    place = other.shape[1] - 4 * rank
    other_mix = other[:, place : place + 2 * rank]
    ab = dot_nt(high, other_mix) + dot_nt(low, other_mix)
    place += 2 * rank
    other_level = other[:, place : place + rank].astype(F32) + other[:, place + rank :].astype(F32)
    gram = square_of(own_level[...], ab, other_level)
    diag = eye_mask(gram.shape[0])
    mean = jnp.sum(jnp.where(diag, gram, 0.0), axis=(0, 1), keepdims=True) / gram.shape[0]
    return gram - jnp.where(diag, mean, 0.0), mean


def filter_kernel(count, first, last, used, base, *refs):
    grams, refs = refs[:count], refs[count:]
    compress, places, own, other, refs = *refs[:4], refs[4:]
    *out, pair, turned, sems = refs
    if not last:
        *sketch, packed, mix_out, level = out
        place = packed.shape[1] - 4 * own.shape[0]
        sketch = sketch[0] if sketch else packed
    rank, width = own.shape[0], pair.shape[1]
    if width < used:
        span = pl.ds(pl.multiple_of(places[base], 128), width)
    else:
        span = slice(0, width)
    copies = [
        pltpu.make_async_copy(source.at[:, span], pair.at[slice(i * rank, (i + 1) * rank)], sems.at[i])
        for i, source in enumerate((own, other))
    ]
    for copy in copies:
        copy.start()
    flip = places[base + 1]
    for i in range(2):
        half = compress[pl.ds(pl.multiple_of((flip + i) % 2 * rank, 128), rank), :]
        turned[:, i * rank : (i + 1) * rank] = half.T
    if last:
        share = out[0].shape[0]
        compress_t = jnp.concatenate(
            [
                turned[pl.ds(pl.multiple_of(places[base + 2 + i] * share, 8), share), :]
                for i in range(len(out))
            ],
            0,
        )
    else:
        compress_t = turned[...]
    gram, mean = first_gram(grams) if first else later_gram(*grams)
    size = gram.shape[0]
    eye = jnp.where(eye_mask(size), 1.0, 0.0)
    z = gram * lax.rsqrt(jnp.sum(gram * gram, axis=(0, 1), keepdims=True) + 1e-6)
    for step in range(K_ITERS):
        zh, zl = split(z)
        square = dot3_split(zh, zl, zh, zl)
        factor = split(1.5 * eye - 0.5 * square)
        if step < K_ITERS - 1:
            z = dot3_split(zh, zl, *factor)
        else:
            turn = dot3_split(*split(compress_t), zh, zl)
            mixing = 0.5 * (compress_t + dot3_split(*split(turn), *factor))
    for copy in copies:
        copy.wait()
    high, low = split(mixing)
    both = jnp.concatenate([high, low], 0)
    rows = mixing.shape[0]
    tile = next((t for t in (640, 512, 256, 128) if width % t == 0), width)
    for c in range(0, width, tile):
        part = dot(both, pair[:, c : c + tile])
        part = part[:rows] + part[rows:]
        if last:
            for i, piece in enumerate(out):
                piece[:, c : c + tile] = part[i * share : (i + 1) * share]
        else:
            sketch[:, c : c + tile] = part.astype(BF16)
    if not last:
        block = dot3_nt(dot3(mixing, gram + mean * eye), mixing)
        mix_out[...] = mixing
        level[...] = block
        packed[:, place : place + 2 * rank] = high
        high, low = split(block)
        packed[:, place + 2 * rank : place + 3 * rank] = high
        packed[:, place + 3 * rank :] = low


def filter_call(grams, compress, places, base, own, other, used, width, first, last, pieces, joint):
    rank = own.shape[0]
    if last:
        share = rank // lax.axis_size("tm")
        out = [jax.ShapeDtypeStruct((share, width), F32)] * pieces
    else:
        out = [] if joint else [jax.ShapeDtypeStruct((rank, width), BF16)]
        out += [
            jax.ShapeDtypeStruct((rank, width * joint + 4 * rank), BF16),
            jax.ShapeDtypeStruct((rank, 2 * rank), F32),
            jax.ShapeDtypeStruct((rank, rank), F32),
        ]
    args = [*grams, compress]
    return pl.pallas_call(
        functools.partial(filter_kernel, len(grams), first, last, used, base),
        in_specs=[VMEM] * len(args) + [SMEM, ANY, ANY],
        out_shape=out,
        scratch_shapes=[
            pltpu.VMEM((2 * rank, width), BF16),
            pltpu.VMEM((rank, 2 * rank), F32),
            pltpu.SemaphoreType.DMA((2,)),
        ],
        compiler_params=PARAMS,
        name="sign_filter",
    )(*args, places, own, other)


def swap(value, axis, mask):
    count = lax.axis_size(axis)
    return lax.ppermute(value, axis, [(source, source ^ mask) for source in range(count)])


def gather_parts(value, axis):
    count = lax.axis_size(axis)
    if count > 4 or count & (count - 1):
        return [lax.psum(value.astype(F32), axis)]
    return [value] + [swap(value, axis, mask) for mask in range(1, count)]


def join_kernel(base, places, *refs):
    out = refs[-1]
    width = refs[0].shape[1]
    for i, piece in enumerate(refs[:-1]):
        out[:, pl.ds(pl.multiple_of(places[base + i], 128), width)] = piece[...]


def join(places, base, pieces):
    share, width = pieces[0].shape
    return pl.pallas_call(
        functools.partial(join_kernel, base),
        in_specs=[SMEM] + [VMEM] * len(pieces),
        out_shape=jax.ShapeDtypeStruct((share, width * len(pieces)), F32),
        compiler_params=pltpu.CompilerParams(vmem_limit_bytes=16 * 2**20),
        name="join",
    )(places, *pieces)


def on_device(record, fir_taps, gauge_lag, projector, compress):
    rows, cols = record.shape
    rank = projector.shape[1]
    count = lax.axis_size("tm")
    position = lax.axis_index("tm")
    depths = count.bit_length() - 1
    share = rank // count
    halo = lax.ppermute(
        record[rows - HALO :], "tm", [(source, source + 1) for source in range(count - 1)]
    )
    sketch = front(record, halo, gauge_lag, fir_taps[None, :], projector)

    widths = [cols]
    for depth in range(1, depths):
        widths.append(widths[-1] // 2 if widths[-1] % 256 == 0 else widths[-1])
    narrowed = [depth for depth in range(depths - 1) if widths[depth + 1] < widths[depth]]
    assert narrowed == list(range(len(narrowed)))
    span = 2 ** len(narrowed)

    def bit_of(where, bit):
        return where // 2**bit % 2

    places = []
    for depth in range(depths):
        half = widths[depth] // 2 if depth in narrowed else 0
        flip = bit_of(position, depth)
        places += [flip * half, flip]
    places += [position ^ part for part in range(span)]
    joined = len(places)
    for part in range(span):
        places.append(sum([bit_of(position ^ part, bit) * (cols >> (bit + 1)) for bit in narrowed], 0))
    places = jnp.stack([position * 0 + place for place in places]).astype(jnp.int32)
    kept = ahead = None
    for depth in range(depths):
        first, last = depth == 0, depth == depths - 1
        mask = 2**depth
        here = widths[depth]
        other = swap(sketch, "tm", mask)
        if first:
            grams = gather_parts(pair_gram(sketch, other), "chan")
        else:
            grams = [*kept, *ahead, other if packed is None else swap(packed, "tm", mask)]
        if last:
            sketch, *kept = filter_call(
                grams, compress, places, 2 * depth, sketch, other, here, here, first, last, span, False
            )
            continue
        width = widths[depth + 1]
        joint = depth + 1 == depths - 1
        sent = sketch if sketch.shape[1] == here else sketch[:, :here]
        part = ahead_gram(sketch, other, swap(sent, "tm", 2 * mask), here)
        out = filter_call(
            grams, compress, places, 2 * depth, sketch, other, here, width, first, last, span, joint
        )
        for bit in [b for b in narrowed if b < depth]:
            part = (part.astype(F32) + swap(part, "tm", 2**bit).astype(F32)).astype(BF16)
        parts = gather_parts(part, "chan")
        total = sum(piece.astype(F32) for piece in parts).astype(BF16)
        ahead = [total, swap(total, "tm", mask)]
        sketch, *kept = out
        packed = None if joint else kept.pop(0)
    if span == 1:
        return sketch
    pieces = [sketch] + [
        swap(piece, "tm", part) for part, piece in enumerate(kept, 1)
    ]
    return join(places, joined, pieces)


def solution(mesh):
    return jax.shard_map(
        on_device,
        mesh=mesh,
        in_specs=(P("tm", "chan"), P(), P("chan"), P("tm", None), P()),
        out_specs=P("tm", "chan"),
        check_vma=False,
    )
```

```python
import functools

import jax
import jax.numpy as jnp
from jax import lax
from jax.experimental import pallas as pl
from jax.experimental.pallas import tpu as pltpu
from jax.sharding import PartitionSpec as P

TAPS = 64
GAUGE_MAX = 16
K_ITERS = 8
HALO = TAPS + GAUGE_MAX
BLOCK = 128
STEP = 16
CHUNK = 256
EXTRA = 16
F32 = jnp.float32
BF16 = jnp.bfloat16
ANY = pl.BlockSpec(memory_space=pl.ANY)
HBM = pl.BlockSpec(memory_space=pltpu.HBM)
SMEM = pl.BlockSpec(memory_space=pltpu.SMEM)
VMEM = pl.BlockSpec(memory_space=pltpu.VMEM)
PARAMS = pltpu.CompilerParams(vmem_limit_bytes=40 * 2**20)


def dot(a, b):
    return jnp.dot(a, b, preferred_element_type=F32)


def dot_nt(a, b):
    return lax.dot_general(a, b, (((1,), (1,)), ((), ())), preferred_element_type=F32)


def split(a):
    high = a.astype(BF16)
    return high, (a - high.astype(F32)).astype(BF16)


def dot3_split(ah, al, bh, bl):
    rows = ah.shape[0]
    wide = dot(jnp.concatenate([ah, al], 0), bh)
    return wide[:rows] + (wide[rows:] + dot(ah, bl))


def dot3(a, b):
    return dot3_split(*split(a), *split(b))


def dot3_nt(a, b):
    ah, al = split(a)
    bh, bl = split(b)
    return dot_nt(ah, bh) + (dot_nt(ah, bl) + dot_nt(al, bh))


def eye_mask(n):
    row = lax.broadcasted_iota(jnp.int32, (n, n), 0)
    col = lax.broadcasted_iota(jnp.int32, (n, n), 1)
    return row == col


def one_hot(shape, place):
    row = lax.broadcasted_iota(jnp.int32, shape, 0)
    col = lax.broadcasted_iota(jnp.int32, shape, 1)
    return jnp.where(place(row) == col, 1.0, 0.0).astype(BF16)


def front_kernel(first, last, *refs):
    if first == 0:
        record, halo, lag, band, weights, begun, out, strain = refs
    else:
        record, lag_ref, taps_ref, projector_ref, out, band, head_weights, head = refs[:8]
        strain, weights, lag, taps, projector, sems = refs[8:]
        halo = begun = None

        @pl.when(pl.program_id(0) == 0)
        def _():
            sources, targets = (lag_ref, taps_ref, projector_ref), (lag, taps, projector)
            copies = [
                pltpu.make_async_copy(source, target, sems.at[i])
                for i, (source, target) in enumerate(zip(sources, targets))
            ]
            for copy in copies:
                copy.start()
            for copy in copies:
                copy.wait()
            turn = one_hot((TAPS, 256), lambda tap: TAPS - tap)
            line = dot(jnp.broadcast_to(taps[...], (8, TAPS)), turn)[0:1]
            line = jnp.broadcast_to(line, (BLOCK + GAUGE_MAX, 256))
            rolled = pltpu.roll(line, 0, 1, stride=1, stride_axis=0)[:, : BLOCK + HALO]
            order = one_hot((2 * BLOCK, BLOCK + GAUGE_MAX), lambda row: row // 8 + STEP * (row % 8))
            band[...] = dot(order, rolled.astype(BF16)).astype(BF16)
            order = one_hot((BLOCK, BLOCK), lambda row: row // 8 + STEP * (row % 8))
            for block in range(projector.shape[0] // BLOCK):
                part = slice(block * BLOCK, (block + 1) * BLOCK)
                weights[:, part] = dot(order, projector[part, :]).T.astype(BF16)
            head_weights[...] = weights[:, 0:BLOCK]

    cols = record.shape[1]
    lane = min(128, cols)
    lanes = cols // lane
    group = 256 if cols % 256 == 0 else lane
    total = None
    used = first * BLOCK
    if first > 0:
        head[...] = record[0:BLOCK, :]
    for block in range(first, last):
        start = block * BLOCK
        for g in range(0, cols, group):
            if block == 0:
                segment = jnp.concatenate([halo[:, g : g + group], record[0:BLOCK, g : g + group]], 0)
            else:
                segment = record[start - HALO : start + BLOCK, g : g + group]
            result = dot(band[...], segment)
            for c in range(0, group, lane):
                line = pl.program_id(0) * lanes + (g + c) // lane
                shift = GAUGE_MAX - lag[pl.ds(line, 1), :]
                wide = result[:, c : c + lane]
                picked = wide
                for step in (8, 4, 2, 1):
                    length = BLOCK + 8 * (step - 1)
                    picked = jnp.where(
                        (shift & step) != 0, picked[8 * step : 8 * step + length], picked[:length]
                    )
                strain[start : start + BLOCK, g + c : g + c + lane] = (wide[BLOCK:] - picked).astype(
                    BF16
                )
        done = start + BLOCK
        if done % CHUNK == 0 or block == last - 1:
            part = dot(weights[:, used:done], strain[used:done, :])
            total = part if total is None else total + part
            used = done
    if begun is None:
        out[...] = total
    else:
        out[...] = (total + begun[...]).astype(BF16)


def front_call(blocks, args, in_specs, out_specs, out_shape, scratch, steps, grant):
    return pl.pallas_call(
        functools.partial(front_kernel, *blocks),
        grid=(steps,),
        in_specs=in_specs,
        out_specs=out_specs,
        out_shape=out_shape,
        scratch_shapes=scratch,
        compiler_params=pltpu.CompilerParams(vmem_limit_bytes=grant * 2**20),
        name="front",
    )(*args)


def front(record, halo, lag, taps, projector):
    rows, cols = record.shape
    rank = projector.shape[1]
    lag = lag.reshape(cols // 128, 128) if cols % 128 == 0 else lag[None, :]
    whole = lambda a: pl.BlockSpec(a.shape, lambda i: (0, 0))
    columns = lambda count, tile: pl.BlockSpec((count, tile), lambda i: (0, i))
    tile = next((t for t in (512, 640, 256, 128) if cols % t == 0), cols)
    shapes = [
        jax.ShapeDtypeStruct((rank, cols), F32),
        jax.ShapeDtypeStruct((2 * BLOCK, BLOCK + HALO), BF16),
        jax.ShapeDtypeStruct((rank, BLOCK), BF16),
        jax.ShapeDtypeStruct((BLOCK, cols), BF16),
    ]
    begun, band, weights, head = front_call(
        (1, rows // BLOCK),
        (record, lag, taps, projector),
        [columns(rows, tile), HBM, HBM, HBM],
        [columns(rank, tile), whole(shapes[1]), whole(shapes[2]), columns(BLOCK, tile)],
        shapes,
        [
            pltpu.VMEM((rows, tile), BF16),
            pltpu.VMEM((rank, rows), BF16),
            pltpu.VMEM(lag.shape, lag.dtype),
            pltpu.VMEM(taps.shape, BF16),
            pltpu.VMEM(projector.shape, BF16),
            pltpu.SemaphoreType.DMA((3,)),
        ],
        cols // tile,
        48,
    )
    tile = cols // 2 if cols % 256 == 0 else cols
    return front_call(
        (0, 1),
        (head, halo, lag, band, weights, begun),
        [
            columns(BLOCK, tile),
            columns(HALO, tile),
            whole(lag),
            whole(band),
            whole(weights),
            columns(rank, tile),
        ],
        columns(rank, tile),
        jax.ShapeDtypeStruct((rank, cols), BF16),
        [pltpu.VMEM((BLOCK, tile), BF16)],
        cols // tile,
        32,
    )


def pair_kernel(own, other, out):
    rank = own.shape[0]
    a, b = own[...], other[...]
    aa, ab, bb = dot_nt(a, a), dot_nt(a, b), dot_nt(b, b)
    diag = eye_mask(rank)
    trace = jnp.sum(jnp.where(diag, aa + bb, 0.0), axis=(0, 1), keepdims=True)
    mean = trace / (2 * rank)
    aa = aa - jnp.where(diag, mean, 0.0)
    bb = bb - jnp.where(diag, mean, 0.0)
    row = lax.broadcasted_iota(jnp.int32, (rank, rank), 0)
    col = lax.broadcasted_iota(jnp.int32, (rank, rank), 1)
    out[0:rank, :] = jnp.where(row <= col, aa, bb).astype(BF16)
    out[rank : 2 * rank, :] = ab.astype(BF16)
    bottom = jnp.sum(jnp.where(diag, bb, 0.0), axis=0, keepdims=True)
    full = jnp.broadcast_to(mean, (EXTRA, rank))
    high = full.astype(BF16).astype(F32)
    mid = (full - high).astype(BF16).astype(F32)
    low = full - high - mid
    line = lax.broadcasted_iota(jnp.int32, (EXTRA, rank), 0)
    extra = jnp.where(line == 0, high, jnp.where(line == 1, mid, jnp.where(line == 2, low, 0.0)))
    out[2 * rank :, :] = jnp.where(line == 3, jnp.broadcast_to(bottom, (EXTRA, rank)), extra).astype(
        BF16
    )


def pair_gram(own, other):
    rank = own.shape[0]
    return pl.pallas_call(
        pair_kernel,
        out_shape=jax.ShapeDtypeStruct((2 * rank + EXTRA, rank), BF16),
        compiler_params=PARAMS,
        name="pair_gram",
    )(own, other)


def ahead_kernel(width, own, sibling, partner, out):
    rank = own.shape[0]
    there = partner[:, :width]
    out[0:rank, :] = dot_nt(own[:, :width], there).astype(out.dtype)
    out[rank:, :] = dot_nt(sibling[:, :width], there).astype(out.dtype)


def ahead_gram(own, sibling, partner, width):
    rank = own.shape[0]
    return pl.pallas_call(
        functools.partial(ahead_kernel, width),
        out_shape=jax.ShapeDtypeStruct((2 * rank, rank), BF16),
        compiler_params=PARAMS,
        name="ahead_gram",
    )(own, sibling, partner)


def summed(parts):
    total = parts[0][...].astype(F32)
    for part in parts[1:]:
        total = total + part[...].astype(F32)
    return total


def square_of(aa, ab, bb):
    return jnp.concatenate(
        [jnp.concatenate([aa, ab], 1), jnp.concatenate([ab.T, bb], 1)], 0
    )


def first_gram(parts):
    total = summed(parts)
    rank = total.shape[1]
    both = total[0:rank]
    ab = total[rank : 2 * rank]
    extra = total[2 * rank :]
    mean = extra[0:1, 0:1] + extra[1:2, 0:1] + extra[2:3, 0:1]
    row = lax.broadcasted_iota(jnp.int32, (rank, rank), 0)
    col = lax.broadcasted_iota(jnp.int32, (rank, rank), 1)
    turned = both.T
    aa = jnp.where(row <= col, both, turned)
    bb = jnp.where(row > col, both, jnp.where(row < col, turned, extra[3:4, :]))
    return square_of(aa, ab, bb), mean


def later_gram(own_mix, own_level, ahead, sibling_ahead, other):
    rank = own_mix.shape[0]
    mine, theirs = ahead[...], sibling_ahead[...]
    cross = jnp.concatenate(
        [
            jnp.concatenate([mine[:rank], theirs[rank:]], 1),
            jnp.concatenate([mine[rank:], theirs[:rank]], 1),
        ],
        0,
    )
    high, low = split(own_mix[...])
    half = dot(high, cross) + dot(low, cross)
    high, low = split(half)
    place = other.shape[1] - 4 * rank
    other_mix = other[:, place : place + 2 * rank]
    ab = dot_nt(high, other_mix) + dot_nt(low, other_mix)
    place += 2 * rank
    other_level = other[:, place : place + rank].astype(F32) + other[:, place + rank :].astype(F32)
    gram = square_of(own_level[...], ab, other_level)
    diag = eye_mask(gram.shape[0])
    mean = jnp.sum(jnp.where(diag, gram, 0.0), axis=(0, 1), keepdims=True) / gram.shape[0]
    return gram - jnp.where(diag, mean, 0.0), mean


def filter_kernel(count, first, last, used, base, *refs):
    grams, refs = refs[:count], refs[count:]
    compress, places, refs = refs[0], refs[1], refs[2:]
    if last:
        mix_out, turned = refs
        rank, share = compress.shape[1], mix_out.shape[0] // used
    else:
        own, other, sketch, packed, mix_out, level, pair, turned, sems = refs
        rank, width = own.shape[0], pair.shape[1]
        if width < used:
            span = pl.ds(pl.multiple_of(places[base], 128), width)
        else:
            span = slice(0, width)
        copies = [
            pltpu.make_async_copy(
                source.at[:, span], pair.at[slice(i * rank, (i + 1) * rank)], sems.at[i]
            )
            for i, source in enumerate((own, other))
        ]
        for copy in copies:
            copy.start()
    flip = places[base + 1]
    for i in range(2):
        half = compress[pl.ds(pl.multiple_of((flip + i) % 2 * rank, 128), rank), :]
        turned[:, i * rank : (i + 1) * rank] = half.T
    if last:
        parts = [
            turned[pl.ds(pl.multiple_of(places[base + 2 + i] * share, 8), share), :]
            for i in range(used)
        ]
        compress_t = jnp.concatenate(parts, 0) if used > 1 else parts[0]
    else:
        compress_t = turned[...]
    gram, mean = first_gram(grams) if first else later_gram(*grams)
    size = gram.shape[0]
    eye = jnp.where(eye_mask(size), 1.0, 0.0)
    z = gram * lax.rsqrt(jnp.sum(gram * gram, axis=(0, 1), keepdims=True) + 1e-6)
    for step in range(K_ITERS):
        zh, zl = split(z)
        square = dot3_split(zh, zl, zh, zl)
        factor = split(1.5 * eye - 0.5 * square)
        if step < K_ITERS - 1:
            z = dot3_split(zh, zl, *factor)
        else:
            turn = dot3_split(*split(compress_t), zh, zl)
            mixing = 0.5 * (compress_t + dot3_split(*split(turn), *factor))
    mix_out[...] = mixing
    if last:
        return
    for copy in copies:
        copy.wait()
    high, low = split(mixing)
    both = jnp.concatenate([high, low], 0)
    tile = next((t for t in (640, 512, 256, 128) if width % t == 0), width)
    for c in range(0, width, tile):
        part = dot(both, pair[:, c : c + tile])
        sketch[:, c : c + tile] = (part[:rank] + part[rank:]).astype(BF16)
    block = dot3_nt(dot3(mixing, gram + mean * eye), mixing)
    level[...] = block
    packed[:, : 2 * rank] = high
    high, low = split(block)
    packed[:, 2 * rank : 3 * rank] = high
    packed[:, 3 * rank :] = low


def filter_call(grams, compress, places, base, own, other, used, width, first):
    rank = own.shape[0]
    args = [*grams, compress]
    return pl.pallas_call(
        functools.partial(filter_kernel, len(grams), first, False, used, base),
        in_specs=[VMEM] * len(args) + [SMEM, ANY, ANY],
        out_shape=[
            jax.ShapeDtypeStruct((rank, width), BF16),
            jax.ShapeDtypeStruct((rank, 4 * rank), BF16),
            jax.ShapeDtypeStruct((rank, 2 * rank), F32),
            jax.ShapeDtypeStruct((rank, rank), F32),
        ],
        scratch_shapes=[
            pltpu.VMEM((2 * rank, width), BF16),
            pltpu.VMEM((rank, 2 * rank), F32),
            pltpu.SemaphoreType.DMA((2,)),
        ],
        compiler_params=PARAMS,
        name="sign_filter",
    )(*args, places, own, other)


def last_filter_call(grams, compress, places, base, first, share, pieces):
    rank = compress.shape[1]
    args = [*grams, compress]
    return pl.pallas_call(
        functools.partial(filter_kernel, len(grams), first, True, pieces, base),
        in_specs=[VMEM] * len(args) + [SMEM],
        out_shape=jax.ShapeDtypeStruct((share * pieces, 2 * rank), F32),
        scratch_shapes=[pltpu.VMEM((rank, 2 * rank), F32)],
        compiler_params=PARAMS,
        name="sign_filter",
    )(*args, places)


def mix_kernel(mixing, own, other, *out):
    rank = own.shape[0]
    rows, share = mixing.shape[0], out[0].shape[0]
    both = jnp.concatenate(split(mixing[...]), 0)
    width = own.shape[1]
    tile = next((t for t in (640, 512, 256, 128) if width % t == 0), width)
    for c in range(0, width, tile):
        span = slice(c, c + tile)
        part = dot(both, jnp.concatenate([own[:, span], other[:, span]], 0))
        part = part[:rows] + part[rows:]
        for i, piece in enumerate(out):
            piece[:, span] = part[i * share : (i + 1) * share]


def mix(mixing, own, other, pieces):
    shape = jax.ShapeDtypeStruct((mixing.shape[0] // pieces, own.shape[1]), F32)
    return pl.pallas_call(
        mix_kernel,
        out_shape=[shape] * pieces,
        compiler_params=pltpu.CompilerParams(vmem_limit_bytes=16 * 2**20),
        name="mix",
    )(mixing, own, other)


def swap(value, axis, mask):
    count = lax.axis_size(axis)
    return lax.ppermute(value, axis, [(source, source ^ mask) for source in range(count)])


def gather_parts(value, axis):
    count = lax.axis_size(axis)
    if count > 4 or count & (count - 1):
        return [lax.psum(value.astype(F32), axis)]
    return [value] + [swap(value, axis, mask) for mask in range(1, count)]


def join_kernel(base, places, *refs):
    out = refs[-1]
    width = refs[0].shape[1]
    for i, piece in enumerate(refs[:-1]):
        out[:, pl.ds(pl.multiple_of(places[base + i], 128), width)] = piece[...]


def join(places, base, pieces):
    share, width = pieces[0].shape
    return pl.pallas_call(
        functools.partial(join_kernel, base),
        in_specs=[SMEM] + [VMEM] * len(pieces),
        out_shape=jax.ShapeDtypeStruct((share, width * len(pieces)), F32),
        compiler_params=pltpu.CompilerParams(vmem_limit_bytes=16 * 2**20),
        name="join",
    )(places, *pieces)


def on_device(record, fir_taps, gauge_lag, projector, compress):
    rows, cols = record.shape
    rank = projector.shape[1]
    count = lax.axis_size("tm")
    position = lax.axis_index("tm")
    depths = count.bit_length() - 1
    share = rank // count
    halo = lax.ppermute(
        record[rows - HALO :], "tm", [(source, source + 1) for source in range(count - 1)]
    )
    sketch = front(record, halo, gauge_lag, fir_taps[None, :], projector)

    widths = [cols]
    for depth in range(1, depths):
        widths.append(cols // 2 if cols % 256 == 0 else cols)
    narrowed = [depth for depth in range(depths - 1) if widths[depth + 1] < widths[depth]]
    assert narrowed == list(range(len(narrowed)))
    span = 2 ** len(narrowed)

    def bit_of(where, bit):
        return where // 2**bit % 2

    places = []
    for depth in range(depths):
        half = widths[depth] // 2 if depth in narrowed else 0
        flip = bit_of(position, depth)
        places += [flip * half, flip]
    places += [position ^ part for part in range(span)]
    joined = len(places)
    for part in range(span):
        places.append(sum([bit_of(position ^ part, bit) * (cols >> (bit + 1)) for bit in narrowed], 0))
    places = jnp.stack([position * 0 + place for place in places]).astype(jnp.int32)
    kept = ahead = None
    for depth in range(depths):
        first, last = depth == 0, depth == depths - 1
        mask = 2**depth
        here = widths[depth]
        other = swap(sketch, "tm", mask)
        if first:
            grams = gather_parts(pair_gram(sketch, other), "chan")
        else:
            packed, *kept = kept
            grams = [*kept, *ahead, swap(packed, "tm", mask)]
        if last:
            mixing = last_filter_call(grams, compress, places, 2 * depth, first, share, span)
            pieces = mix(mixing, sketch, other, span)
            break
        part = ahead_gram(sketch, other, swap(sketch, "tm", 2 * mask), here)
        merged, *kept = filter_call(
            grams, compress, places, 2 * depth, sketch, other, here, widths[depth + 1], first
        )
        for bit in [b for b in narrowed if b < depth]:
            part = (part.astype(F32) + swap(part, "tm", 2**bit).astype(F32)).astype(BF16)
        parts = gather_parts(part, "chan")
        total = sum(piece.astype(F32) for piece in parts).astype(BF16)
        ahead = [total, swap(total, "tm", mask)]
        sketch = merged
    if span == 1:
        return pieces[0]
    pieces = [pieces[0]] + [swap(piece, "tm", part) for part, piece in enumerate(pieces[1:], 1)]
    return join(places, joined, pieces)


def solution(mesh):
    return jax.shard_map(
        on_device,
        mesh=mesh,
        in_specs=(P("tm", "chan"), P(), P("chan"), P("tm", None), P()),
        out_specs=P("tm", "chan"),
        check_vma=False,
    )
```

```python
import functools

import jax
import jax.numpy as jnp
from jax import lax
from jax.experimental import pallas as pl
from jax.experimental.pallas import tpu as pltpu
from jax.sharding import PartitionSpec as P

TAPS = 64
GAUGE_MAX = 16
K_ITERS = 8
HALO = TAPS + GAUGE_MAX
BLOCK = 128
STEP = 16
CHUNK = 256
EXTRA = 16
F32 = jnp.float32
BF16 = jnp.bfloat16
ANY = pl.BlockSpec(memory_space=pl.ANY)
HBM = pl.BlockSpec(memory_space=pltpu.HBM)
SMEM = pl.BlockSpec(memory_space=pltpu.SMEM)
VMEM = pl.BlockSpec(memory_space=pltpu.VMEM)
PARAMS = pltpu.CompilerParams(vmem_limit_bytes=40 * 2**20)


def dot(a, b):
    return jnp.dot(a, b, preferred_element_type=F32)


def dot_nt(a, b):
    return lax.dot_general(a, b, (((1,), (1,)), ((), ())), preferred_element_type=F32)


def split(a):
    high = a.astype(BF16)
    return high, (a - high.astype(F32)).astype(BF16)


def dot3_split(ah, al, bh, bl):
    rows = ah.shape[0]
    wide = dot(jnp.concatenate([ah, al], 0), bh)
    return wide[:rows] + (wide[rows:] + dot(ah, bl))


def dot3(a, b):
    return dot3_split(*split(a), *split(b))


def dot3_nt(a, b):
    ah, al = split(a)
    bh, bl = split(b)
    return dot_nt(ah, bh) + (dot_nt(ah, bl) + dot_nt(al, bh))


def eye_mask(n):
    row = lax.broadcasted_iota(jnp.int32, (n, n), 0)
    col = lax.broadcasted_iota(jnp.int32, (n, n), 1)
    return row == col


def one_hot(shape, place):
    row = lax.broadcasted_iota(jnp.int32, shape, 0)
    col = lax.broadcasted_iota(jnp.int32, shape, 1)
    return jnp.where(place(row) == col, 1.0, 0.0).astype(BF16)


def front_kernel(first, last, *refs):
    if first == 0:
        record, halo, lag, band, weights, begun, out, strain = refs
    else:
        record, lag_ref, taps_ref, projector_ref, out, band, head_weights, head = refs[:8]
        strain, weights, lag, taps, projector, sems = refs[8:]
        halo = begun = None

        @pl.when(pl.program_id(0) == 0)
        def _():
            sources, targets = (lag_ref, taps_ref, projector_ref), (lag, taps, projector)
            copies = [
                pltpu.make_async_copy(source, target, sems.at[i])
                for i, (source, target) in enumerate(zip(sources, targets))
            ]
            for copy in copies:
                copy.start()
            for copy in copies:
                copy.wait()
            turn = one_hot((TAPS, 256), lambda tap: TAPS - tap)
            line = dot(jnp.broadcast_to(taps[...], (8, TAPS)), turn)[0:1]
            line = jnp.broadcast_to(line, (BLOCK + GAUGE_MAX, 256))
            rolled = pltpu.roll(line, 0, 1, stride=1, stride_axis=0)[:, : BLOCK + HALO]
            order = one_hot((2 * BLOCK, BLOCK + GAUGE_MAX), lambda row: row // 8 + STEP * (row % 8))
            band[...] = dot(order, rolled.astype(BF16)).astype(BF16)
            order = one_hot((BLOCK, BLOCK), lambda row: row // 8 + STEP * (row % 8))
            for block in range(projector.shape[0] // BLOCK):
                part = slice(block * BLOCK, (block + 1) * BLOCK)
                weights[:, part] = dot(order, projector[part, :]).T.astype(BF16)
            head_weights[...] = weights[:, 0:BLOCK]

    cols = record.shape[1]
    lane = min(128, cols)
    lanes = cols // lane
    group = 256 if cols % 256 == 0 else lane
    total = None
    used = first * BLOCK
    if first > 0:
        head[...] = record[0:BLOCK, :]
    for block in range(first, last):
        start = block * BLOCK
        for g in range(0, cols, group):
            if block == 0:
                segment = jnp.concatenate([halo[:, g : g + group], record[0:BLOCK, g : g + group]], 0)
            else:
                segment = record[start - HALO : start + BLOCK, g : g + group]
            result = dot(band[...], segment)
            for c in range(0, group, lane):
                line = pl.program_id(0) * lanes + (g + c) // lane
                shift = GAUGE_MAX - lag[pl.ds(line, 1), :]
                wide = result[:, c : c + lane]
                picked = wide
                for step in (8, 4, 2, 1):
                    length = BLOCK + 8 * (step - 1)
                    picked = jnp.where(
                        (shift & step) != 0, picked[8 * step : 8 * step + length], picked[:length]
                    )
                strain[start : start + BLOCK, g + c : g + c + lane] = (wide[BLOCK:] - picked).astype(
                    BF16
                )
        done = start + BLOCK
        if done % CHUNK == 0 or block == last - 1:
            part = dot(weights[:, used:done], strain[used:done, :])
            total = part if total is None else total + part
            used = done
    if begun is None:
        out[...] = total
    else:
        out[...] = (total + begun[...]).astype(BF16)


def front_call(blocks, args, in_specs, out_specs, out_shape, scratch, steps, grant):
    return pl.pallas_call(
        functools.partial(front_kernel, *blocks),
        grid=(steps,),
        in_specs=in_specs,
        out_specs=out_specs,
        out_shape=out_shape,
        scratch_shapes=scratch,
        compiler_params=pltpu.CompilerParams(vmem_limit_bytes=grant * 2**20),
        name="front",
    )(*args)


def front(record, halo, lag, taps, projector):
    rows, cols = record.shape
    rank = projector.shape[1]
    lag = lag.reshape(cols // 128, 128) if cols % 128 == 0 else lag[None, :]
    whole = lambda a: pl.BlockSpec(a.shape, lambda i: (0, 0))
    columns = lambda count, tile: pl.BlockSpec((count, tile), lambda i: (0, i))
    tile = next((t for t in (512, 640, 256, 128) if cols % t == 0), cols)
    shapes = [
        jax.ShapeDtypeStruct((rank, cols), F32),
        jax.ShapeDtypeStruct((2 * BLOCK, BLOCK + HALO), BF16),
        jax.ShapeDtypeStruct((rank, BLOCK), BF16),
        jax.ShapeDtypeStruct((BLOCK, cols), BF16),
    ]
    begun, band, weights, head = front_call(
        (1, rows // BLOCK),
        (record, lag, taps, projector),
        [columns(rows, tile), HBM, HBM, HBM],
        [columns(rank, tile), whole(shapes[1]), whole(shapes[2]), columns(BLOCK, tile)],
        shapes,
        [
            pltpu.VMEM((rows, tile), BF16),
            pltpu.VMEM((rank, rows), BF16),
            pltpu.VMEM(lag.shape, lag.dtype),
            pltpu.VMEM(taps.shape, BF16),
            pltpu.VMEM(projector.shape, BF16),
            pltpu.SemaphoreType.DMA((3,)),
        ],
        cols // tile,
        48,
    )
    tile = cols // 2 if cols % 256 == 0 else cols
    return front_call(
        (0, 1),
        (head, halo, lag, band, weights, begun),
        [
            columns(BLOCK, tile),
            columns(HALO, tile),
            whole(lag),
            whole(band),
            whole(weights),
            columns(rank, tile),
        ],
        columns(rank, tile),
        jax.ShapeDtypeStruct((rank, cols), BF16),
        [pltpu.VMEM((BLOCK, tile), BF16)],
        cols // tile,
        32,
    )


def pair_kernel(own, other, out):
    rank = own.shape[0]
    a, b = own[...], other[...]
    aa, ab, bb = dot_nt(a, a), dot_nt(a, b), dot_nt(b, b)
    diag = eye_mask(rank)
    trace = jnp.sum(jnp.where(diag, aa + bb, 0.0), axis=(0, 1), keepdims=True)
    mean = trace / (2 * rank)
    aa = aa - jnp.where(diag, mean, 0.0)
    bb = bb - jnp.where(diag, mean, 0.0)
    row = lax.broadcasted_iota(jnp.int32, (rank, rank), 0)
    col = lax.broadcasted_iota(jnp.int32, (rank, rank), 1)
    out[0:rank, :] = jnp.where(row <= col, aa, bb).astype(BF16)
    out[rank : 2 * rank, :] = ab.astype(BF16)
    bottom = jnp.sum(jnp.where(diag, bb, 0.0), axis=0, keepdims=True)
    full = jnp.broadcast_to(mean, (EXTRA, rank))
    high = full.astype(BF16).astype(F32)
    mid = (full - high).astype(BF16).astype(F32)
    low = full - high - mid
    line = lax.broadcasted_iota(jnp.int32, (EXTRA, rank), 0)
    extra = jnp.where(line == 0, high, jnp.where(line == 1, mid, jnp.where(line == 2, low, 0.0)))
    out[2 * rank :, :] = jnp.where(line == 3, jnp.broadcast_to(bottom, (EXTRA, rank)), extra).astype(
        BF16
    )


def pair_gram(own, other):
    rank = own.shape[0]
    return pl.pallas_call(
        pair_kernel,
        out_shape=jax.ShapeDtypeStruct((2 * rank + EXTRA, rank), BF16),
        compiler_params=PARAMS,
        name="pair_gram",
    )(own, other)


def ahead_kernel(width, own, sibling, partner, out):
    rank = own.shape[0]
    there = partner[:, :width]
    out[0:rank, :] = dot_nt(own[:, :width], there).astype(out.dtype)
    out[rank:, :] = dot_nt(sibling[:, :width], there).astype(out.dtype)


def ahead_gram(own, sibling, partner, width):
    rank = own.shape[0]
    return pl.pallas_call(
        functools.partial(ahead_kernel, width),
        out_shape=jax.ShapeDtypeStruct((2 * rank, rank), BF16),
        compiler_params=PARAMS,
        name="ahead_gram",
    )(own, sibling, partner)


def summed(parts):
    total = parts[0][...].astype(F32)
    for part in parts[1:]:
        total = total + part[...].astype(F32)
    return total


def hold_kernel(*refs):
    pass


def hold(value, *until):
    return pl.pallas_call(
        hold_kernel,
        in_specs=[ANY] * (1 + len(until)),
        out_specs=ANY,
        out_shape=jax.ShapeDtypeStruct(value.shape, value.dtype),
        input_output_aliases={0: 0},
        compiler_params=pltpu.CompilerParams(vmem_limit_bytes=16 * 2**20),
        name="hold",
    )(value, *until)


def square_of(aa, ab, bb):
    return jnp.concatenate(
        [jnp.concatenate([aa, ab], 1), jnp.concatenate([ab.T, bb], 1)], 0
    )


def first_gram(parts):
    total = summed(parts)
    rank = total.shape[1]
    both = total[0:rank]
    ab = total[rank : 2 * rank]
    extra = total[2 * rank :]
    mean = extra[0:1, 0:1] + extra[1:2, 0:1] + extra[2:3, 0:1]
    row = lax.broadcasted_iota(jnp.int32, (rank, rank), 0)
    col = lax.broadcasted_iota(jnp.int32, (rank, rank), 1)
    turned = both.T
    aa = jnp.where(row <= col, both, turned)
    bb = jnp.where(row > col, both, jnp.where(row < col, turned, extra[3:4, :]))
    return square_of(aa, ab, bb), mean


def later_gram(own_mix, own_level, ahead, sibling_ahead, other):
    rank = own_mix.shape[0]
    mine, theirs = ahead[...], sibling_ahead[...]
    cross = jnp.concatenate(
        [
            jnp.concatenate([mine[:rank], theirs[rank:]], 1),
            jnp.concatenate([mine[rank:], theirs[:rank]], 1),
        ],
        0,
    )
    high, low = split(own_mix[...])
    half = dot(high, cross) + dot(low, cross)
    high, low = split(half)
    place = other.shape[1] - 4 * rank
    other_mix = other[:, place : place + 2 * rank]
    ab = dot_nt(high, other_mix) + dot_nt(low, other_mix)
    place += 2 * rank
    other_level = other[:, place : place + rank].astype(F32) + other[:, place + rank :].astype(F32)
    gram = square_of(own_level[...], ab, other_level)
    diag = eye_mask(gram.shape[0])
    mean = jnp.sum(jnp.where(diag, gram, 0.0), axis=(0, 1), keepdims=True) / gram.shape[0]
    return gram - jnp.where(diag, mean, 0.0), mean


def filter_kernel(count, first, last, used, base, *refs):
    grams, refs = refs[:count], refs[count:]
    compress, places, refs = refs[0], refs[1], refs[2:]
    if last:
        mix_out, turned = refs
        rank, share = compress.shape[1], mix_out.shape[0] // used
    else:
        own, other, sketch, packed, mix_out, level, pair, turned, sems = refs
        rank, width = own.shape[0], pair.shape[1]
        if width < used:
            span = pl.ds(pl.multiple_of(places[base], 128), width)
        else:
            span = slice(0, width)
        copies = [
            pltpu.make_async_copy(
                source.at[:, span], pair.at[slice(i * rank, (i + 1) * rank)], sems.at[i]
            )
            for i, source in enumerate((own, other))
        ]
        for copy in copies:
            copy.start()
    flip = places[base + 1]
    for i in range(2):
        half = compress[pl.ds(pl.multiple_of((flip + i) % 2 * rank, 128), rank), :]
        turned[:, i * rank : (i + 1) * rank] = half.T
    if last:
        parts = [
            turned[pl.ds(pl.multiple_of(places[base + 2 + i] * share, 8), share), :]
            for i in range(used)
        ]
        compress_t = jnp.concatenate(parts, 0) if used > 1 else parts[0]
    else:
        compress_t = turned[...]
    gram, mean = first_gram(grams) if first else later_gram(*grams)
    size = gram.shape[0]
    eye = jnp.where(eye_mask(size), 1.0, 0.0)
    z = gram * lax.rsqrt(jnp.sum(gram * gram, axis=(0, 1), keepdims=True) + 1e-6)
    for step in range(K_ITERS):
        zh, zl = split(z)
        square = dot3_split(zh, zl, zh, zl)
        factor = split(1.5 * eye - 0.5 * square)
        if step < K_ITERS - 1:
            z = dot3_split(zh, zl, *factor)
        else:
            turn = dot3_split(*split(compress_t), zh, zl)
            mixing = 0.5 * (compress_t + dot3_split(*split(turn), *factor))
    mix_out[...] = mixing
    if last:
        return
    for copy in copies:
        copy.wait()
    high, low = split(mixing)
    both = jnp.concatenate([high, low], 0)
    tile = next((t for t in (640, 512, 256, 128) if width % t == 0), width)
    for c in range(0, width, tile):
        part = dot(both, pair[:, c : c + tile])
        sketch[:, c : c + tile] = (part[:rank] + part[rank:]).astype(BF16)
    block = dot3_nt(dot3(mixing, gram + mean * eye), mixing)
    level[...] = block
    packed[:, : 2 * rank] = high
    high, low = split(block)
    packed[:, 2 * rank : 3 * rank] = high
    packed[:, 3 * rank :] = low


def filter_call(grams, compress, places, base, own, other, used, width, first):
    rank = own.shape[0]
    args = [*grams, compress]
    return pl.pallas_call(
        functools.partial(filter_kernel, len(grams), first, False, used, base),
        in_specs=[VMEM] * len(args) + [SMEM, ANY, ANY],
        out_shape=[
            jax.ShapeDtypeStruct((rank, width), BF16),
            jax.ShapeDtypeStruct((rank, 4 * rank), BF16),
            jax.ShapeDtypeStruct((rank, 2 * rank), F32),
            jax.ShapeDtypeStruct((rank, rank), F32),
        ],
        scratch_shapes=[
            pltpu.VMEM((2 * rank, width), BF16),
            pltpu.VMEM((rank, 2 * rank), F32),
            pltpu.SemaphoreType.DMA((2,)),
        ],
        compiler_params=PARAMS,
        name="sign_filter",
    )(*args, places, own, other)


def last_filter_call(grams, compress, places, base, first, share, pieces):
    rank = compress.shape[1]
    args = [*grams, compress]
    return pl.pallas_call(
        functools.partial(filter_kernel, len(grams), first, True, pieces, base),
        in_specs=[VMEM] * len(args) + [SMEM],
        out_shape=jax.ShapeDtypeStruct((share * pieces, 2 * rank), F32),
        scratch_shapes=[pltpu.VMEM((rank, 2 * rank), F32)],
        compiler_params=PARAMS,
        cost_estimate=pl.CostEstimate(
            flops=50 * K_ITERS * (2 * rank) ** 3, bytes_accessed=0, transcendentals=0
        ),
        name="sign_filter",
    )(*args, places)


def mix_kernel(mixing, own, other, *out):
    rank = own.shape[0]
    rows, share = mixing.shape[0], out[0].shape[0]
    both = jnp.concatenate(split(mixing[...]), 0)
    width = own.shape[1]
    tile = next((t for t in (640, 512, 256, 128) if width % t == 0), width)
    for c in range(0, width, tile):
        span = slice(c, c + tile)
        part = dot(both, jnp.concatenate([own[:, span], other[:, span]], 0))
        part = part[:rows] + part[rows:]
        for i, piece in enumerate(out):
            piece[:, span] = part[i * share : (i + 1) * share]


def mix(mixing, own, other, pieces):
    shape = jax.ShapeDtypeStruct((mixing.shape[0] // pieces, own.shape[1]), F32)
    return pl.pallas_call(
        mix_kernel,
        out_shape=[shape] * pieces,
        compiler_params=pltpu.CompilerParams(vmem_limit_bytes=16 * 2**20),
        name="mix",
    )(mixing, own, other)


def swap(value, axis, mask):
    count = lax.axis_size(axis)
    return lax.ppermute(value, axis, [(source, source ^ mask) for source in range(count)])


def gather_parts(value, axis):
    count = lax.axis_size(axis)
    if count > 4 or count & (count - 1):
        return [lax.psum(value.astype(F32), axis)]
    return [value] + [swap(value, axis, mask) for mask in range(1, count)]


def join_kernel(base, places, *refs):
    out = refs[-1]
    width = refs[0].shape[1]
    for i, piece in enumerate(refs[:-1]):
        out[:, pl.ds(pl.multiple_of(places[base + i], 128), width)] = piece[...]


def join(places, base, pieces):
    share, width = pieces[0].shape
    return pl.pallas_call(
        functools.partial(join_kernel, base),
        in_specs=[SMEM] + [VMEM] * len(pieces),
        out_shape=jax.ShapeDtypeStruct((share, width * len(pieces)), F32),
        compiler_params=pltpu.CompilerParams(vmem_limit_bytes=16 * 2**20),
        name="join",
    )(places, *pieces)


def on_device(record, fir_taps, gauge_lag, projector, compress):
    rows, cols = record.shape
    rank = projector.shape[1]
    count = lax.axis_size("tm")
    position = lax.axis_index("tm")
    depths = count.bit_length() - 1
    share = rank // count
    halo = lax.ppermute(
        record[rows - HALO :], "tm", [(source, source + 1) for source in range(count - 1)]
    )
    sketch = front(record, halo, gauge_lag, fir_taps[None, :], projector)

    widths = [cols]
    for depth in range(1, depths):
        widths.append(cols // 2 if cols % 256 == 0 else cols)
    narrowed = [depth for depth in range(depths - 1) if widths[depth + 1] < widths[depth]]
    assert narrowed == list(range(len(narrowed)))
    span = 2 ** len(narrowed)

    def bit_of(where, bit):
        return where // 2**bit % 2

    places = []
    for depth in range(depths):
        half = widths[depth] // 2 if depth in narrowed else 0
        flip = bit_of(position, depth)
        places += [flip * half, flip]
    places += [position ^ part for part in range(span)]
    joined = len(places)
    for part in range(span):
        places.append(sum([bit_of(position ^ part, bit) * (cols >> (bit + 1)) for bit in narrowed], 0))
    places = jnp.stack([position * 0 + place for place in places]).astype(jnp.int32)
    kept = ahead = None
    for depth in range(depths):
        first, last = depth == 0, depth == depths - 1
        mask = 2**depth
        here = widths[depth]
        if not last:
            other = swap(sketch, "tm", mask)
        if first:
            grams = gather_parts(pair_gram(sketch, other), "chan")
        else:
            packed, *kept = kept
            grams = [*kept, *ahead, swap(packed, "tm", mask)]
        if last:
            if not first:
                sketch = hold(sketch, *grams[-2:])
            other = swap(sketch, "tm", mask)
            mixing = last_filter_call(grams, compress, places, 2 * depth, first, share, span)
            pieces = mix(mixing, sketch, other, span)
            break
        part = ahead_gram(sketch, other, swap(sketch, "tm", 2 * mask), here)
        merged, *kept = filter_call(
            grams, compress, places, 2 * depth, sketch, other, here, widths[depth + 1], first
        )
        for bit in [b for b in narrowed if b < depth]:
            part = (part.astype(F32) + swap(part, "tm", 2**bit).astype(F32)).astype(BF16)
        parts = gather_parts(part, "chan")
        total = sum(piece.astype(F32) for piece in parts).astype(BF16)
        ahead = [total, swap(total, "tm", mask)]
        sketch = merged
    if span == 1:
        return pieces[0]
    pieces = [pieces[0]] + [swap(piece, "tm", part) for part, piece in enumerate(pieces[1:], 1)]
    return join(places, joined, pieces)


def solution(mesh):
    return jax.shard_map(
        on_device,
        mesh=mesh,
        in_specs=(P("tm", "chan"), P(), P("chan"), P("tm", None), P()),
        out_specs=P("tm", "chan"),
        check_vma=False,
    )
```

```python
import functools

import jax
import jax.numpy as jnp
from jax import lax
from jax.experimental import pallas as pl
from jax.experimental.pallas import tpu as pltpu
from jax.sharding import PartitionSpec as P

TAPS = 64
GAUGE_MAX = 16
K_ITERS = 8
HALO = TAPS + GAUGE_MAX
BLOCK = 128
STEP = 16
CHUNK = 256
EXTRA = 16
F32 = jnp.float32
BF16 = jnp.bfloat16
ANY = pl.BlockSpec(memory_space=pl.ANY)
HBM = pl.BlockSpec(memory_space=pltpu.HBM)
SMEM = pl.BlockSpec(memory_space=pltpu.SMEM)
VMEM = pl.BlockSpec(memory_space=pltpu.VMEM)
PARAMS = pltpu.CompilerParams(vmem_limit_bytes=40 * 2**20)


def dot(a, b):
    return jnp.dot(a, b, preferred_element_type=F32)


def dot_nt(a, b):
    return lax.dot_general(a, b, (((1,), (1,)), ((), ())), preferred_element_type=F32)


def split(a):
    high = a.astype(BF16)
    return high, (a - high.astype(F32)).astype(BF16)


def dot3_split(ah, al, bh, bl):
    rows = ah.shape[0]
    wide = dot(jnp.concatenate([ah, al], 0), bh)
    return wide[:rows] + (wide[rows:] + dot(ah, bl))


def dot3(a, b):
    return dot3_split(*split(a), *split(b))


def dot3_nt(a, b):
    ah, al = split(a)
    bh, bl = split(b)
    return dot_nt(ah, bh) + (dot_nt(ah, bl) + dot_nt(al, bh))


def eye_mask(n):
    row = lax.broadcasted_iota(jnp.int32, (n, n), 0)
    col = lax.broadcasted_iota(jnp.int32, (n, n), 1)
    return row == col


def one_hot(shape, place):
    row = lax.broadcasted_iota(jnp.int32, shape, 0)
    col = lax.broadcasted_iota(jnp.int32, shape, 1)
    return jnp.where(place(row) == col, 1.0, 0.0).astype(BF16)


def front_kernel(first, last, *refs):
    if first == 0:
        record, halo, lag, band, weights, begun, out, strain = refs
    else:
        record, lag_ref, taps_ref, projector_ref, out, band, head_weights, head = refs[:8]
        strain, weights, lag, taps, projector, sems = refs[8:]
        halo = begun = None

        @pl.when(pl.program_id(0) == 0)
        def _():
            sources, targets = (lag_ref, taps_ref, projector_ref), (lag, taps, projector)
            copies = [
                pltpu.make_async_copy(source, target, sems.at[i])
                for i, (source, target) in enumerate(zip(sources, targets))
            ]
            for copy in copies:
                copy.start()
            for copy in copies:
                copy.wait()
            turn = one_hot((TAPS, 256), lambda tap: TAPS - tap)
            line = dot(jnp.broadcast_to(taps[...], (8, TAPS)), turn)[0:1]
            line = jnp.broadcast_to(line, (BLOCK + GAUGE_MAX, 256))
            rolled = pltpu.roll(line, 0, 1, stride=1, stride_axis=0)[:, : BLOCK + HALO]
            order = one_hot((2 * BLOCK, BLOCK + GAUGE_MAX), lambda row: row // 8 + STEP * (row % 8))
            band[...] = dot(order, rolled.astype(BF16)).astype(BF16)
            order = one_hot((BLOCK, BLOCK), lambda row: row // 8 + STEP * (row % 8))
            for block in range(projector.shape[0] // BLOCK):
                part = slice(block * BLOCK, (block + 1) * BLOCK)
                weights[:, part] = dot(order, projector[part, :]).T.astype(BF16)
            head_weights[...] = weights[:, 0:BLOCK]

    cols = record.shape[1]
    lane = min(128, cols)
    lanes = cols // lane
    group = 256 if cols % 256 == 0 else lane
    total = None
    used = first * BLOCK
    if first > 0:
        head[...] = record[0:BLOCK, :]
    for block in range(first, last):
        start = block * BLOCK
        for g in range(0, cols, group):
            if block == 0:
                segment = jnp.concatenate([halo[:, g : g + group], record[0:BLOCK, g : g + group]], 0)
            else:
                segment = record[start - HALO : start + BLOCK, g : g + group]
            result = dot(band[...], segment)
            for c in range(0, group, lane):
                line = pl.program_id(0) * lanes + (g + c) // lane
                shift = GAUGE_MAX - lag[pl.ds(line, 1), :]
                wide = result[:, c : c + lane]
                picked = wide
                for step in (8, 4, 2, 1):
                    length = BLOCK + 8 * (step - 1)
                    picked = jnp.where(
                        (shift & step) != 0, picked[8 * step : 8 * step + length], picked[:length]
                    )
                strain[start : start + BLOCK, g + c : g + c + lane] = (wide[BLOCK:] - picked).astype(
                    BF16
                )
        done = start + BLOCK
        if done % CHUNK == 0 or block == last - 1:
            part = dot(weights[:, used:done], strain[used:done, :])
            total = part if total is None else total + part
            used = done
    if begun is None:
        out[...] = total
    else:
        out[...] = (total + begun[...]).astype(BF16)


def front_call(blocks, args, in_specs, out_specs, out_shape, scratch, steps, grant):
    return pl.pallas_call(
        functools.partial(front_kernel, *blocks),
        grid=(steps,),
        in_specs=in_specs,
        out_specs=out_specs,
        out_shape=out_shape,
        scratch_shapes=scratch,
        compiler_params=pltpu.CompilerParams(vmem_limit_bytes=grant * 2**20),
        name="front",
    )(*args)


def front(record, halo, lag, taps, projector):
    rows, cols = record.shape
    rank = projector.shape[1]
    lag = lag.reshape(cols // 128, 128) if cols % 128 == 0 else lag[None, :]
    whole = lambda a: pl.BlockSpec(a.shape, lambda i: (0, 0))
    columns = lambda count, tile: pl.BlockSpec((count, tile), lambda i: (0, i))
    tile = next((t for t in (512, 640, 256, 128) if cols % t == 0), cols)
    shapes = [
        jax.ShapeDtypeStruct((rank, cols), F32),
        jax.ShapeDtypeStruct((2 * BLOCK, BLOCK + HALO), BF16),
        jax.ShapeDtypeStruct((rank, BLOCK), BF16),
        jax.ShapeDtypeStruct((BLOCK, cols), BF16),
    ]
    begun, band, weights, head = front_call(
        (1, rows // BLOCK),
        (record, lag, taps, projector),
        [columns(rows, tile), HBM, HBM, HBM],
        [columns(rank, tile), whole(shapes[1]), whole(shapes[2]), columns(BLOCK, tile)],
        shapes,
        [
            pltpu.VMEM((rows, tile), BF16),
            pltpu.VMEM((rank, rows), BF16),
            pltpu.VMEM(lag.shape, lag.dtype),
            pltpu.VMEM(taps.shape, BF16),
            pltpu.VMEM(projector.shape, BF16),
            pltpu.SemaphoreType.DMA((3,)),
        ],
        cols // tile,
        48,
    )
    tile = cols // 2 if cols % 256 == 0 else cols
    return front_call(
        (0, 1),
        (head, halo, lag, band, weights, begun),
        [
            columns(BLOCK, tile),
            columns(HALO, tile),
            whole(lag),
            whole(band),
            whole(weights),
            columns(rank, tile),
        ],
        columns(rank, tile),
        jax.ShapeDtypeStruct((rank, cols), BF16),
        [pltpu.VMEM((BLOCK, tile), BF16)],
        cols // tile,
        32,
    )


def pair_kernel(own, other, out):
    rank = own.shape[0]
    a, b = own[...], other[...]
    aa, ab, bb = dot_nt(a, a), dot_nt(a, b), dot_nt(b, b)
    diag = eye_mask(rank)
    trace = jnp.sum(jnp.where(diag, aa + bb, 0.0), axis=(0, 1), keepdims=True)
    mean = trace / (2 * rank)
    aa = aa - jnp.where(diag, mean, 0.0)
    bb = bb - jnp.where(diag, mean, 0.0)
    row = lax.broadcasted_iota(jnp.int32, (rank, rank), 0)
    col = lax.broadcasted_iota(jnp.int32, (rank, rank), 1)
    out[0:rank, :] = jnp.where(row <= col, aa, bb).astype(BF16)
    out[rank : 2 * rank, :] = ab.astype(BF16)
    bottom = jnp.sum(jnp.where(diag, bb, 0.0), axis=0, keepdims=True)
    full = jnp.broadcast_to(mean, (EXTRA, rank))
    high = full.astype(BF16).astype(F32)
    mid = (full - high).astype(BF16).astype(F32)
    low = full - high - mid
    line = lax.broadcasted_iota(jnp.int32, (EXTRA, rank), 0)
    extra = jnp.where(line == 0, high, jnp.where(line == 1, mid, jnp.where(line == 2, low, 0.0)))
    out[2 * rank :, :] = jnp.where(line == 3, jnp.broadcast_to(bottom, (EXTRA, rank)), extra).astype(
        BF16
    )


def pair_gram(own, other):
    rank = own.shape[0]
    return pl.pallas_call(
        pair_kernel,
        out_shape=jax.ShapeDtypeStruct((2 * rank + EXTRA, rank), BF16),
        compiler_params=PARAMS,
        name="pair_gram",
    )(own, other)


def ahead_kernel(width, own, sibling, partner, *refs):
    out = refs[-1]
    rank = own.shape[0]
    there = partner[:, :width]
    out[0:rank, :] = dot_nt(own[:, :width], there).astype(out.dtype)
    out[rank:, :] = dot_nt(sibling[:, :width], there).astype(out.dtype)


def ahead_gram(own, sibling, partner, width, *after):
    rank = own.shape[0]
    return pl.pallas_call(
        functools.partial(ahead_kernel, width),
        in_specs=[VMEM] * 3 + [ANY] * len(after),
        out_shape=jax.ShapeDtypeStruct((2 * rank, rank), BF16),
        compiler_params=PARAMS,
        name="ahead_gram",
    )(own, sibling, partner, *after)


def summed(parts):
    total = parts[0][...].astype(F32)
    for part in parts[1:]:
        total = total + part[...].astype(F32)
    return total


def hold_kernel(*refs):
    pass


def hold(value, *until):
    return pl.pallas_call(
        hold_kernel,
        in_specs=[ANY] * (1 + len(until)),
        out_specs=ANY,
        out_shape=jax.ShapeDtypeStruct(value.shape, value.dtype),
        input_output_aliases={0: 0},
        compiler_params=pltpu.CompilerParams(vmem_limit_bytes=16 * 2**20),
        name="hold",
    )(value, *until)


def square_of(aa, ab, bb):
    return jnp.concatenate(
        [jnp.concatenate([aa, ab], 1), jnp.concatenate([ab.T, bb], 1)], 0
    )


def first_gram(parts):
    total = summed(parts)
    rank = total.shape[1]
    both = total[0:rank]
    ab = total[rank : 2 * rank]
    extra = total[2 * rank :]
    mean = extra[0:1, 0:1] + extra[1:2, 0:1] + extra[2:3, 0:1]
    row = lax.broadcasted_iota(jnp.int32, (rank, rank), 0)
    col = lax.broadcasted_iota(jnp.int32, (rank, rank), 1)
    turned = both.T
    aa = jnp.where(row <= col, both, turned)
    bb = jnp.where(row > col, both, jnp.where(row < col, turned, extra[3:4, :]))
    return square_of(aa, ab, bb), mean


def later_gram(own_mix, own_level, ahead, sibling_ahead, other):
    rank = own_mix.shape[0]
    mine, theirs = ahead[...], sibling_ahead[...]
    cross = jnp.concatenate(
        [
            jnp.concatenate([mine[:rank], theirs[rank:]], 1),
            jnp.concatenate([mine[rank:], theirs[:rank]], 1),
        ],
        0,
    )
    high, low = split(own_mix[...])
    half = dot(high, cross) + dot(low, cross)
    high, low = split(half)
    place = other.shape[1] - 4 * rank
    other_mix = other[:, place : place + 2 * rank]
    ab = dot_nt(high, other_mix) + dot_nt(low, other_mix)
    place += 2 * rank
    other_level = other[:, place : place + rank].astype(F32) + other[:, place + rank :].astype(F32)
    gram = square_of(own_level[...], ab, other_level)
    diag = eye_mask(gram.shape[0])
    mean = jnp.sum(jnp.where(diag, gram, 0.0), axis=(0, 1), keepdims=True) / gram.shape[0]
    return gram - jnp.where(diag, mean, 0.0), mean


def filter_kernel(count, first, kind, used, base, *refs):
    grams, refs = refs[:count], refs[count:]
    compress, places, refs = refs[0], refs[1], refs[2:]
    last = kind == "last"
    rank = compress.shape[1]
    if last:
        mix_out, turned = refs
        share = mix_out.shape[0] // used
    elif kind == "level":
        mix_out, packed, level, turned = refs
    else:
        own, other, mix_out, sketch, whole, pair, turned, sems = refs
        width = pair.shape[1]
        if width < used:
            span = pl.ds(pl.multiple_of(places[base], 128), width)
        else:
            span = slice(0, width)
        copies = [
            pltpu.make_async_copy(
                source.at[:, span], pair.at[slice(i * rank, (i + 1) * rank)], sems.at[i]
            )
            for i, source in enumerate((own, other))
        ]
        for copy in copies:
            copy.start()
    flip = places[base + 1]
    for i in range(2):
        half = compress[pl.ds(pl.multiple_of((flip + i) % 2 * rank, 128), rank), :]
        turned[:, i * rank : (i + 1) * rank] = half.T
    if last:
        parts = [
            turned[pl.ds(pl.multiple_of(places[base + 2 + i] * share, 8), share), :]
            for i in range(used)
        ]
        compress_t = jnp.concatenate(parts, 0) if used > 1 else parts[0]
    else:
        compress_t = turned[...]
    gram, mean = first_gram(grams) if first else later_gram(*grams)
    size = gram.shape[0]
    eye = jnp.where(eye_mask(size), 1.0, 0.0)
    z = gram * lax.rsqrt(jnp.sum(gram * gram, axis=(0, 1), keepdims=True) + 1e-6)
    for step in range(K_ITERS):
        zh, zl = split(z)
        square = dot3_split(zh, zl, zh, zl)
        factor = split(1.5 * eye - 0.5 * square)
        if step < K_ITERS - 1:
            z = dot3_split(zh, zl, *factor)
        else:
            turn = dot3_split(*split(compress_t), zh, zl)
            mixing = 0.5 * (compress_t + dot3_split(*split(turn), *factor))
    mix_out[...] = mixing
    if last:
        return
    full = gram + mean * eye
    if kind == "level":
        pack_level(mixing, full, packed, level)
        return
    whole[...] = full
    for copy in copies:
        copy.wait()
    both = jnp.concatenate(split(mixing), 0)
    tile = next((t for t in (640, 512, 256, 128) if width % t == 0), width)
    for c in range(0, width, tile):
        part = dot(both, pair[:, c : c + tile])
        sketch[:, c : c + tile] = (part[:rank] + part[rank:]).astype(BF16)


def pack_level(mixing, full, packed, level):
    rank = mixing.shape[0]
    block = dot3_nt(dot3(mixing, full), mixing)
    level[...] = block
    packed[:, : 2 * rank] = mixing.astype(BF16)
    high, low = split(block)
    packed[:, 2 * rank : 3 * rank] = high
    packed[:, 3 * rank :] = low


def level_kernel(mixing, full, packed, level):
    pack_level(mixing[...], full[...], packed, level)


def level_shapes(rank):
    return [
        jax.ShapeDtypeStruct((rank, 4 * rank), BF16),
        jax.ShapeDtypeStruct((rank, rank), F32),
    ]


def level_call(mixing, full):
    return pl.pallas_call(
        level_kernel,
        out_shape=level_shapes(mixing.shape[0]),
        compiler_params=pltpu.CompilerParams(vmem_limit_bytes=16 * 2**20),
        name="level",
    )(mixing, full)


def level_filter_call(grams, compress, places, base, first):
    rank = compress.shape[1]
    args = [*grams, compress]
    return pl.pallas_call(
        functools.partial(filter_kernel, len(grams), first, "level", 0, base),
        in_specs=[VMEM] * len(args) + [SMEM],
        out_shape=[jax.ShapeDtypeStruct((rank, 2 * rank), F32), *level_shapes(rank)],
        scratch_shapes=[pltpu.VMEM((rank, 2 * rank), F32)],
        compiler_params=PARAMS,
        name="sign_filter",
    )(*args, places)


def filter_call(grams, compress, places, base, own, other, used, width, first):
    rank = own.shape[0]
    args = [*grams, compress]
    return pl.pallas_call(
        functools.partial(filter_kernel, len(grams), first, "sketch", used, base),
        in_specs=[VMEM] * len(args) + [SMEM, ANY, ANY],
        out_shape=[
            jax.ShapeDtypeStruct((rank, 2 * rank), F32),
            jax.ShapeDtypeStruct((rank, width), BF16),
            jax.ShapeDtypeStruct((2 * rank, 2 * rank), F32),
        ],
        scratch_shapes=[
            pltpu.VMEM((2 * rank, width), BF16),
            pltpu.VMEM((rank, 2 * rank), F32),
            pltpu.SemaphoreType.DMA((2,)),
        ],
        compiler_params=PARAMS,
        name="sign_filter",
    )(*args, places, own, other)


def last_filter_call(grams, compress, places, base, first, share, pieces):
    rank = compress.shape[1]
    args = [*grams, compress]
    return pl.pallas_call(
        functools.partial(filter_kernel, len(grams), first, "last", pieces, base),
        in_specs=[VMEM] * len(args) + [SMEM],
        out_shape=jax.ShapeDtypeStruct((share * pieces, 2 * rank), F32),
        scratch_shapes=[pltpu.VMEM((rank, 2 * rank), F32)],
        compiler_params=PARAMS,
        cost_estimate=pl.CostEstimate(
            flops=50 * K_ITERS * (2 * rank) ** 3, bytes_accessed=0, transcendentals=0
        ),
        name="sign_filter",
    )(*args, places)


def mix_kernel(mixing, own, other, *out):
    rank = own.shape[0]
    rows, share = mixing.shape[0], out[0].shape[0]
    both = jnp.concatenate(split(mixing[...]), 0)
    width = own.shape[1]
    tile = next((t for t in (640, 512, 256, 128) if width % t == 0), width)
    for c in range(0, width, tile):
        span = slice(c, c + tile)
        part = dot(both, jnp.concatenate([own[:, span], other[:, span]], 0))
        part = part[:rows] + part[rows:]
        for i, piece in enumerate(out):
            piece[:, span] = part[i * share : (i + 1) * share].astype(piece.dtype)


def mix(mixing, own, other, pieces, dtype):
    shape = jax.ShapeDtypeStruct((mixing.shape[0] // pieces, own.shape[1]), dtype)
    return pl.pallas_call(
        mix_kernel,
        out_shape=[shape] * pieces,
        compiler_params=pltpu.CompilerParams(vmem_limit_bytes=16 * 2**20),
        name="mix",
    )(mixing, own, other)


def swap(value, axis, mask):
    count = lax.axis_size(axis)
    return lax.ppermute(value, axis, [(source, source ^ mask) for source in range(count)])


def gather_parts(value, axis):
    count = lax.axis_size(axis)
    if count > 4 or count & (count - 1):
        return [lax.psum(value.astype(F32), axis)]
    return [value] + [swap(value, axis, mask) for mask in range(1, count)]


def join_kernel(base, places, *refs):
    out = refs[-1]
    width = refs[0].shape[1]
    for i, piece in enumerate(refs[:-1]):
        out[:, pl.ds(pl.multiple_of(places[base + i], 128), width)] = piece[...]


def join(places, base, pieces):
    share, width = pieces[0].shape
    return pl.pallas_call(
        functools.partial(join_kernel, base),
        in_specs=[SMEM] + [VMEM] * len(pieces),
        out_shape=jax.ShapeDtypeStruct((share, width * len(pieces)), F32),
        compiler_params=pltpu.CompilerParams(vmem_limit_bytes=16 * 2**20),
        name="join",
    )(places, *pieces)


def on_device(record, fir_taps, gauge_lag, projector, compress):
    rows, cols = record.shape
    rank = projector.shape[1]
    count = lax.axis_size("tm")
    position = lax.axis_index("tm")
    depths = count.bit_length() - 1
    share = rank // count
    halo = lax.ppermute(
        record[rows - HALO :], "tm", [(source, source + 1) for source in range(count - 1)]
    )
    sketch = front(record, halo, gauge_lag, fir_taps[None, :], projector)

    widths = [cols]
    for depth in range(1, depths):
        widths.append(cols // 2 if cols % 256 == 0 else cols)
    narrowed = [depth for depth in range(depths - 1) if widths[depth + 1] < widths[depth]]
    assert narrowed == list(range(len(narrowed)))
    span = 2 ** len(narrowed)

    def bit_of(where, bit):
        return where // 2**bit % 2

    places = []
    for depth in range(depths):
        half = widths[depth] // 2 if depth in narrowed else 0
        flip = bit_of(position, depth)
        places += [flip * half, flip]
    places += [position ^ part for part in range(span)]
    joined = len(places)
    for part in range(span):
        places.append(sum([bit_of(position ^ part, bit) * (cols >> (bit + 1)) for bit in narrowed], 0))
    places = jnp.stack([position * 0 + place for place in places]).astype(jnp.int32)
    kept = ahead = None
    for depth in range(depths):
        first, last = depth == 0, depth == depths - 1
        mask = 2**depth
        here = widths[depth]
        if not last:
            other = swap(sketch, "tm", mask)
        if first:
            grams = gather_parts(pair_gram(sketch, other), "chan")
        else:
            packed, *kept = kept
            grams = [*kept, *ahead, swap(packed, "tm", mask)]
        if last:
            if not first:
                sketch = hold(sketch, *grams[-2:])
            other = swap(sketch, "tm", mask)
            mixing = last_filter_call(grams, compress, places, 2 * depth, first, share, span)
            pieces = mix(mixing, sketch, other, span, F32)
            break
        after = [] if first else [packed]
        part = ahead_gram(sketch, other, swap(sketch, "tm", 2 * mask), here, *after)
        if widths[depth + 1] == here and depth + 2 == depths:
            mixing, packed, level = level_filter_call(grams, compress, places, 2 * depth, first)
            (merged,) = mix(mixing, sketch, other, 1, BF16)
        else:
            mixing, merged, full = filter_call(
                grams, compress, places, 2 * depth, sketch, other, here, widths[depth + 1], first
            )
            packed, level = level_call(mixing, full)
        kept = packed, mixing, level
        for bit in [b for b in narrowed if b < depth]:
            part = (part.astype(F32) + swap(part, "tm", 2**bit).astype(F32)).astype(BF16)
        parts = gather_parts(part, "chan")
        total = sum(piece.astype(F32) for piece in parts).astype(BF16)
        ahead = [total, swap(total, "tm", mask)]
        sketch = merged
    if span == 1:
        return pieces[0]
    pieces = [pieces[0]] + [swap(piece, "tm", part) for part, piece in enumerate(pieces[1:], 1)]
    return join(places, joined, pieces)


def solution(mesh):
    return jax.shard_map(
        on_device,
        mesh=mesh,
        in_specs=(P("tm", "chan"), P(), P("chan"), P("tm", None), P()),
        out_specs=P("tm", "chan"),
        check_vma=False,
    )
```

```python
import functools

import jax
import jax.numpy as jnp
from jax import lax
from jax.experimental import pallas as pl
from jax.experimental.pallas import tpu as pltpu
from jax.sharding import PartitionSpec as P

TAPS = 64
GAUGE_MAX = 16
K_ITERS = 8
HALO = TAPS + GAUGE_MAX
BLOCK = 128
STEP = 16
CHUNK = 256
EXTRA = 16
F32 = jnp.float32
BF16 = jnp.bfloat16
ANY = pl.BlockSpec(memory_space=pl.ANY)
HBM = pl.BlockSpec(memory_space=pltpu.HBM)
SMEM = pl.BlockSpec(memory_space=pltpu.SMEM)
VMEM = pl.BlockSpec(memory_space=pltpu.VMEM)
PARAMS = pltpu.CompilerParams(vmem_limit_bytes=40 * 2**20)


def dot(a, b):
    return jnp.dot(a, b, preferred_element_type=F32)


def dot_nt(a, b):
    return lax.dot_general(a, b, (((1,), (1,)), ((), ())), preferred_element_type=F32)


def split(a):
    high = a.astype(BF16)
    return high, (a - high.astype(F32)).astype(BF16)


def dot3_split(ah, al, bh, bl):
    rows = ah.shape[0]
    wide = dot(jnp.concatenate([ah, al], 0), bh)
    return wide[:rows] + (wide[rows:] + dot(ah, bl))


def dot3(a, b):
    return dot3_split(*split(a), *split(b))


def dot3_nt(a, b):
    ah, al = split(a)
    bh, bl = split(b)
    return dot_nt(ah, bh) + (dot_nt(ah, bl) + dot_nt(al, bh))


def eye_mask(n):
    row = lax.broadcasted_iota(jnp.int32, (n, n), 0)
    col = lax.broadcasted_iota(jnp.int32, (n, n), 1)
    return row == col


def one_hot(shape, place):
    row = lax.broadcasted_iota(jnp.int32, shape, 0)
    col = lax.broadcasted_iota(jnp.int32, shape, 1)
    return jnp.where(place(row) == col, 1.0, 0.0).astype(BF16)


def front_kernel(first, last, *refs):
    if first == 0:
        record, halo, lag, band, weights, begun, out, strain = refs
    else:
        record, lag_ref, taps_ref, projector_ref, out, band, head_weights, head = refs[:8]
        strain, weights, lag, taps, projector, sems = refs[8:]
        halo = begun = None

        @pl.when(pl.program_id(0) == 0)
        def _():
            sources, targets = (lag_ref, taps_ref, projector_ref), (lag, taps, projector)
            copies = [
                pltpu.make_async_copy(source, target, sems.at[i])
                for i, (source, target) in enumerate(zip(sources, targets))
            ]
            for copy in copies:
                copy.start()
            for copy in copies:
                copy.wait()
            turn = one_hot((TAPS, 256), lambda tap: TAPS - tap)
            line = dot(jnp.broadcast_to(taps[...], (8, TAPS)), turn)[0:1]
            line = jnp.broadcast_to(line, (BLOCK + GAUGE_MAX, 256))
            rolled = pltpu.roll(line, 0, 1, stride=1, stride_axis=0)[:, : BLOCK + HALO]
            order = one_hot((2 * BLOCK, BLOCK + GAUGE_MAX), lambda row: row // 8 + STEP * (row % 8))
            band[...] = dot(order, rolled.astype(BF16)).astype(BF16)
            order = one_hot((BLOCK, BLOCK), lambda row: row // 8 + STEP * (row % 8))
            for block in range(projector.shape[0] // BLOCK):
                part = slice(block * BLOCK, (block + 1) * BLOCK)
                weights[:, part] = dot(order, projector[part, :]).T.astype(BF16)
            head_weights[...] = weights[:, 0:BLOCK]

    cols = record.shape[1]
    lane = min(128, cols)
    lanes = cols // lane
    group = 256 if cols % 256 == 0 else lane
    total = None
    used = first * BLOCK
    if first > 0:
        head[...] = record[0:BLOCK, :]
    for block in range(first, last):
        start = block * BLOCK
        for g in range(0, cols, group):
            if block == 0:
                segment = jnp.concatenate([halo[:, g : g + group], record[0:BLOCK, g : g + group]], 0)
            else:
                segment = record[start - HALO : start + BLOCK, g : g + group]
            result = dot(band[...], segment)
            for c in range(0, group, lane):
                line = pl.program_id(0) * lanes + (g + c) // lane
                shift = GAUGE_MAX - lag[pl.ds(line, 1), :]
                wide = result[:, c : c + lane]
                picked = wide
                for step in (8, 4, 2, 1):
                    length = BLOCK + 8 * (step - 1)
                    picked = jnp.where(
                        (shift & step) != 0, picked[8 * step : 8 * step + length], picked[:length]
                    )
                strain[start : start + BLOCK, g + c : g + c + lane] = (wide[BLOCK:] - picked).astype(
                    BF16
                )
        done = start + BLOCK
        if done % CHUNK == 0 or block == last - 1:
            part = dot(weights[:, used:done], strain[used:done, :])
            total = part if total is None else total + part
            used = done
    if begun is None:
        out[...] = total
    else:
        out[...] = (total + begun[...]).astype(BF16)


def front_call(blocks, args, in_specs, out_specs, out_shape, scratch, steps, grant):
    return pl.pallas_call(
        functools.partial(front_kernel, *blocks),
        grid=(steps,),
        in_specs=in_specs,
        out_specs=out_specs,
        out_shape=out_shape,
        scratch_shapes=scratch,
        compiler_params=pltpu.CompilerParams(vmem_limit_bytes=grant * 2**20),
        name="front",
    )(*args)


def front(record, halo, lag, taps, projector):
    rows, cols = record.shape
    rank = projector.shape[1]
    lag = lag.reshape(cols // 128, 128) if cols % 128 == 0 else lag[None, :]
    whole = lambda a: pl.BlockSpec(a.shape, lambda i: (0, 0))
    columns = lambda count, tile: pl.BlockSpec((count, tile), lambda i: (0, i))
    tile = next((t for t in (512, 640, 256, 128) if cols % t == 0), cols)
    shapes = [
        jax.ShapeDtypeStruct((rank, cols), F32),
        jax.ShapeDtypeStruct((2 * BLOCK, BLOCK + HALO), BF16),
        jax.ShapeDtypeStruct((rank, BLOCK), BF16),
        jax.ShapeDtypeStruct((BLOCK, cols), BF16),
    ]
    begun, band, weights, head = front_call(
        (1, rows // BLOCK),
        (record, lag, taps, projector),
        [columns(rows, tile), HBM, HBM, HBM],
        [columns(rank, tile), whole(shapes[1]), whole(shapes[2]), columns(BLOCK, tile)],
        shapes,
        [
            pltpu.VMEM((rows, tile), BF16),
            pltpu.VMEM((rank, rows), BF16),
            pltpu.VMEM(lag.shape, lag.dtype),
            pltpu.VMEM(taps.shape, BF16),
            pltpu.VMEM(projector.shape, BF16),
            pltpu.SemaphoreType.DMA((3,)),
        ],
        cols // tile,
        48,
    )
    tile = cols // 2 if cols % 256 == 0 else cols
    return front_call(
        (0, 1),
        (head, halo, lag, band, weights, begun),
        [
            columns(BLOCK, tile),
            columns(HALO, tile),
            whole(lag),
            whole(band),
            whole(weights),
            columns(rank, tile),
        ],
        columns(rank, tile),
        jax.ShapeDtypeStruct((rank, cols), BF16),
        [pltpu.VMEM((BLOCK, tile), BF16)],
        cols // tile,
        32,
    )


def pair_kernel(own, other, out):
    rank = own.shape[0]
    a, b = own[...], other[...]
    aa, ab, bb = dot_nt(a, a), dot_nt(a, b), dot_nt(b, b)
    diag = eye_mask(rank)
    trace = jnp.sum(jnp.where(diag, aa + bb, 0.0), axis=(0, 1), keepdims=True)
    mean = trace / (2 * rank)
    aa = aa - jnp.where(diag, mean, 0.0)
    bb = bb - jnp.where(diag, mean, 0.0)
    row = lax.broadcasted_iota(jnp.int32, (rank, rank), 0)
    col = lax.broadcasted_iota(jnp.int32, (rank, rank), 1)
    out[0:rank, :] = jnp.where(row <= col, aa, bb).astype(BF16)
    out[rank : 2 * rank, :] = ab.astype(BF16)
    bottom = jnp.sum(jnp.where(diag, bb, 0.0), axis=0, keepdims=True)
    full = jnp.broadcast_to(mean, (EXTRA, rank))
    high = full.astype(BF16).astype(F32)
    mid = (full - high).astype(BF16).astype(F32)
    low = full - high - mid
    line = lax.broadcasted_iota(jnp.int32, (EXTRA, rank), 0)
    extra = jnp.where(line == 0, high, jnp.where(line == 1, mid, jnp.where(line == 2, low, 0.0)))
    out[2 * rank :, :] = jnp.where(line == 3, jnp.broadcast_to(bottom, (EXTRA, rank)), extra).astype(
        BF16
    )


def pair_gram(own, other):
    rank = own.shape[0]
    return pl.pallas_call(
        pair_kernel,
        out_shape=jax.ShapeDtypeStruct((2 * rank + EXTRA, rank), BF16),
        compiler_params=PARAMS,
        name="pair_gram",
    )(own, other)


def ahead_kernel(width, own, sibling, partner, *refs):
    out = refs[-1]
    rank = own.shape[0]
    there = partner[:, :width]
    out[0:rank, :] = dot_nt(own[:, :width], there).astype(out.dtype)
    out[rank:, :] = dot_nt(sibling[:, :width], there).astype(out.dtype)


def ahead_gram(own, sibling, partner, width, *after):
    rank = own.shape[0]
    return pl.pallas_call(
        functools.partial(ahead_kernel, width),
        in_specs=[VMEM] * 3 + [ANY] * len(after),
        out_shape=jax.ShapeDtypeStruct((2 * rank, rank), BF16),
        compiler_params=PARAMS,
        name="ahead_gram",
    )(own, sibling, partner, *after)


def summed(parts):
    total = parts[0][...].astype(F32)
    for part in parts[1:]:
        total = total + part[...].astype(F32)
    return total


def hold_kernel(*refs):
    pass


def hold(value, *until):
    return pl.pallas_call(
        hold_kernel,
        in_specs=[ANY] * (1 + len(until)),
        out_specs=ANY,
        out_shape=jax.ShapeDtypeStruct(value.shape, value.dtype),
        input_output_aliases={0: 0},
        compiler_params=pltpu.CompilerParams(vmem_limit_bytes=16 * 2**20),
        name="hold",
    )(value, *until)


def add_kernel(one, two, _, out):
    out[...] = (one[...].astype(F32) + two[...].astype(F32)).astype(BF16)


def add_after(one, two, after):
    return pl.pallas_call(
        add_kernel,
        in_specs=[VMEM, VMEM, ANY],
        out_shape=jax.ShapeDtypeStruct(one.shape, BF16),
        compiler_params=pltpu.CompilerParams(vmem_limit_bytes=16 * 2**20),
        name="add_after",
    )(one, two, after)


def square_of(aa, ab, bb):
    return jnp.concatenate(
        [jnp.concatenate([aa, ab], 1), jnp.concatenate([ab.T, bb], 1)], 0
    )


def first_gram(parts):
    total = summed(parts)
    rank = total.shape[1]
    both = total[0:rank]
    ab = total[rank : 2 * rank]
    extra = total[2 * rank :]
    mean = extra[0:1, 0:1] + extra[1:2, 0:1] + extra[2:3, 0:1]
    row = lax.broadcasted_iota(jnp.int32, (rank, rank), 0)
    col = lax.broadcasted_iota(jnp.int32, (rank, rank), 1)
    turned = both.T
    aa = jnp.where(row <= col, both, turned)
    bb = jnp.where(row > col, both, jnp.where(row < col, turned, extra[3:4, :]))
    return square_of(aa, ab, bb), mean


def later_gram(own_mix, own_level, ahead, sibling_ahead, other):
    rank = own_mix.shape[0]
    mine, theirs = ahead[...], sibling_ahead[...]
    cross = jnp.concatenate(
        [
            jnp.concatenate([mine[:rank], theirs[rank:]], 1),
            jnp.concatenate([mine[rank:], theirs[:rank]], 1),
        ],
        0,
    )
    high, low = split(own_mix[...])
    half = dot(high, cross) + dot(low, cross)
    high, low = split(half)
    place = other.shape[1] - 4 * rank
    other_mix = other[:, place : place + 2 * rank]
    ab = dot_nt(high, other_mix) + dot_nt(low, other_mix)
    place += 2 * rank
    other_level = other[:, place : place + rank].astype(F32) + other[:, place + rank :].astype(F32)
    gram = square_of(own_level[...], ab, other_level)
    diag = eye_mask(gram.shape[0])
    mean = jnp.sum(jnp.where(diag, gram, 0.0), axis=(0, 1), keepdims=True) / gram.shape[0]
    return gram - jnp.where(diag, mean, 0.0), mean


def filter_kernel(count, first, kind, used, base, *refs):
    grams, refs = refs[:count], refs[count:]
    compress, places, refs = refs[0], refs[1], refs[2:]
    last = kind == "last"
    rank = compress.shape[1]
    if last:
        mix_out, turned = refs
        share = mix_out.shape[0] // used
    elif kind == "level":
        mix_out, packed, level, turned = refs
    else:
        own, other, mix_out, sketch, whole, pair, turned, sems = refs
        width = pair.shape[1]
        if width < used:
            span = pl.ds(pl.multiple_of(places[base], 128), width)
        else:
            span = slice(0, width)
        copies = [
            pltpu.make_async_copy(
                source.at[:, span], pair.at[slice(i * rank, (i + 1) * rank)], sems.at[i]
            )
            for i, source in enumerate((own, other))
        ]
        for copy in copies:
            copy.start()
    flip = places[base + 1]
    for i in range(2):
        half = compress[pl.ds(pl.multiple_of((flip + i) % 2 * rank, 128), rank), :]
        turned[:, i * rank : (i + 1) * rank] = half.T
    if last:
        parts = [
            turned[pl.ds(pl.multiple_of(places[base + 2 + i] * share, 8), share), :]
            for i in range(used)
        ]
        compress_t = jnp.concatenate(parts, 0) if used > 1 else parts[0]
    else:
        compress_t = turned[...]
    gram, mean = first_gram(grams) if first else later_gram(*grams)
    size = gram.shape[0]
    eye = jnp.where(eye_mask(size), 1.0, 0.0)
    z = gram * lax.rsqrt(jnp.sum(gram * gram, axis=(0, 1), keepdims=True) + 1e-6)
    for step in range(K_ITERS):
        zh, zl = split(z)
        square = dot3_split(zh, zl, zh, zl)
        factor = split(1.5 * eye - 0.5 * square)
        if step < K_ITERS - 1:
            z = dot3_split(zh, zl, *factor)
        else:
            turn = dot3_split(*split(compress_t), zh, zl)
            mixing = 0.5 * (compress_t + dot3_split(*split(turn), *factor))
    mix_out[...] = mixing
    if last:
        return
    full = gram + mean * eye
    if kind == "level":
        pack_level(mixing, full, packed, level)
        return
    whole[...] = full
    for copy in copies:
        copy.wait()
    both = jnp.concatenate(split(mixing), 0)
    tile = next((t for t in (640, 512, 256, 128) if width % t == 0), width)
    for c in range(0, width, tile):
        part = dot(both, pair[:, c : c + tile])
        sketch[:, c : c + tile] = (part[:rank] + part[rank:]).astype(BF16)


def pack_level(mixing, full, packed, level):
    rank = mixing.shape[0]
    block = dot3_nt(dot3(mixing, full), mixing)
    level[...] = block
    packed[:, : 2 * rank] = mixing.astype(BF16)
    high, low = split(block)
    packed[:, 2 * rank : 3 * rank] = high
    packed[:, 3 * rank :] = low


def level_kernel(mixing, full, packed, level):
    pack_level(mixing[...], full[...], packed, level)


def level_shapes(rank):
    return [
        jax.ShapeDtypeStruct((rank, 4 * rank), BF16),
        jax.ShapeDtypeStruct((rank, rank), F32),
    ]


def level_call(mixing, full):
    return pl.pallas_call(
        level_kernel,
        out_shape=level_shapes(mixing.shape[0]),
        compiler_params=pltpu.CompilerParams(vmem_limit_bytes=16 * 2**20),
        name="level",
    )(mixing, full)


def level_filter_call(grams, compress, places, base, first):
    rank = compress.shape[1]
    args = [*grams, compress]
    return pl.pallas_call(
        functools.partial(filter_kernel, len(grams), first, "level", 0, base),
        in_specs=[VMEM] * len(args) + [SMEM],
        out_shape=[jax.ShapeDtypeStruct((rank, 2 * rank), F32), *level_shapes(rank)],
        scratch_shapes=[pltpu.VMEM((rank, 2 * rank), F32)],
        compiler_params=PARAMS,
        name="sign_filter",
    )(*args, places)


def filter_call(grams, compress, places, base, own, other, used, width, first):
    rank = own.shape[0]
    args = [*grams, compress]
    return pl.pallas_call(
        functools.partial(filter_kernel, len(grams), first, "sketch", used, base),
        in_specs=[VMEM] * len(args) + [SMEM, ANY, ANY],
        out_shape=[
            jax.ShapeDtypeStruct((rank, 2 * rank), F32),
            jax.ShapeDtypeStruct((rank, width), BF16),
            jax.ShapeDtypeStruct((2 * rank, 2 * rank), F32),
        ],
        scratch_shapes=[
            pltpu.VMEM((2 * rank, width), BF16),
            pltpu.VMEM((rank, 2 * rank), F32),
            pltpu.SemaphoreType.DMA((2,)),
        ],
        compiler_params=PARAMS,
        name="sign_filter",
    )(*args, places, own, other)


def last_filter_call(grams, compress, places, base, first, share, pieces):
    rank = compress.shape[1]
    args = [*grams, compress]
    return pl.pallas_call(
        functools.partial(filter_kernel, len(grams), first, "last", pieces, base),
        in_specs=[VMEM] * len(args) + [SMEM],
        out_shape=jax.ShapeDtypeStruct((share * pieces, 2 * rank), F32),
        scratch_shapes=[pltpu.VMEM((rank, 2 * rank), F32)],
        compiler_params=PARAMS,
        cost_estimate=pl.CostEstimate(
            flops=50 * K_ITERS * (2 * rank) ** 3, bytes_accessed=0, transcendentals=0
        ),
        name="sign_filter",
    )(*args, places)


def mix_kernel(mixing, own, other, *out):
    rank = own.shape[0]
    rows, share = mixing.shape[0], out[0].shape[0]
    both = jnp.concatenate(split(mixing[...]), 0)
    width = own.shape[1]
    tile = next((t for t in (640, 512, 256, 128) if width % t == 0), width)
    for c in range(0, width, tile):
        span = slice(c, c + tile)
        part = dot(both, jnp.concatenate([own[:, span], other[:, span]], 0))
        part = part[:rows] + part[rows:]
        for i, piece in enumerate(out):
            piece[:, span] = part[i * share : (i + 1) * share].astype(piece.dtype)


def mix(mixing, own, other, pieces, dtype):
    shape = jax.ShapeDtypeStruct((mixing.shape[0] // pieces, own.shape[1]), dtype)
    return pl.pallas_call(
        mix_kernel,
        out_shape=[shape] * pieces,
        compiler_params=pltpu.CompilerParams(vmem_limit_bytes=16 * 2**20),
        name="mix",
    )(mixing, own, other)


def swap(value, axis, mask):
    count = lax.axis_size(axis)
    return lax.ppermute(value, axis, [(source, source ^ mask) for source in range(count)])


def gather_parts(value, axis):
    count = lax.axis_size(axis)
    if count > 4 or count & (count - 1):
        return [lax.psum(value.astype(F32), axis)]
    return [value] + [swap(value, axis, mask) for mask in range(1, count)]


def join_kernel(base, places, *refs):
    out = refs[-1]
    width = refs[0].shape[1]
    for i, piece in enumerate(refs[:-1]):
        out[:, pl.ds(pl.multiple_of(places[base + i], 128), width)] = piece[...]


def join(places, base, pieces):
    share, width = pieces[0].shape
    return pl.pallas_call(
        functools.partial(join_kernel, base),
        in_specs=[SMEM] + [VMEM] * len(pieces),
        out_shape=jax.ShapeDtypeStruct((share, width * len(pieces)), F32),
        compiler_params=pltpu.CompilerParams(vmem_limit_bytes=16 * 2**20),
        name="join",
    )(places, *pieces)


def on_device(record, fir_taps, gauge_lag, projector, compress):
    rows, cols = record.shape
    rank = projector.shape[1]
    count = lax.axis_size("tm")
    position = lax.axis_index("tm")
    depths = count.bit_length() - 1
    share = rank // count
    halo = lax.ppermute(
        record[rows - HALO :], "tm", [(source, source + 1) for source in range(count - 1)]
    )
    sketch = front(record, halo, gauge_lag, fir_taps[None, :], projector)

    widths = [cols]
    for depth in range(1, depths):
        widths.append(cols // 2 if cols % 256 == 0 else cols)
    narrowed = [depth for depth in range(depths - 1) if widths[depth + 1] < widths[depth]]
    assert narrowed == list(range(len(narrowed)))
    span = 2 ** len(narrowed)

    def bit_of(where, bit):
        return where // 2**bit % 2

    places = []
    for depth in range(depths):
        half = widths[depth] // 2 if depth in narrowed else 0
        flip = bit_of(position, depth)
        places += [flip * half, flip]
    places += [position ^ part for part in range(span)]
    joined = len(places)
    for part in range(span):
        places.append(sum([bit_of(position ^ part, bit) * (cols >> (bit + 1)) for bit in narrowed], 0))
    places = jnp.stack([position * 0 + place for place in places]).astype(jnp.int32)
    kept = ahead = None
    for depth in range(depths):
        first, last = depth == 0, depth == depths - 1
        mask = 2**depth
        here = widths[depth]
        if not last:
            other = swap(sketch, "tm", mask)
        if first:
            grams = gather_parts(pair_gram(sketch, other), "chan")
        else:
            packed, *kept = kept
            grams = [*kept, *ahead, swap(packed, "tm", mask)]
        if last:
            if not first:
                sketch = hold(sketch, *grams[-2:])
            other = swap(sketch, "tm", mask)
            mixing = last_filter_call(grams, compress, places, 2 * depth, first, share, span)
            pieces = mix(mixing, sketch, other, span, F32)
            break
        after = [] if first else [packed]
        part = ahead_gram(sketch, other, swap(sketch, "tm", 2 * mask), here, *after)
        if widths[depth + 1] == here and depth + 2 == depths:
            mixing, packed, level = level_filter_call(grams, compress, places, 2 * depth, first)
            (merged,) = mix(mixing, sketch, other, 1, BF16)
        else:
            mixing, merged, full = filter_call(
                grams, compress, places, 2 * depth, sketch, other, here, widths[depth + 1], first
            )
            packed, level = level_call(mixing, full)
        kept = packed, mixing, level
        for bit in [b for b in narrowed if b < depth]:
            part = add_after(part, swap(part, "tm", 2**bit), grams[-1])
        parts = gather_parts(part, "chan")
        total = sum(piece.astype(F32) for piece in parts).astype(BF16)
        ahead = [total, swap(total, "tm", mask)]
        sketch = merged
    if span == 1:
        return pieces[0]
    pieces = [pieces[0]] + [swap(piece, "tm", part) for part, piece in enumerate(pieces[1:], 1)]
    return join(places, joined, pieces)


def solution(mesh):
    return jax.shard_map(
        on_device,
        mesh=mesh,
        in_specs=(P("tm", "chan"), P(), P("chan"), P("tm", None), P()),
        out_specs=P("tm", "chan"),
        check_vma=False,
    )
```

```python
import functools

import jax
import jax.numpy as jnp
from jax import lax
from jax.experimental import pallas as pl
from jax.experimental.pallas import tpu as pltpu
from jax.sharding import PartitionSpec as P

TAPS = 64
GAUGE_MAX = 16
K_ITERS = 8
HALO = TAPS + GAUGE_MAX
BLOCK = 128
STEP = 16
CHUNK = 512
EXTRA = 16
F32 = jnp.float32
BF16 = jnp.bfloat16
ANY = pl.BlockSpec(memory_space=pl.ANY)
HBM = pl.BlockSpec(memory_space=pltpu.HBM)
SMEM = pl.BlockSpec(memory_space=pltpu.SMEM)
VMEM = pl.BlockSpec(memory_space=pltpu.VMEM)
PARAMS = pltpu.CompilerParams(vmem_limit_bytes=40 * 2**20)


def dot(a, b):
    return jnp.dot(a, b, preferred_element_type=F32)


def dot_nt(a, b):
    return lax.dot_general(a, b, (((1,), (1,)), ((), ())), preferred_element_type=F32)


def split(a):
    high = a.astype(BF16)
    return high, (a - high.astype(F32)).astype(BF16)


def dot3_split(ah, al, bh, bl):
    rows = ah.shape[0]
    wide = dot(jnp.concatenate([ah, al], 0), bh)
    return wide[:rows] + (wide[rows:] + dot(ah, bl))


def dot3(a, b):
    return dot3_split(*split(a), *split(b))


def dot3_nt(a, b):
    ah, al = split(a)
    bh, bl = split(b)
    return dot_nt(ah, bh) + (dot_nt(ah, bl) + dot_nt(al, bh))


def eye_mask(n):
    row = lax.broadcasted_iota(jnp.int32, (n, n), 0)
    col = lax.broadcasted_iota(jnp.int32, (n, n), 1)
    return row == col


def one_hot(shape, place):
    row = lax.broadcasted_iota(jnp.int32, shape, 0)
    col = lax.broadcasted_iota(jnp.int32, shape, 1)
    return jnp.where(place(row) == col, 1.0, 0.0).astype(BF16)


def front_kernel(first, last, *refs):
    if first == 0:
        record, halo, lag, band, weights, begun, out, strain = refs
    else:
        record, lag_ref, taps_ref, projector_ref, out, band, head_weights, head = refs[:8]
        strain, weights, lag, taps, projector, sems = refs[8:]
        halo = begun = None

        @pl.when(pl.program_id(0) == 0)
        def _():
            sources, targets = (lag_ref, taps_ref, projector_ref), (lag, taps, projector)
            copies = [
                pltpu.make_async_copy(source, target, sems.at[i])
                for i, (source, target) in enumerate(zip(sources, targets))
            ]
            for copy in copies:
                copy.start()
            for copy in copies:
                copy.wait()
            turn = one_hot((TAPS, 256), lambda tap: TAPS - tap)
            line = dot(jnp.broadcast_to(taps[...], (8, TAPS)), turn)[0:1]
            line = jnp.broadcast_to(line, (BLOCK + GAUGE_MAX, 256))
            rolled = pltpu.roll(line, 0, 1, stride=1, stride_axis=0)[:, : BLOCK + HALO]
            order = one_hot((2 * BLOCK, BLOCK + GAUGE_MAX), lambda row: row // 8 + STEP * (row % 8))
            band[...] = dot(order, rolled.astype(BF16)).astype(BF16)
            order = one_hot((BLOCK, BLOCK), lambda row: row // 8 + STEP * (row % 8))
            for block in range(projector.shape[0] // BLOCK):
                part = slice(block * BLOCK, (block + 1) * BLOCK)
                weights[:, part] = dot(order, projector[part, :]).T.astype(BF16)
            head_weights[...] = weights[:, 0:BLOCK]

    cols = record.shape[1]
    lane = min(128, cols)
    lanes = cols // lane
    group = 256 if cols % 256 == 0 else lane
    total = None
    used = first * BLOCK
    if first > 0:
        head[...] = record[0:BLOCK, :]
    for block in range(first, last):
        start = block * BLOCK
        for g in range(0, cols, group):
            if block == 0:
                segment = jnp.concatenate([halo[:, g : g + group], record[0:BLOCK, g : g + group]], 0)
            else:
                segment = record[start - HALO : start + BLOCK, g : g + group]
            result = dot(band[...], segment)
            for c in range(0, group, lane):
                line = pl.program_id(0) * lanes + (g + c) // lane
                shift = GAUGE_MAX - lag[pl.ds(line, 1), :]
                wide = result[:, c : c + lane]
                picked = wide
                for step in (8, 4, 2, 1):
                    length = BLOCK + 8 * (step - 1)
                    picked = jnp.where(
                        (shift & step) != 0, picked[8 * step : 8 * step + length], picked[:length]
                    )
                strain[start : start + BLOCK, g + c : g + c + lane] = (wide[BLOCK:] - picked).astype(
                    BF16
                )
        done = start + BLOCK
        if done % CHUNK == 0 or block == last - 1:
            part = dot(weights[:, used:done], strain[used:done, :])
            total = part if total is None else total + part
            used = done
    if begun is None:
        out[...] = total
    else:
        out[...] = (total + begun[...]).astype(BF16)


def front_call(blocks, args, in_specs, out_specs, out_shape, scratch, steps, grant):
    return pl.pallas_call(
        functools.partial(front_kernel, *blocks),
        grid=(steps,),
        in_specs=in_specs,
        out_specs=out_specs,
        out_shape=out_shape,
        scratch_shapes=scratch,
        compiler_params=pltpu.CompilerParams(vmem_limit_bytes=grant * 2**20),
        name="front",
    )(*args)


def front(record, halo, lag, taps, projector):
    rows, cols = record.shape
    rank = projector.shape[1]
    lag = lag.reshape(cols // 128, 128) if cols % 128 == 0 else lag[None, :]
    whole = lambda a: pl.BlockSpec(a.shape, lambda i: (0, 0))
    columns = lambda count, tile: pl.BlockSpec((count, tile), lambda i: (0, i))
    tile = next((t for t in (512, 640, 256, 128) if cols % t == 0), cols)
    shapes = [
        jax.ShapeDtypeStruct((rank, cols), F32),
        jax.ShapeDtypeStruct((2 * BLOCK, BLOCK + HALO), BF16),
        jax.ShapeDtypeStruct((rank, BLOCK), BF16),
        jax.ShapeDtypeStruct((BLOCK, cols), BF16),
    ]
    begun, band, weights, head = front_call(
        (1, rows // BLOCK),
        (record, lag, taps, projector),
        [columns(rows, tile), HBM, HBM, HBM],
        [columns(rank, tile), whole(shapes[1]), whole(shapes[2]), columns(BLOCK, tile)],
        shapes,
        [
            pltpu.VMEM((rows, tile), BF16),
            pltpu.VMEM((rank, rows), BF16),
            pltpu.VMEM(lag.shape, lag.dtype),
            pltpu.VMEM(taps.shape, BF16),
            pltpu.VMEM(projector.shape, BF16),
            pltpu.SemaphoreType.DMA((3,)),
        ],
        cols // tile,
        48,
    )
    tile = cols // 2 if cols % 256 == 0 else cols
    return front_call(
        (0, 1),
        (head, halo, lag, band, weights, begun),
        [
            columns(BLOCK, tile),
            columns(HALO, tile),
            whole(lag),
            whole(band),
            whole(weights),
            columns(rank, tile),
        ],
        columns(rank, tile),
        jax.ShapeDtypeStruct((rank, cols), BF16),
        [pltpu.VMEM((BLOCK, tile), BF16)],
        cols // tile,
        32,
    )


def pair_kernel(own, other, out):
    rank = own.shape[0]
    a, b = own[...], other[...]
    aa, ab, bb = dot_nt(a, a), dot_nt(a, b), dot_nt(b, b)
    diag = eye_mask(rank)
    trace = jnp.sum(jnp.where(diag, aa + bb, 0.0), axis=(0, 1), keepdims=True)
    mean = trace / (2 * rank)
    aa = aa - jnp.where(diag, mean, 0.0)
    bb = bb - jnp.where(diag, mean, 0.0)
    row = lax.broadcasted_iota(jnp.int32, (rank, rank), 0)
    col = lax.broadcasted_iota(jnp.int32, (rank, rank), 1)
    out[0:rank, :] = jnp.where(row <= col, aa, bb).astype(BF16)
    out[rank : 2 * rank, :] = ab.astype(BF16)
    bottom = jnp.sum(jnp.where(diag, bb, 0.0), axis=0, keepdims=True)
    full = jnp.broadcast_to(mean, (EXTRA, rank))
    high = full.astype(BF16).astype(F32)
    mid = (full - high).astype(BF16).astype(F32)
    low = full - high - mid
    line = lax.broadcasted_iota(jnp.int32, (EXTRA, rank), 0)
    extra = jnp.where(line == 0, high, jnp.where(line == 1, mid, jnp.where(line == 2, low, 0.0)))
    out[2 * rank :, :] = jnp.where(line == 3, jnp.broadcast_to(bottom, (EXTRA, rank)), extra).astype(
        BF16
    )


def pair_gram(own, other):
    rank = own.shape[0]
    return pl.pallas_call(
        pair_kernel,
        out_shape=jax.ShapeDtypeStruct((2 * rank + EXTRA, rank), BF16),
        compiler_params=PARAMS,
        name="pair_gram",
    )(own, other)


def ahead_kernel(width, own, sibling, partner, *refs):
    out = refs[-1]
    rank = own.shape[0]
    there = partner[:, :width]
    out[0:rank, :] = dot_nt(own[:, :width], there).astype(out.dtype)
    out[rank:, :] = dot_nt(sibling[:, :width], there).astype(out.dtype)


def ahead_gram(own, sibling, partner, width, *after):
    rank = own.shape[0]
    return pl.pallas_call(
        functools.partial(ahead_kernel, width),
        in_specs=[VMEM] * 3 + [ANY] * len(after),
        out_shape=jax.ShapeDtypeStruct((2 * rank, rank), BF16),
        compiler_params=PARAMS,
        name="ahead_gram",
    )(own, sibling, partner, *after)


def summed(parts):
    total = parts[0][...].astype(F32)
    for part in parts[1:]:
        total = total + part[...].astype(F32)
    return total


def hold_kernel(*refs):
    pass


def hold(value, *until):
    return pl.pallas_call(
        hold_kernel,
        in_specs=[ANY] * (1 + len(until)),
        out_specs=ANY,
        out_shape=jax.ShapeDtypeStruct(value.shape, value.dtype),
        input_output_aliases={0: 0},
        compiler_params=pltpu.CompilerParams(vmem_limit_bytes=16 * 2**20),
        name="hold",
    )(value, *until)


def add_kernel(one, two, _, out):
    out[...] = (one[...].astype(F32) + two[...].astype(F32)).astype(BF16)


def add_after(one, two, after):
    return pl.pallas_call(
        add_kernel,
        in_specs=[VMEM, VMEM, ANY],
        out_shape=jax.ShapeDtypeStruct(one.shape, BF16),
        compiler_params=pltpu.CompilerParams(vmem_limit_bytes=16 * 2**20),
        name="add_after",
    )(one, two, after)


def square_of(aa, ab, bb):
    return jnp.concatenate(
        [jnp.concatenate([aa, ab], 1), jnp.concatenate([ab.T, bb], 1)], 0
    )


def first_gram(parts):
    total = summed(parts)
    rank = total.shape[1]
    both = total[0:rank]
    ab = total[rank : 2 * rank]
    extra = total[2 * rank :]
    mean = extra[0:1, 0:1] + extra[1:2, 0:1] + extra[2:3, 0:1]
    row = lax.broadcasted_iota(jnp.int32, (rank, rank), 0)
    col = lax.broadcasted_iota(jnp.int32, (rank, rank), 1)
    turned = both.T
    aa = jnp.where(row <= col, both, turned)
    bb = jnp.where(row > col, both, jnp.where(row < col, turned, extra[3:4, :]))
    return square_of(aa, ab, bb), mean


def later_gram(own_mix, own_level, ahead, sibling_ahead, other):
    rank = own_mix.shape[0]
    mine, theirs = ahead[...], sibling_ahead[...]
    cross = jnp.concatenate(
        [
            jnp.concatenate([mine[:rank], theirs[rank:]], 1),
            jnp.concatenate([mine[rank:], theirs[:rank]], 1),
        ],
        0,
    )
    high, low = split(own_mix[...])
    half = dot(high, cross) + dot(low, cross)
    high, low = split(half)
    place = other.shape[1] - 4 * rank
    other_mix = other[:, place : place + 2 * rank]
    ab = dot_nt(high, other_mix) + dot_nt(low, other_mix)
    place += 2 * rank
    other_level = other[:, place : place + rank].astype(F32) + other[:, place + rank :].astype(F32)
    gram = square_of(own_level[...], ab, other_level)
    diag = eye_mask(gram.shape[0])
    mean = jnp.sum(jnp.where(diag, gram, 0.0), axis=(0, 1), keepdims=True) / gram.shape[0]
    return gram - jnp.where(diag, mean, 0.0), mean


def filter_kernel(count, first, kind, used, base, *refs):
    grams, refs = refs[:count], refs[count:]
    compress, places, refs = refs[0], refs[1], refs[2:]
    last = kind == "last"
    rank = compress.shape[1]
    if last:
        mix_out, turned = refs
        share = mix_out.shape[0] // used
    elif kind == "level":
        mix_out, packed, level, turned = refs
    else:
        own, other, mix_out, sketch, whole, pair, turned, sems = refs
        width = pair.shape[1]
        if width < used:
            span = pl.ds(pl.multiple_of(places[base], 128), width)
        else:
            span = slice(0, width)
        copies = [
            pltpu.make_async_copy(
                source.at[:, span], pair.at[slice(i * rank, (i + 1) * rank)], sems.at[i]
            )
            for i, source in enumerate((own, other))
        ]
        for copy in copies:
            copy.start()
    flip = places[base + 1]
    for i in range(2):
        half = compress[pl.ds(pl.multiple_of((flip + i) % 2 * rank, 128), rank), :]
        turned[:, i * rank : (i + 1) * rank] = half.T
    if last:
        parts = [
            turned[pl.ds(pl.multiple_of(places[base + 2 + i] * share, 8), share), :]
            for i in range(used)
        ]
        compress_t = jnp.concatenate(parts, 0) if used > 1 else parts[0]
    else:
        compress_t = turned[...]
    gram, mean = first_gram(grams) if first else later_gram(*grams)
    size = gram.shape[0]
    eye = jnp.where(eye_mask(size), 1.0, 0.0)
    z = gram * lax.rsqrt(jnp.sum(gram * gram, axis=(0, 1), keepdims=True) + 1e-6)
    for step in range(K_ITERS):
        zh, zl = split(z)
        square = dot3_split(zh, zl, zh, zl)
        factor = split(1.5 * eye - 0.5 * square)
        if step < K_ITERS - 1:
            z = dot3_split(zh, zl, *factor)
        else:
            turn = dot3_split(*split(compress_t), zh, zl)
            mixing = 0.5 * (compress_t + dot3_split(*split(turn), *factor))
    mix_out[...] = mixing
    if last:
        return
    full = gram + mean * eye
    if kind == "level":
        pack_level(mixing, full, packed, level)
        return
    whole[...] = full
    for copy in copies:
        copy.wait()
    both = jnp.concatenate(split(mixing), 0)
    tile = next((t for t in (640, 512, 256, 128) if width % t == 0), width)
    for c in range(0, width, tile):
        part = dot(both, pair[:, c : c + tile])
        sketch[:, c : c + tile] = (part[:rank] + part[rank:]).astype(BF16)


def pack_level(mixing, full, packed, level):
    rank = mixing.shape[0]
    block = dot3_nt(dot3(mixing, full), mixing)
    level[...] = block
    packed[:, : 2 * rank] = mixing.astype(BF16)
    high, low = split(block)
    packed[:, 2 * rank : 3 * rank] = high
    packed[:, 3 * rank :] = low


def level_kernel(mixing, full, packed, level):
    pack_level(mixing[...], full[...], packed, level)


def level_shapes(rank):
    return [
        jax.ShapeDtypeStruct((rank, 4 * rank), BF16),
        jax.ShapeDtypeStruct((rank, rank), F32),
    ]


def level_call(mixing, full):
    return pl.pallas_call(
        level_kernel,
        out_shape=level_shapes(mixing.shape[0]),
        compiler_params=pltpu.CompilerParams(vmem_limit_bytes=16 * 2**20),
        name="level",
    )(mixing, full)


def level_filter_call(grams, compress, places, base, first):
    rank = compress.shape[1]
    args = [*grams, compress]
    return pl.pallas_call(
        functools.partial(filter_kernel, len(grams), first, "level", 0, base),
        in_specs=[VMEM] * len(args) + [SMEM],
        out_shape=[jax.ShapeDtypeStruct((rank, 2 * rank), F32), *level_shapes(rank)],
        scratch_shapes=[pltpu.VMEM((rank, 2 * rank), F32)],
        compiler_params=PARAMS,
        name="sign_filter",
    )(*args, places)


def filter_call(grams, compress, places, base, own, other, used, width, first):
    rank = own.shape[0]
    args = [*grams, compress]
    return pl.pallas_call(
        functools.partial(filter_kernel, len(grams), first, "sketch", used, base),
        in_specs=[VMEM] * len(args) + [SMEM, ANY, ANY],
        out_shape=[
            jax.ShapeDtypeStruct((rank, 2 * rank), F32),
            jax.ShapeDtypeStruct((rank, width), BF16),
            jax.ShapeDtypeStruct((2 * rank, 2 * rank), F32),
        ],
        scratch_shapes=[
            pltpu.VMEM((2 * rank, width), BF16),
            pltpu.VMEM((rank, 2 * rank), F32),
            pltpu.SemaphoreType.DMA((2,)),
        ],
        compiler_params=PARAMS,
        name="sign_filter",
    )(*args, places, own, other)


def last_filter_call(grams, compress, places, base, first, share, pieces):
    rank = compress.shape[1]
    args = [*grams, compress]
    return pl.pallas_call(
        functools.partial(filter_kernel, len(grams), first, "last", pieces, base),
        in_specs=[VMEM] * len(args) + [SMEM],
        out_shape=jax.ShapeDtypeStruct((share * pieces, 2 * rank), F32),
        scratch_shapes=[pltpu.VMEM((rank, 2 * rank), F32)],
        compiler_params=PARAMS,
        cost_estimate=pl.CostEstimate(
            flops=50 * K_ITERS * (2 * rank) ** 3, bytes_accessed=0, transcendentals=0
        ),
        name="sign_filter",
    )(*args, places)


def mix_kernel(mixing, own, other, *out):
    rank = own.shape[0]
    rows, share = mixing.shape[0], out[0].shape[0]
    both = jnp.concatenate(split(mixing[...]), 0)
    width = own.shape[1]
    tile = next((t for t in (640, 512, 256, 128) if width % t == 0), width)
    for c in range(0, width, tile):
        span = slice(c, c + tile)
        part = dot(both, jnp.concatenate([own[:, span], other[:, span]], 0))
        part = part[:rows] + part[rows:]
        for i, piece in enumerate(out):
            piece[:, span] = part[i * share : (i + 1) * share].astype(piece.dtype)


def mix(mixing, own, other, pieces, dtype):
    shape = jax.ShapeDtypeStruct((mixing.shape[0] // pieces, own.shape[1]), dtype)
    return pl.pallas_call(
        mix_kernel,
        out_shape=[shape] * pieces,
        compiler_params=pltpu.CompilerParams(vmem_limit_bytes=16 * 2**20),
        name="mix",
    )(mixing, own, other)


def swap(value, axis, mask):
    count = lax.axis_size(axis)
    return lax.ppermute(value, axis, [(source, source ^ mask) for source in range(count)])


def gather_parts(value, axis):
    count = lax.axis_size(axis)
    if count > 4 or count & (count - 1):
        return [lax.psum(value.astype(F32), axis)]
    return [value] + [swap(value, axis, mask) for mask in range(1, count)]


def join_kernel(base, places, *refs):
    out = refs[-1]
    width = refs[0].shape[1]
    for i, piece in enumerate(refs[:-1]):
        out[:, pl.ds(pl.multiple_of(places[base + i], 128), width)] = piece[...]


def join(places, base, pieces):
    share, width = pieces[0].shape
    return pl.pallas_call(
        functools.partial(join_kernel, base),
        in_specs=[SMEM] + [VMEM] * len(pieces),
        out_shape=jax.ShapeDtypeStruct((share, width * len(pieces)), F32),
        compiler_params=pltpu.CompilerParams(vmem_limit_bytes=16 * 2**20),
        name="join",
    )(places, *pieces)


def on_device(record, fir_taps, gauge_lag, projector, compress):
    rows, cols = record.shape
    rank = projector.shape[1]
    count = lax.axis_size("tm")
    position = lax.axis_index("tm")
    depths = count.bit_length() - 1
    share = rank // count
    halo = lax.ppermute(
        record[rows - HALO :], "tm", [(source, source + 1) for source in range(count - 1)]
    )
    sketch = front(record, halo, gauge_lag, fir_taps[None, :], projector)

    widths = [cols]
    for depth in range(1, depths):
        widths.append(cols // 2 if cols % 256 == 0 else cols)
    narrowed = [depth for depth in range(depths - 1) if widths[depth + 1] < widths[depth]]
    assert narrowed == list(range(len(narrowed)))
    span = 2 ** len(narrowed)

    def bit_of(where, bit):
        return where // 2**bit % 2

    places = []
    for depth in range(depths):
        half = widths[depth] // 2 if depth in narrowed else 0
        flip = bit_of(position, depth)
        places += [flip * half, flip]
    places += [position ^ part for part in range(span)]
    joined = len(places)
    for part in range(span):
        places.append(sum([bit_of(position ^ part, bit) * (cols >> (bit + 1)) for bit in narrowed], 0))
    places = jnp.stack([position * 0 + place for place in places]).astype(jnp.int32)
    kept = ahead = None
    for depth in range(depths):
        first, last = depth == 0, depth == depths - 1
        mask = 2**depth
        here = widths[depth]
        if not last:
            other = swap(sketch, "tm", mask)
        if first:
            grams = gather_parts(pair_gram(sketch, other), "chan")
        else:
            packed, *kept = kept
            grams = [*kept, *ahead, swap(packed, "tm", mask)]
        if last:
            if not first:
                sketch = hold(sketch, *grams[-2:])
            other = swap(sketch, "tm", mask)
            mixing = last_filter_call(grams, compress, places, 2 * depth, first, share, span)
            pieces = mix(mixing, sketch, other, span, F32)
            break
        after = [] if first else [packed]
        part = ahead_gram(sketch, other, swap(sketch, "tm", 2 * mask), here, *after)
        if widths[depth + 1] == here and depth + 2 == depths:
            mixing, packed, level = level_filter_call(grams, compress, places, 2 * depth, first)
            (merged,) = mix(mixing, sketch, other, 1, BF16)
        else:
            mixing, merged, full = filter_call(
                grams, compress, places, 2 * depth, sketch, other, here, widths[depth + 1], first
            )
            packed, level = level_call(mixing, full)
        kept = packed, mixing, level
        for bit in [b for b in narrowed if b < depth]:
            part = add_after(part, swap(part, "tm", 2**bit), grams[-1])
        parts = gather_parts(part, "chan")
        total = sum(piece.astype(F32) for piece in parts).astype(BF16)
        ahead = [total, swap(total, "tm", mask)]
        sketch = merged
    if span == 1:
        return pieces[0]
    pieces = [pieces[0]] + [swap(piece, "tm", part) for part, piece in enumerate(pieces[1:], 1)]
    return join(places, joined, pieces)


def solution(mesh):
    return jax.shard_map(
        on_device,
        mesh=mesh,
        in_specs=(P("tm", "chan"), P(), P("chan"), P("tm", None), P()),
        out_specs=P("tm", "chan"),
        check_vma=False,
    )
```

```python
import functools

import jax
import jax.numpy as jnp
from jax import lax
from jax.experimental import pallas as pl
from jax.experimental.pallas import tpu as pltpu
from jax.sharding import PartitionSpec as P

TAPS = 64
GAUGE_MAX = 16
K_ITERS = 8
HALO = TAPS + GAUGE_MAX
BLOCK = 128
STEP = 16
CHUNK = 1024
EXTRA = 16
F32 = jnp.float32
BF16 = jnp.bfloat16
ANY = pl.BlockSpec(memory_space=pl.ANY)
HBM = pl.BlockSpec(memory_space=pltpu.HBM)
SMEM = pl.BlockSpec(memory_space=pltpu.SMEM)
VMEM = pl.BlockSpec(memory_space=pltpu.VMEM)
PARAMS = pltpu.CompilerParams(vmem_limit_bytes=40 * 2**20)


def dot(a, b):
    return jnp.dot(a, b, preferred_element_type=F32)


def dot_nt(a, b):
    return lax.dot_general(a, b, (((1,), (1,)), ((), ())), preferred_element_type=F32)


def split(a):
    high = a.astype(BF16)
    return high, (a - high.astype(F32)).astype(BF16)


def dot3_split(ah, al, bh, bl):
    rows = ah.shape[0]
    wide = dot(jnp.concatenate([ah, al], 0), bh)
    return wide[:rows] + (wide[rows:] + dot(ah, bl))


def dot3(a, b):
    return dot3_split(*split(a), *split(b))


def dot3_nt(a, b):
    ah, al = split(a)
    bh, bl = split(b)
    return dot_nt(ah, bh) + (dot_nt(ah, bl) + dot_nt(al, bh))


def eye_mask(n):
    row = lax.broadcasted_iota(jnp.int32, (n, n), 0)
    col = lax.broadcasted_iota(jnp.int32, (n, n), 1)
    return row == col


def one_hot(shape, place):
    row = lax.broadcasted_iota(jnp.int32, shape, 0)
    col = lax.broadcasted_iota(jnp.int32, shape, 1)
    return jnp.where(place(row) == col, 1.0, 0.0).astype(BF16)


def front_kernel(first, last, *refs):
    if first == 0:
        record, halo, lag, band, weights, begun, out, strain = refs
    else:
        record, lag_ref, taps_ref, projector_ref, out, band, head_weights, head = refs[:8]
        strain, weights, lag, taps, projector, sems = refs[8:]
        halo = begun = None

        @pl.when(pl.program_id(0) == 0)
        def _():
            sources, targets = (lag_ref, taps_ref, projector_ref), (lag, taps, projector)
            copies = [
                pltpu.make_async_copy(source, target, sems.at[i])
                for i, (source, target) in enumerate(zip(sources, targets))
            ]
            for copy in copies:
                copy.start()
            for copy in copies:
                copy.wait()
            turn = one_hot((TAPS, 256), lambda tap: TAPS - tap)
            line = dot(jnp.broadcast_to(taps[...], (8, TAPS)), turn)[0:1]
            line = jnp.broadcast_to(line, (BLOCK + GAUGE_MAX, 256))
            rolled = pltpu.roll(line, 0, 1, stride=1, stride_axis=0)[:, : BLOCK + HALO]
            order = one_hot((2 * BLOCK, BLOCK + GAUGE_MAX), lambda row: row // 8 + STEP * (row % 8))
            band[...] = dot(order, rolled.astype(BF16)).astype(BF16)
            order = one_hot((BLOCK, BLOCK), lambda row: row // 8 + STEP * (row % 8))
            for block in range(projector.shape[0] // BLOCK):
                part = slice(block * BLOCK, (block + 1) * BLOCK)
                weights[:, part] = dot(order, projector[part, :]).T.astype(BF16)
            head_weights[...] = weights[:, 0:BLOCK]

    cols = record.shape[1]
    lane = min(128, cols)
    lanes = cols // lane
    group = 256 if cols % 256 == 0 else lane
    total = None
    used = first * BLOCK
    if first > 0:
        head[...] = record[0:BLOCK, :]
    for block in range(first, last):
        start = block * BLOCK
        for g in range(0, cols, group):
            if block == 0:
                segment = jnp.concatenate([halo[:, g : g + group], record[0:BLOCK, g : g + group]], 0)
            else:
                segment = record[start - HALO : start + BLOCK, g : g + group]
            result = dot(band[...], segment)
            for c in range(0, group, lane):
                line = pl.program_id(0) * lanes + (g + c) // lane
                shift = GAUGE_MAX - lag[pl.ds(line, 1), :]
                wide = result[:, c : c + lane]
                picked = wide
                for step in (8, 4, 2, 1):
                    length = BLOCK + 8 * (step - 1)
                    picked = jnp.where(
                        (shift & step) != 0, picked[8 * step : 8 * step + length], picked[:length]
                    )
                strain[start : start + BLOCK, g + c : g + c + lane] = (wide[BLOCK:] - picked).astype(
                    BF16
                )
        done = start + BLOCK
        if done % CHUNK == 0 or block == last - 1:
            part = dot(weights[:, used:done], strain[used:done, :])
            total = part if total is None else total + part
            used = done
    if begun is None:
        out[...] = total
    else:
        out[...] = (total + begun[...]).astype(BF16)


def front_call(blocks, args, in_specs, out_specs, out_shape, scratch, steps, grant):
    return pl.pallas_call(
        functools.partial(front_kernel, *blocks),
        grid=(steps,),
        in_specs=in_specs,
        out_specs=out_specs,
        out_shape=out_shape,
        scratch_shapes=scratch,
        compiler_params=pltpu.CompilerParams(vmem_limit_bytes=grant * 2**20),
        name="front",
    )(*args)


def front(record, halo, lag, taps, projector):
    rows, cols = record.shape
    rank = projector.shape[1]
    lag = lag.reshape(cols // 128, 128) if cols % 128 == 0 else lag[None, :]
    whole = lambda a: pl.BlockSpec(a.shape, lambda i: (0, 0))
    columns = lambda count, tile: pl.BlockSpec((count, tile), lambda i: (0, i))
    tile = next((t for t in (512, 640, 256, 128) if cols % t == 0), cols)
    shapes = [
        jax.ShapeDtypeStruct((rank, cols), F32),
        jax.ShapeDtypeStruct((2 * BLOCK, BLOCK + HALO), BF16),
        jax.ShapeDtypeStruct((rank, BLOCK), BF16),
        jax.ShapeDtypeStruct((BLOCK, cols), BF16),
    ]
    begun, band, weights, head = front_call(
        (1, rows // BLOCK),
        (record, lag, taps, projector),
        [columns(rows, tile), HBM, HBM, HBM],
        [columns(rank, tile), whole(shapes[1]), whole(shapes[2]), columns(BLOCK, tile)],
        shapes,
        [
            pltpu.VMEM((rows, tile), BF16),
            pltpu.VMEM((rank, rows), BF16),
            pltpu.VMEM(lag.shape, lag.dtype),
            pltpu.VMEM(taps.shape, BF16),
            pltpu.VMEM(projector.shape, BF16),
            pltpu.SemaphoreType.DMA((3,)),
        ],
        cols // tile,
        48,
    )
    tile = cols // 2 if cols % 256 == 0 else cols
    return front_call(
        (0, 1),
        (head, halo, lag, band, weights, begun),
        [
            columns(BLOCK, tile),
            columns(HALO, tile),
            whole(lag),
            whole(band),
            whole(weights),
            columns(rank, tile),
        ],
        columns(rank, tile),
        jax.ShapeDtypeStruct((rank, cols), BF16),
        [pltpu.VMEM((BLOCK, tile), BF16)],
        cols // tile,
        32,
    )


def pair_kernel(own, other, out):
    rank = own.shape[0]
    a, b = own[...], other[...]
    aa, ab, bb = dot_nt(a, a), dot_nt(a, b), dot_nt(b, b)
    diag = eye_mask(rank)
    trace = jnp.sum(jnp.where(diag, aa + bb, 0.0), axis=(0, 1), keepdims=True)
    mean = trace / (2 * rank)
    aa = aa - jnp.where(diag, mean, 0.0)
    bb = bb - jnp.where(diag, mean, 0.0)
    row = lax.broadcasted_iota(jnp.int32, (rank, rank), 0)
    col = lax.broadcasted_iota(jnp.int32, (rank, rank), 1)
    out[0:rank, :] = jnp.where(row <= col, aa, bb).astype(BF16)
    out[rank : 2 * rank, :] = ab.astype(BF16)
    bottom = jnp.sum(jnp.where(diag, bb, 0.0), axis=0, keepdims=True)
    full = jnp.broadcast_to(mean, (EXTRA, rank))
    high = full.astype(BF16).astype(F32)
    mid = (full - high).astype(BF16).astype(F32)
    low = full - high - mid
    line = lax.broadcasted_iota(jnp.int32, (EXTRA, rank), 0)
    extra = jnp.where(line == 0, high, jnp.where(line == 1, mid, jnp.where(line == 2, low, 0.0)))
    out[2 * rank :, :] = jnp.where(line == 3, jnp.broadcast_to(bottom, (EXTRA, rank)), extra).astype(
        BF16
    )


def pair_gram(own, other):
    rank = own.shape[0]
    return pl.pallas_call(
        pair_kernel,
        out_shape=jax.ShapeDtypeStruct((2 * rank + EXTRA, rank), BF16),
        compiler_params=PARAMS,
        name="pair_gram",
    )(own, other)


def ahead_kernel(width, own, sibling, partner, *refs):
    out = refs[-1]
    rank = own.shape[0]
    there = partner[:, :width]
    out[0:rank, :] = dot_nt(own[:, :width], there).astype(out.dtype)
    out[rank:, :] = dot_nt(sibling[:, :width], there).astype(out.dtype)


def ahead_gram(own, sibling, partner, width, *after):
    rank = own.shape[0]
    return pl.pallas_call(
        functools.partial(ahead_kernel, width),
        in_specs=[VMEM] * 3 + [ANY] * len(after),
        out_shape=jax.ShapeDtypeStruct((2 * rank, rank), BF16),
        compiler_params=PARAMS,
        name="ahead_gram",
    )(own, sibling, partner, *after)


def summed(parts):
    total = parts[0][...].astype(F32)
    for part in parts[1:]:
        total = total + part[...].astype(F32)
    return total


def hold_kernel(*refs):
    pass


def hold(value, *until):
    return pl.pallas_call(
        hold_kernel,
        in_specs=[ANY] * (1 + len(until)),
        out_specs=ANY,
        out_shape=jax.ShapeDtypeStruct(value.shape, value.dtype),
        input_output_aliases={0: 0},
        compiler_params=pltpu.CompilerParams(vmem_limit_bytes=16 * 2**20),
        name="hold",
    )(value, *until)


def add_kernel(one, two, _, out):
    out[...] = (one[...].astype(F32) + two[...].astype(F32)).astype(BF16)


def add_after(one, two, after):
    return pl.pallas_call(
        add_kernel,
        in_specs=[VMEM, VMEM, ANY],
        out_shape=jax.ShapeDtypeStruct(one.shape, BF16),
        compiler_params=pltpu.CompilerParams(vmem_limit_bytes=16 * 2**20),
        name="add_after",
    )(one, two, after)


def square_of(aa, ab, bb):
    return jnp.concatenate(
        [jnp.concatenate([aa, ab], 1), jnp.concatenate([ab.T, bb], 1)], 0
    )


def first_gram(parts):
    total = summed(parts)
    rank = total.shape[1]
    both = total[0:rank]
    ab = total[rank : 2 * rank]
    extra = total[2 * rank :]
    mean = extra[0:1, 0:1] + extra[1:2, 0:1] + extra[2:3, 0:1]
    row = lax.broadcasted_iota(jnp.int32, (rank, rank), 0)
    col = lax.broadcasted_iota(jnp.int32, (rank, rank), 1)
    turned = both.T
    aa = jnp.where(row <= col, both, turned)
    bb = jnp.where(row > col, both, jnp.where(row < col, turned, extra[3:4, :]))
    return square_of(aa, ab, bb), mean


def later_gram(own_mix, own_level, ahead, sibling_ahead, other):
    rank = own_mix.shape[0]
    mine, theirs = ahead[...], sibling_ahead[...]
    cross = jnp.concatenate(
        [
            jnp.concatenate([mine[:rank], theirs[rank:]], 1),
            jnp.concatenate([mine[rank:], theirs[:rank]], 1),
        ],
        0,
    )
    high, low = split(own_mix[...])
    half = dot(high, cross) + dot(low, cross)
    high, low = split(half)
    place = other.shape[1] - 4 * rank
    other_mix = other[:, place : place + 2 * rank]
    ab = dot_nt(high, other_mix) + dot_nt(low, other_mix)
    place += 2 * rank
    other_level = other[:, place : place + rank].astype(F32) + other[:, place + rank :].astype(F32)
    gram = square_of(own_level[...], ab, other_level)
    diag = eye_mask(gram.shape[0])
    mean = jnp.sum(jnp.where(diag, gram, 0.0), axis=(0, 1), keepdims=True) / gram.shape[0]
    return gram - jnp.where(diag, mean, 0.0), mean


def filter_kernel(count, first, kind, used, base, *refs):
    grams, refs = refs[:count], refs[count:]
    compress, places, refs = refs[0], refs[1], refs[2:]
    last = kind == "last"
    rank = compress.shape[1]
    if last:
        mix_out, turned = refs
        share = mix_out.shape[0] // used
    elif kind == "level":
        mix_out, packed, level, turned = refs
    else:
        own, other, mix_out, sketch, whole, pair, turned, sems = refs
        width = pair.shape[1]
        if width < used:
            span = pl.ds(pl.multiple_of(places[base], 128), width)
        else:
            span = slice(0, width)
        copies = [
            pltpu.make_async_copy(
                source.at[:, span], pair.at[slice(i * rank, (i + 1) * rank)], sems.at[i]
            )
            for i, source in enumerate((own, other))
        ]
        for copy in copies:
            copy.start()
    flip = places[base + 1]
    for i in range(2):
        half = compress[pl.ds(pl.multiple_of((flip + i) % 2 * rank, 128), rank), :]
        turned[:, i * rank : (i + 1) * rank] = half.T
    if last:
        parts = [
            turned[pl.ds(pl.multiple_of(places[base + 2 + i] * share, 8), share), :]
            for i in range(used)
        ]
        compress_t = jnp.concatenate(parts, 0) if used > 1 else parts[0]
    else:
        compress_t = turned[...]
    gram, mean = first_gram(grams) if first else later_gram(*grams)
    size = gram.shape[0]
    eye = jnp.where(eye_mask(size), 1.0, 0.0)
    z = gram * lax.rsqrt(jnp.sum(gram * gram, axis=(0, 1), keepdims=True) + 1e-6)
    for step in range(K_ITERS):
        zh, zl = split(z)
        square = dot3_split(zh, zl, zh, zl)
        factor = split(1.5 * eye - 0.5 * square)
        if step < K_ITERS - 1:
            z = dot3_split(zh, zl, *factor)
        else:
            turn = dot3_split(*split(compress_t), zh, zl)
            mixing = 0.5 * (compress_t + dot3_split(*split(turn), *factor))
    mix_out[...] = mixing
    if last:
        return
    full = gram + mean * eye
    if kind == "level":
        pack_level(mixing, full, packed, level)
        return
    whole[...] = full
    for copy in copies:
        copy.wait()
    both = jnp.concatenate(split(mixing), 0)
    tile = next((t for t in (640, 512, 256, 128) if width % t == 0), width)
    for c in range(0, width, tile):
        part = dot(both, pair[:, c : c + tile])
        sketch[:, c : c + tile] = (part[:rank] + part[rank:]).astype(BF16)


def pack_level(mixing, full, packed, level):
    rank = mixing.shape[0]
    block = dot3_nt(dot3(mixing, full), mixing)
    level[...] = block
    packed[:, : 2 * rank] = mixing.astype(BF16)
    high, low = split(block)
    packed[:, 2 * rank : 3 * rank] = high
    packed[:, 3 * rank :] = low


def level_kernel(mixing, full, packed, level):
    pack_level(mixing[...], full[...], packed, level)


def level_shapes(rank):
    return [
        jax.ShapeDtypeStruct((rank, 4 * rank), BF16),
        jax.ShapeDtypeStruct((rank, rank), F32),
    ]


def level_call(mixing, full):
    return pl.pallas_call(
        level_kernel,
        out_shape=level_shapes(mixing.shape[0]),
        compiler_params=pltpu.CompilerParams(vmem_limit_bytes=16 * 2**20),
        name="level",
    )(mixing, full)


def level_filter_call(grams, compress, places, base, first):
    rank = compress.shape[1]
    args = [*grams, compress]
    return pl.pallas_call(
        functools.partial(filter_kernel, len(grams), first, "level", 0, base),
        in_specs=[VMEM] * len(args) + [SMEM],
        out_shape=[jax.ShapeDtypeStruct((rank, 2 * rank), F32), *level_shapes(rank)],
        scratch_shapes=[pltpu.VMEM((rank, 2 * rank), F32)],
        compiler_params=PARAMS,
        name="sign_filter",
    )(*args, places)


def filter_call(grams, compress, places, base, own, other, used, width, first):
    rank = own.shape[0]
    args = [*grams, compress]
    return pl.pallas_call(
        functools.partial(filter_kernel, len(grams), first, "sketch", used, base),
        in_specs=[VMEM] * len(args) + [SMEM, ANY, ANY],
        out_shape=[
            jax.ShapeDtypeStruct((rank, 2 * rank), F32),
            jax.ShapeDtypeStruct((rank, width), BF16),
            jax.ShapeDtypeStruct((2 * rank, 2 * rank), F32),
        ],
        scratch_shapes=[
            pltpu.VMEM((2 * rank, width), BF16),
            pltpu.VMEM((rank, 2 * rank), F32),
            pltpu.SemaphoreType.DMA((2,)),
        ],
        compiler_params=PARAMS,
        name="sign_filter",
    )(*args, places, own, other)


def last_filter_call(grams, compress, places, base, first, share, pieces):
    rank = compress.shape[1]
    args = [*grams, compress]
    return pl.pallas_call(
        functools.partial(filter_kernel, len(grams), first, "last", pieces, base),
        in_specs=[VMEM] * len(args) + [SMEM],
        out_shape=jax.ShapeDtypeStruct((share * pieces, 2 * rank), F32),
        scratch_shapes=[pltpu.VMEM((rank, 2 * rank), F32)],
        compiler_params=PARAMS,
        cost_estimate=pl.CostEstimate(
            flops=50 * K_ITERS * (2 * rank) ** 3, bytes_accessed=0, transcendentals=0
        ),
        name="sign_filter",
    )(*args, places)


def mix_kernel(mixing, own, other, *out):
    rank = own.shape[0]
    rows, share = mixing.shape[0], out[0].shape[0]
    both = jnp.concatenate(split(mixing[...]), 0)
    width = own.shape[1]
    tile = next((t for t in (640, 512, 256, 128) if width % t == 0), width)
    for c in range(0, width, tile):
        span = slice(c, c + tile)
        part = dot(both, jnp.concatenate([own[:, span], other[:, span]], 0))
        part = part[:rows] + part[rows:]
        for i, piece in enumerate(out):
            piece[:, span] = part[i * share : (i + 1) * share].astype(piece.dtype)


def mix(mixing, own, other, pieces, dtype):
    shape = jax.ShapeDtypeStruct((mixing.shape[0] // pieces, own.shape[1]), dtype)
    return pl.pallas_call(
        mix_kernel,
        out_shape=[shape] * pieces,
        compiler_params=pltpu.CompilerParams(vmem_limit_bytes=16 * 2**20),
        name="mix",
    )(mixing, own, other)


def swap(value, axis, mask):
    count = lax.axis_size(axis)
    return lax.ppermute(value, axis, [(source, source ^ mask) for source in range(count)])


def gather_parts(value, axis):
    count = lax.axis_size(axis)
    if count > 4 or count & (count - 1):
        return [lax.psum(value.astype(F32), axis)]
    return [value] + [swap(value, axis, mask) for mask in range(1, count)]


def join_kernel(base, places, *refs):
    out = refs[-1]
    width = refs[0].shape[1]
    for i, piece in enumerate(refs[:-1]):
        out[:, pl.ds(pl.multiple_of(places[base + i], 128), width)] = piece[...]


def join(places, base, pieces):
    share, width = pieces[0].shape
    return pl.pallas_call(
        functools.partial(join_kernel, base),
        in_specs=[SMEM] + [VMEM] * len(pieces),
        out_shape=jax.ShapeDtypeStruct((share, width * len(pieces)), F32),
        compiler_params=pltpu.CompilerParams(vmem_limit_bytes=16 * 2**20),
        name="join",
    )(places, *pieces)


def on_device(record, fir_taps, gauge_lag, projector, compress):
    rows, cols = record.shape
    rank = projector.shape[1]
    count = lax.axis_size("tm")
    position = lax.axis_index("tm")
    depths = count.bit_length() - 1
    share = rank // count
    halo = lax.ppermute(
        record[rows - HALO :], "tm", [(source, source + 1) for source in range(count - 1)]
    )
    sketch = front(record, halo, gauge_lag, fir_taps[None, :], projector)

    widths = [cols]
    for depth in range(1, depths):
        widths.append(cols // 2 if cols % 256 == 0 else cols)
    narrowed = [depth for depth in range(depths - 1) if widths[depth + 1] < widths[depth]]
    assert narrowed == list(range(len(narrowed)))
    span = 2 ** len(narrowed)

    def bit_of(where, bit):
        return where // 2**bit % 2

    places = []
    for depth in range(depths):
        half = widths[depth] // 2 if depth in narrowed else 0
        flip = bit_of(position, depth)
        places += [flip * half, flip]
    places += [position ^ part for part in range(span)]
    joined = len(places)
    for part in range(span):
        places.append(sum([bit_of(position ^ part, bit) * (cols >> (bit + 1)) for bit in narrowed], 0))
    places = jnp.stack([position * 0 + place for place in places]).astype(jnp.int32)
    kept = ahead = None
    for depth in range(depths):
        first, last = depth == 0, depth == depths - 1
        mask = 2**depth
        here = widths[depth]
        if not last:
            other = swap(sketch, "tm", mask)
        if first:
            grams = gather_parts(pair_gram(sketch, other), "chan")
        else:
            packed, *kept = kept
            grams = [*kept, *ahead, swap(packed, "tm", mask)]
        if last:
            if not first:
                sketch = hold(sketch, *grams[-2:])
            other = swap(sketch, "tm", mask)
            mixing = last_filter_call(grams, compress, places, 2 * depth, first, share, span)
            pieces = mix(mixing, sketch, other, span, F32)
            break
        after = [] if first else [packed]
        part = ahead_gram(sketch, other, swap(sketch, "tm", 2 * mask), here, *after)
        if widths[depth + 1] == here and depth + 2 == depths:
            mixing, packed, level = level_filter_call(grams, compress, places, 2 * depth, first)
            (merged,) = mix(mixing, sketch, other, 1, BF16)
        else:
            mixing, merged, full = filter_call(
                grams, compress, places, 2 * depth, sketch, other, here, widths[depth + 1], first
            )
            packed, level = level_call(mixing, full)
        kept = packed, mixing, level
        for bit in [b for b in narrowed if b < depth]:
            part = add_after(part, swap(part, "tm", 2**bit), grams[-1])
        parts = gather_parts(part, "chan")
        total = sum(piece.astype(F32) for piece in parts).astype(BF16)
        ahead = [total, swap(total, "tm", mask)]
        sketch = merged
    if span == 1:
        return pieces[0]
    pieces = [pieces[0]] + [swap(piece, "tm", part) for part, piece in enumerate(pieces[1:], 1)]
    return join(places, joined, pieces)


def solution(mesh):
    return jax.shard_map(
        on_device,
        mesh=mesh,
        in_specs=(P("tm", "chan"), P(), P("chan"), P("tm", None), P()),
        out_specs=P("tm", "chan"),
        check_vma=False,
    )
```

```python
import functools

import jax
import jax.numpy as jnp
from jax import lax
from jax.experimental import pallas as pl
from jax.experimental.pallas import tpu as pltpu
from jax.sharding import PartitionSpec as P

TAPS = 64
GAUGE_MAX = 16
K_ITERS = 8
HALO = TAPS + GAUGE_MAX
BLOCK = 128
STEP = 16
CHUNK = 1024
EXTRA = 16
F32 = jnp.float32
BF16 = jnp.bfloat16
ANY = pl.BlockSpec(memory_space=pl.ANY)
HBM = pl.BlockSpec(memory_space=pltpu.HBM)
SMEM = pl.BlockSpec(memory_space=pltpu.SMEM)
VMEM = pl.BlockSpec(memory_space=pltpu.VMEM)
PARAMS = pltpu.CompilerParams(vmem_limit_bytes=40 * 2**20)


def dot(a, b):
    return jnp.dot(a, b, preferred_element_type=F32)


def dot_nt(a, b):
    return lax.dot_general(a, b, (((1,), (1,)), ((), ())), preferred_element_type=F32)


def split(a):
    high = a.astype(BF16)
    return high, (a - high.astype(F32)).astype(BF16)


def dot3_split(ah, al, bh, bl):
    rows = ah.shape[0]
    wide = dot(jnp.concatenate([ah, al], 0), bh)
    return wide[:rows] + (wide[rows:] + dot(ah, bl))


def dot3(a, b):
    return dot3_split(*split(a), *split(b))


def dot3_nt(a, b):
    ah, al = split(a)
    bh, bl = split(b)
    return dot_nt(ah, bh) + (dot_nt(ah, bl) + dot_nt(al, bh))


def eye_mask(n):
    row = lax.broadcasted_iota(jnp.int32, (n, n), 0)
    col = lax.broadcasted_iota(jnp.int32, (n, n), 1)
    return row == col


def one_hot(shape, place):
    row = lax.broadcasted_iota(jnp.int32, shape, 0)
    col = lax.broadcasted_iota(jnp.int32, shape, 1)
    return jnp.where(place(row) == col, 1.0, 0.0).astype(BF16)


def front_kernel(first, last, *refs):
    if first == 0:
        record, halo, lag, band, weights, begun, out, strain = refs
    else:
        record, lag_ref, taps_ref, projector_ref, out, band, head_weights, head = refs[:8]
        strain, weights, lag, taps, projector, sems = refs[8:]
        halo = begun = None

        @pl.when(pl.program_id(0) == 0)
        def _():
            sources, targets = (lag_ref, taps_ref, projector_ref), (lag, taps, projector)
            copies = [
                pltpu.make_async_copy(source, target, sems.at[i])
                for i, (source, target) in enumerate(zip(sources, targets))
            ]
            for copy in copies:
                copy.start()
            for copy in copies:
                copy.wait()
            turn = one_hot((TAPS, 256), lambda tap: TAPS - tap)
            line = dot(jnp.broadcast_to(taps[...], (8, TAPS)), turn)[0:1]
            line = jnp.broadcast_to(line, (BLOCK + GAUGE_MAX, 256))
            rolled = pltpu.roll(line, 0, 1, stride=1, stride_axis=0)[:, : BLOCK + HALO]
            order = one_hot((2 * BLOCK, BLOCK + GAUGE_MAX), lambda row: row // 8 + STEP * (row % 8))
            band[...] = dot(order, rolled.astype(BF16)).astype(BF16)
            order = one_hot((BLOCK, BLOCK), lambda row: row // 8 + STEP * (row % 8))
            for block in range(projector.shape[0] // BLOCK):
                part = slice(block * BLOCK, (block + 1) * BLOCK)
                weights[:, part] = dot(order, projector[part, :]).T.astype(BF16)
            head_weights[...] = weights[:, 0:BLOCK]

    cols = record.shape[1]
    lane = min(128, cols)
    lanes = cols // lane
    group = 256 if cols % 256 == 0 else lane
    total = None
    used = first * BLOCK
    if first > 0:
        head[...] = record[0:BLOCK, :]
    for block in range(first, last):
        start = block * BLOCK
        for g in range(0, cols, group):
            if block == 0:
                segment = jnp.concatenate([halo[:, g : g + group], record[0:BLOCK, g : g + group]], 0)
            else:
                segment = record[start - HALO : start + BLOCK, g : g + group]
            result = dot(band[...], segment)
            for c in range(0, group, lane):
                line = pl.program_id(0) * lanes + (g + c) // lane
                shift = GAUGE_MAX - lag[pl.ds(line, 1), :]
                wide = result[:, c : c + lane]
                picked = wide
                for step in (8, 4, 2, 1):
                    length = BLOCK + 8 * (step - 1)
                    picked = jnp.where(
                        (shift & step) != 0, picked[8 * step : 8 * step + length], picked[:length]
                    )
                strain[start : start + BLOCK, g + c : g + c + lane] = (wide[BLOCK:] - picked).astype(
                    BF16
                )
        done = start + BLOCK
        if done % CHUNK == 0 or block == last - 1:
            part = dot(weights[:, used:done], strain[used:done, :])
            total = part if total is None else total + part
            used = done
    if begun is None:
        out[...] = total
    else:
        out[...] = (total + begun[...]).astype(BF16)


def front_call(blocks, args, in_specs, out_specs, out_shape, scratch, steps, grant):
    return pl.pallas_call(
        functools.partial(front_kernel, *blocks),
        grid=(steps,),
        in_specs=in_specs,
        out_specs=out_specs,
        out_shape=out_shape,
        scratch_shapes=scratch,
        compiler_params=pltpu.CompilerParams(vmem_limit_bytes=grant * 2**20),
        name="front",
    )(*args)


def front(record, halo, lag, taps, projector):
    rows, cols = record.shape
    rank = projector.shape[1]
    lag = lag.reshape(cols // 128, 128) if cols % 128 == 0 else lag[None, :]
    whole = lambda a: pl.BlockSpec(a.shape, lambda i: (0, 0))
    columns = lambda count, tile: pl.BlockSpec((count, tile), lambda i: (0, i))
    tile = next((t for t in (1280, 640, 512, 256, 128) if cols % t == 0), cols)
    shapes = [
        jax.ShapeDtypeStruct((rank, cols), F32),
        jax.ShapeDtypeStruct((2 * BLOCK, BLOCK + HALO), BF16),
        jax.ShapeDtypeStruct((rank, BLOCK), BF16),
        jax.ShapeDtypeStruct((BLOCK, cols), BF16),
    ]
    begun, band, weights, head = front_call(
        (1, rows // BLOCK),
        (record, lag, taps, projector),
        [columns(rows, tile), HBM, HBM, HBM],
        [columns(rank, tile), whole(shapes[1]), whole(shapes[2]), columns(BLOCK, tile)],
        shapes,
        [
            pltpu.VMEM((rows, tile), BF16),
            pltpu.VMEM((rank, rows), BF16),
            pltpu.VMEM(lag.shape, lag.dtype),
            pltpu.VMEM(taps.shape, BF16),
            pltpu.VMEM(projector.shape, BF16),
            pltpu.SemaphoreType.DMA((3,)),
        ],
        cols // tile,
        48,
    )
    tile = cols // 2 if cols % 256 == 0 else cols
    return front_call(
        (0, 1),
        (head, halo, lag, band, weights, begun),
        [
            columns(BLOCK, tile),
            columns(HALO, tile),
            whole(lag),
            whole(band),
            whole(weights),
            columns(rank, tile),
        ],
        columns(rank, tile),
        jax.ShapeDtypeStruct((rank, cols), BF16),
        [pltpu.VMEM((BLOCK, tile), BF16)],
        cols // tile,
        32,
    )


def pair_kernel(own, other, out):
    rank = own.shape[0]
    a, b = own[...], other[...]
    aa, ab, bb = dot_nt(a, a), dot_nt(a, b), dot_nt(b, b)
    diag = eye_mask(rank)
    trace = jnp.sum(jnp.where(diag, aa + bb, 0.0), axis=(0, 1), keepdims=True)
    mean = trace / (2 * rank)
    aa = aa - jnp.where(diag, mean, 0.0)
    bb = bb - jnp.where(diag, mean, 0.0)
    row = lax.broadcasted_iota(jnp.int32, (rank, rank), 0)
    col = lax.broadcasted_iota(jnp.int32, (rank, rank), 1)
    out[0:rank, :] = jnp.where(row <= col, aa, bb).astype(BF16)
    out[rank : 2 * rank, :] = ab.astype(BF16)
    bottom = jnp.sum(jnp.where(diag, bb, 0.0), axis=0, keepdims=True)
    full = jnp.broadcast_to(mean, (EXTRA, rank))
    high = full.astype(BF16).astype(F32)
    mid = (full - high).astype(BF16).astype(F32)
    low = full - high - mid
    line = lax.broadcasted_iota(jnp.int32, (EXTRA, rank), 0)
    extra = jnp.where(line == 0, high, jnp.where(line == 1, mid, jnp.where(line == 2, low, 0.0)))
    out[2 * rank :, :] = jnp.where(line == 3, jnp.broadcast_to(bottom, (EXTRA, rank)), extra).astype(
        BF16
    )


def pair_gram(own, other):
    rank = own.shape[0]
    return pl.pallas_call(
        pair_kernel,
        out_shape=jax.ShapeDtypeStruct((2 * rank + EXTRA, rank), BF16),
        compiler_params=PARAMS,
        name="pair_gram",
    )(own, other)


def ahead_kernel(width, own, sibling, partner, *refs):
    out = refs[-1]
    rank = own.shape[0]
    there = partner[:, :width]
    out[0:rank, :] = dot_nt(own[:, :width], there).astype(out.dtype)
    out[rank:, :] = dot_nt(sibling[:, :width], there).astype(out.dtype)


def ahead_gram(own, sibling, partner, width, *after):
    rank = own.shape[0]
    return pl.pallas_call(
        functools.partial(ahead_kernel, width),
        in_specs=[VMEM] * 3 + [ANY] * len(after),
        out_shape=jax.ShapeDtypeStruct((2 * rank, rank), BF16),
        compiler_params=PARAMS,
        name="ahead_gram",
    )(own, sibling, partner, *after)


def summed(parts):
    total = parts[0][...].astype(F32)
    for part in parts[1:]:
        total = total + part[...].astype(F32)
    return total


def hold_kernel(*refs):
    pass


def hold(value, *until):
    return pl.pallas_call(
        hold_kernel,
        in_specs=[ANY] * (1 + len(until)),
        out_specs=ANY,
        out_shape=jax.ShapeDtypeStruct(value.shape, value.dtype),
        input_output_aliases={0: 0},
        compiler_params=pltpu.CompilerParams(vmem_limit_bytes=16 * 2**20),
        name="hold",
    )(value, *until)


def add_kernel(one, two, _, out):
    out[...] = (one[...].astype(F32) + two[...].astype(F32)).astype(BF16)


def add_after(one, two, after):
    return pl.pallas_call(
        add_kernel,
        in_specs=[VMEM, VMEM, ANY],
        out_shape=jax.ShapeDtypeStruct(one.shape, BF16),
        compiler_params=pltpu.CompilerParams(vmem_limit_bytes=16 * 2**20),
        name="add_after",
    )(one, two, after)


def square_of(aa, ab, bb):
    return jnp.concatenate(
        [jnp.concatenate([aa, ab], 1), jnp.concatenate([ab.T, bb], 1)], 0
    )


def first_gram(parts):
    total = summed(parts)
    rank = total.shape[1]
    both = total[0:rank]
    ab = total[rank : 2 * rank]
    extra = total[2 * rank :]
    mean = extra[0:1, 0:1] + extra[1:2, 0:1] + extra[2:3, 0:1]
    row = lax.broadcasted_iota(jnp.int32, (rank, rank), 0)
    col = lax.broadcasted_iota(jnp.int32, (rank, rank), 1)
    turned = both.T
    aa = jnp.where(row <= col, both, turned)
    bb = jnp.where(row > col, both, jnp.where(row < col, turned, extra[3:4, :]))
    return square_of(aa, ab, bb), mean


def later_gram(own_mix, own_level, ahead, sibling_ahead, other):
    rank = own_mix.shape[0]
    mine, theirs = ahead[...], sibling_ahead[...]
    cross = jnp.concatenate(
        [
            jnp.concatenate([mine[:rank], theirs[rank:]], 1),
            jnp.concatenate([mine[rank:], theirs[:rank]], 1),
        ],
        0,
    )
    high, low = split(own_mix[...])
    half = dot(high, cross) + dot(low, cross)
    high, low = split(half)
    place = other.shape[1] - 4 * rank
    other_mix = other[:, place : place + 2 * rank]
    ab = dot_nt(high, other_mix) + dot_nt(low, other_mix)
    place += 2 * rank
    other_level = other[:, place : place + rank].astype(F32) + other[:, place + rank :].astype(F32)
    gram = square_of(own_level[...], ab, other_level)
    diag = eye_mask(gram.shape[0])
    mean = jnp.sum(jnp.where(diag, gram, 0.0), axis=(0, 1), keepdims=True) / gram.shape[0]
    return gram - jnp.where(diag, mean, 0.0), mean


def filter_kernel(count, first, kind, used, base, *refs):
    grams, refs = refs[:count], refs[count:]
    compress, places, refs = refs[0], refs[1], refs[2:]
    last = kind == "last"
    rank = compress.shape[1]
    if last:
        mix_out, turned = refs
        share = mix_out.shape[0] // used
    elif kind == "level":
        mix_out, packed, level, turned = refs
    else:
        own, other, mix_out, sketch, whole, pair, turned, sems = refs
        width = pair.shape[1]
        if width < used:
            span = pl.ds(pl.multiple_of(places[base], 128), width)
        else:
            span = slice(0, width)
        copies = [
            pltpu.make_async_copy(
                source.at[:, span], pair.at[slice(i * rank, (i + 1) * rank)], sems.at[i]
            )
            for i, source in enumerate((own, other))
        ]
        for copy in copies:
            copy.start()
    flip = places[base + 1]
    for i in range(2):
        half = compress[pl.ds(pl.multiple_of((flip + i) % 2 * rank, 128), rank), :]
        turned[:, i * rank : (i + 1) * rank] = half.T
    if last:
        parts = [
            turned[pl.ds(pl.multiple_of(places[base + 2 + i] * share, 8), share), :]
            for i in range(used)
        ]
        compress_t = jnp.concatenate(parts, 0) if used > 1 else parts[0]
    else:
        compress_t = turned[...]
    gram, mean = first_gram(grams) if first else later_gram(*grams)
    size = gram.shape[0]
    eye = jnp.where(eye_mask(size), 1.0, 0.0)
    z = gram * lax.rsqrt(jnp.sum(gram * gram, axis=(0, 1), keepdims=True) + 1e-6)
    for step in range(K_ITERS):
        zh, zl = split(z)
        square = dot3_split(zh, zl, zh, zl)
        factor = split(1.5 * eye - 0.5 * square)
        if step < K_ITERS - 1:
            z = dot3_split(zh, zl, *factor)
        else:
            turn = dot3_split(*split(compress_t), zh, zl)
            mixing = 0.5 * (compress_t + dot3_split(*split(turn), *factor))
    mix_out[...] = mixing
    if last:
        return
    full = gram + mean * eye
    if kind == "level":
        pack_level(mixing, full, packed, level)
        return
    whole[...] = full
    for copy in copies:
        copy.wait()
    both = jnp.concatenate(split(mixing), 0)
    tile = next((t for t in (640, 512, 256, 128) if width % t == 0), width)
    for c in range(0, width, tile):
        part = dot(both, pair[:, c : c + tile])
        sketch[:, c : c + tile] = (part[:rank] + part[rank:]).astype(BF16)


def pack_level(mixing, full, packed, level):
    rank = mixing.shape[0]
    block = dot3_nt(dot3(mixing, full), mixing)
    level[...] = block
    packed[:, : 2 * rank] = mixing.astype(BF16)
    high, low = split(block)
    packed[:, 2 * rank : 3 * rank] = high
    packed[:, 3 * rank :] = low


def level_kernel(mixing, full, packed, level):
    pack_level(mixing[...], full[...], packed, level)


def level_shapes(rank):
    return [
        jax.ShapeDtypeStruct((rank, 4 * rank), BF16),
        jax.ShapeDtypeStruct((rank, rank), F32),
    ]


def level_call(mixing, full):
    return pl.pallas_call(
        level_kernel,
        out_shape=level_shapes(mixing.shape[0]),
        compiler_params=pltpu.CompilerParams(vmem_limit_bytes=16 * 2**20),
        name="level",
    )(mixing, full)


def level_filter_call(grams, compress, places, base, first):
    rank = compress.shape[1]
    args = [*grams, compress]
    return pl.pallas_call(
        functools.partial(filter_kernel, len(grams), first, "level", 0, base),
        in_specs=[VMEM] * len(args) + [SMEM],
        out_shape=[jax.ShapeDtypeStruct((rank, 2 * rank), F32), *level_shapes(rank)],
        scratch_shapes=[pltpu.VMEM((rank, 2 * rank), F32)],
        compiler_params=PARAMS,
        name="sign_filter",
    )(*args, places)


def filter_call(grams, compress, places, base, own, other, used, width, first):
    rank = own.shape[0]
    args = [*grams, compress]
    return pl.pallas_call(
        functools.partial(filter_kernel, len(grams), first, "sketch", used, base),
        in_specs=[VMEM] * len(args) + [SMEM, ANY, ANY],
        out_shape=[
            jax.ShapeDtypeStruct((rank, 2 * rank), F32),
            jax.ShapeDtypeStruct((rank, width), BF16),
            jax.ShapeDtypeStruct((2 * rank, 2 * rank), F32),
        ],
        scratch_shapes=[
            pltpu.VMEM((2 * rank, width), BF16),
            pltpu.VMEM((rank, 2 * rank), F32),
            pltpu.SemaphoreType.DMA((2,)),
        ],
        compiler_params=PARAMS,
        name="sign_filter",
    )(*args, places, own, other)


def last_filter_call(grams, compress, places, base, first, share, pieces):
    rank = compress.shape[1]
    args = [*grams, compress]
    return pl.pallas_call(
        functools.partial(filter_kernel, len(grams), first, "last", pieces, base),
        in_specs=[VMEM] * len(args) + [SMEM],
        out_shape=jax.ShapeDtypeStruct((share * pieces, 2 * rank), F32),
        scratch_shapes=[pltpu.VMEM((rank, 2 * rank), F32)],
        compiler_params=PARAMS,
        cost_estimate=pl.CostEstimate(
            flops=50 * K_ITERS * (2 * rank) ** 3, bytes_accessed=0, transcendentals=0
        ),
        name="sign_filter",
    )(*args, places)


def mix_kernel(mixing, own, other, *out):
    rank = own.shape[0]
    rows, share = mixing.shape[0], out[0].shape[0]
    both = jnp.concatenate(split(mixing[...]), 0)
    width = own.shape[1]
    tile = next((t for t in (640, 512, 256, 128) if width % t == 0), width)
    for c in range(0, width, tile):
        span = slice(c, c + tile)
        part = dot(both, jnp.concatenate([own[:, span], other[:, span]], 0))
        part = part[:rows] + part[rows:]
        for i, piece in enumerate(out):
            piece[:, span] = part[i * share : (i + 1) * share].astype(piece.dtype)


def mix(mixing, own, other, pieces, dtype):
    shape = jax.ShapeDtypeStruct((mixing.shape[0] // pieces, own.shape[1]), dtype)
    return pl.pallas_call(
        mix_kernel,
        out_shape=[shape] * pieces,
        compiler_params=pltpu.CompilerParams(vmem_limit_bytes=16 * 2**20),
        name="mix",
    )(mixing, own, other)


def swap(value, axis, mask):
    count = lax.axis_size(axis)
    return lax.ppermute(value, axis, [(source, source ^ mask) for source in range(count)])


def gather_parts(value, axis):
    count = lax.axis_size(axis)
    if count > 4 or count & (count - 1):
        return [lax.psum(value.astype(F32), axis)]
    return [value] + [swap(value, axis, mask) for mask in range(1, count)]


def join_kernel(base, places, *refs):
    out = refs[-1]
    width = refs[0].shape[1]
    for i, piece in enumerate(refs[:-1]):
        out[:, pl.ds(pl.multiple_of(places[base + i], 128), width)] = piece[...]


def join(places, base, pieces):
    share, width = pieces[0].shape
    return pl.pallas_call(
        functools.partial(join_kernel, base),
        in_specs=[SMEM] + [VMEM] * len(pieces),
        out_shape=jax.ShapeDtypeStruct((share, width * len(pieces)), F32),
        compiler_params=pltpu.CompilerParams(vmem_limit_bytes=16 * 2**20),
        name="join",
    )(places, *pieces)


def on_device(record, fir_taps, gauge_lag, projector, compress):
    rows, cols = record.shape
    rank = projector.shape[1]
    count = lax.axis_size("tm")
    position = lax.axis_index("tm")
    depths = count.bit_length() - 1
    share = rank // count
    halo = lax.ppermute(
        record[rows - HALO :], "tm", [(source, source + 1) for source in range(count - 1)]
    )
    sketch = front(record, halo, gauge_lag, fir_taps[None, :], projector)

    widths = [cols]
    for depth in range(1, depths):
        widths.append(cols // 2 if cols % 256 == 0 else cols)
    narrowed = [depth for depth in range(depths - 1) if widths[depth + 1] < widths[depth]]
    assert narrowed == list(range(len(narrowed)))
    span = 2 ** len(narrowed)

    def bit_of(where, bit):
        return where // 2**bit % 2

    places = []
    for depth in range(depths):
        half = widths[depth] // 2 if depth in narrowed else 0
        flip = bit_of(position, depth)
        places += [flip * half, flip]
    places += [position ^ part for part in range(span)]
    joined = len(places)
    for part in range(span):
        places.append(sum([bit_of(position ^ part, bit) * (cols >> (bit + 1)) for bit in narrowed], 0))
    places = jnp.stack([position * 0 + place for place in places]).astype(jnp.int32)
    kept = ahead = None
    for depth in range(depths):
        first, last = depth == 0, depth == depths - 1
        mask = 2**depth
        here = widths[depth]
        if not last:
            other = swap(sketch, "tm", mask)
        if first:
            grams = gather_parts(pair_gram(sketch, other), "chan")
        else:
            packed, *kept = kept
            grams = [*kept, *ahead, swap(packed, "tm", mask)]
        if last:
            if not first:
                sketch = hold(sketch, *grams[-2:])
            other = swap(sketch, "tm", mask)
            mixing = last_filter_call(grams, compress, places, 2 * depth, first, share, span)
            pieces = mix(mixing, sketch, other, span, F32)
            break
        after = [] if first else [packed]
        part = ahead_gram(sketch, other, swap(sketch, "tm", 2 * mask), here, *after)
        if widths[depth + 1] == here and depth + 2 == depths:
            mixing, packed, level = level_filter_call(grams, compress, places, 2 * depth, first)
            (merged,) = mix(mixing, sketch, other, 1, BF16)
        else:
            mixing, merged, full = filter_call(
                grams, compress, places, 2 * depth, sketch, other, here, widths[depth + 1], first
            )
            packed, level = level_call(mixing, full)
        kept = packed, mixing, level
        for bit in [b for b in narrowed if b < depth]:
            part = add_after(part, swap(part, "tm", 2**bit), grams[-1])
        parts = gather_parts(part, "chan")
        total = sum(piece.astype(F32) for piece in parts).astype(BF16)
        ahead = [total, swap(total, "tm", mask)]
        sketch = merged
    if span == 1:
        return pieces[0]
    pieces = [pieces[0]] + [swap(piece, "tm", part) for part, piece in enumerate(pieces[1:], 1)]
    return join(places, joined, pieces)


def solution(mesh):
    return jax.shard_map(
        on_device,
        mesh=mesh,
        in_specs=(P("tm", "chan"), P(), P("chan"), P("tm", None), P()),
        out_specs=P("tm", "chan"),
        check_vma=False,
    )
```

```python
import functools

import jax
import jax.numpy as jnp
from jax import lax
from jax.experimental import pallas as pl
from jax.experimental.pallas import tpu as pltpu
from jax.sharding import PartitionSpec as P

TAPS = 64
GAUGE_MAX = 16
K_ITERS = 8
HALO = TAPS + GAUGE_MAX
BLOCK = 128
STEP = 16
CHUNK = 1024
EXTRA = 16
F32 = jnp.float32
BF16 = jnp.bfloat16
ANY = pl.BlockSpec(memory_space=pl.ANY)
HBM = pl.BlockSpec(memory_space=pltpu.HBM)
SMEM = pl.BlockSpec(memory_space=pltpu.SMEM)
VMEM = pl.BlockSpec(memory_space=pltpu.VMEM)
PARAMS = pltpu.CompilerParams(vmem_limit_bytes=40 * 2**20)


def dot(a, b):
    return jnp.dot(a, b, preferred_element_type=F32)


def dot_nt(a, b):
    return lax.dot_general(a, b, (((1,), (1,)), ((), ())), preferred_element_type=F32)


def split(a):
    high = a.astype(BF16)
    return high, (a - high.astype(F32)).astype(BF16)


def dot3_split(ah, al, bh, bl):
    rows = ah.shape[0]
    wide = dot(jnp.concatenate([ah, al], 0), bh)
    return wide[:rows] + (wide[rows:] + dot(ah, bl))


def dot3(a, b):
    return dot3_split(*split(a), *split(b))


def dot3_nt(a, b):
    ah, al = split(a)
    bh, bl = split(b)
    return dot_nt(ah, bh) + (dot_nt(ah, bl) + dot_nt(al, bh))


def eye_mask(n):
    row = lax.broadcasted_iota(jnp.int32, (n, n), 0)
    col = lax.broadcasted_iota(jnp.int32, (n, n), 1)
    return row == col


def one_hot(shape, place):
    row = lax.broadcasted_iota(jnp.int32, shape, 0)
    col = lax.broadcasted_iota(jnp.int32, shape, 1)
    return jnp.where(place(row) == col, 1.0, 0.0).astype(BF16)


def front_kernel(first, last, *refs):
    if first == 0:
        record, halo, lag, band, weights, begun, out, strain = refs
    else:
        record, lag_ref, taps_ref, projector_ref, out, band, head_weights, head = refs[:8]
        strain, weights, lag, taps, projector, sems = refs[8:]
        halo = begun = None

        @pl.when(pl.program_id(0) == 0)
        def _():
            sources, targets = (lag_ref, taps_ref, projector_ref), (lag, taps, projector)
            copies = [
                pltpu.make_async_copy(source, target, sems.at[i])
                for i, (source, target) in enumerate(zip(sources, targets))
            ]
            for copy in copies:
                copy.start()
            for copy in copies:
                copy.wait()
            turn = one_hot((TAPS, 256), lambda tap: TAPS - tap)
            line = dot(jnp.broadcast_to(taps[...], (8, TAPS)), turn)[0:1]
            line = jnp.broadcast_to(line, (BLOCK + GAUGE_MAX, 256))
            rolled = pltpu.roll(line, 0, 1, stride=1, stride_axis=0)[:, : BLOCK + HALO]
            order = one_hot((2 * BLOCK, BLOCK + GAUGE_MAX), lambda row: row // 8 + STEP * (row % 8))
            band[...] = dot(order, rolled.astype(BF16)).astype(BF16)
            order = one_hot((BLOCK, BLOCK), lambda row: row // 8 + STEP * (row % 8))
            for block in range(projector.shape[0] // BLOCK):
                part = slice(block * BLOCK, (block + 1) * BLOCK)
                weights[:, part] = dot(order, projector[part, :]).T.astype(BF16)
            head_weights[...] = weights[:, 0:BLOCK]

    cols = record.shape[1]
    lane = min(128, cols)
    lanes = cols // lane
    group = 256 if cols % 256 == 0 else lane
    total = None
    used = first * BLOCK
    if first > 0:
        head[...] = record[0:BLOCK, :]
    for block in range(first, last):
        start = block * BLOCK
        for g in range(0, cols, group):
            if block == 0:
                segment = jnp.concatenate([halo[:, g : g + group], record[0:BLOCK, g : g + group]], 0)
            else:
                segment = record[start - HALO : start + BLOCK, g : g + group]
            result = dot(band[...], segment)
            for c in range(0, group, lane):
                line = pl.program_id(0) * lanes + (g + c) // lane
                shift = GAUGE_MAX - lag[pl.ds(line, 1), :]
                wide = result[:, c : c + lane]
                picked = wide
                for step in (8, 4, 2, 1):
                    length = BLOCK + 8 * (step - 1)
                    picked = jnp.where(
                        (shift & step) != 0, picked[8 * step : 8 * step + length], picked[:length]
                    )
                strain[start : start + BLOCK, g + c : g + c + lane] = (wide[BLOCK:] - picked).astype(
                    BF16
                )
        done = start + BLOCK
        if done % CHUNK == 0 or block == last - 1:
            part = dot(weights[:, used:done], strain[used:done, :])
            total = part if total is None else total + part
            used = done
    if begun is None:
        out[...] = total
    else:
        out[...] = (total + begun[...]).astype(BF16)


def front_call(blocks, args, in_specs, out_specs, out_shape, scratch, steps, grant):
    return pl.pallas_call(
        functools.partial(front_kernel, *blocks),
        grid=(steps,),
        in_specs=in_specs,
        out_specs=out_specs,
        out_shape=out_shape,
        scratch_shapes=scratch,
        compiler_params=pltpu.CompilerParams(vmem_limit_bytes=grant * 2**20),
        name="front",
    )(*args)


def front(record, halo, lag, taps, projector):
    rows, cols = record.shape
    rank = projector.shape[1]
    lag = lag.reshape(cols // 128, 128) if cols % 128 == 0 else lag[None, :]
    whole = lambda a: pl.BlockSpec(a.shape, lambda i: (0, 0))
    columns = lambda count, tile: pl.BlockSpec((count, tile), lambda i: (0, i))
    tile = next((t for t in (1280, 640, 512, 256, 128) if cols % t == 0), cols)
    shapes = [
        jax.ShapeDtypeStruct((rank, cols), F32),
        jax.ShapeDtypeStruct((2 * BLOCK, BLOCK + HALO), BF16),
        jax.ShapeDtypeStruct((rank, BLOCK), BF16),
        jax.ShapeDtypeStruct((BLOCK, cols), BF16),
    ]
    begun, band, weights, head = front_call(
        (1, rows // BLOCK),
        (record, lag, taps, projector),
        [columns(rows, tile), HBM, HBM, HBM],
        [columns(rank, tile), whole(shapes[1]), whole(shapes[2]), columns(BLOCK, tile)],
        shapes,
        [
            pltpu.VMEM((rows, tile), BF16),
            pltpu.VMEM((rank, rows), BF16),
            pltpu.VMEM(lag.shape, lag.dtype),
            pltpu.VMEM(taps.shape, BF16),
            pltpu.VMEM(projector.shape, BF16),
            pltpu.SemaphoreType.DMA((3,)),
        ],
        cols // tile,
        48,
    )
    tile = cols
    return front_call(
        (0, 1),
        (head, halo, lag, band, weights, begun),
        [
            columns(BLOCK, tile),
            columns(HALO, tile),
            whole(lag),
            whole(band),
            whole(weights),
            columns(rank, tile),
        ],
        columns(rank, tile),
        jax.ShapeDtypeStruct((rank, cols), BF16),
        [pltpu.VMEM((BLOCK, tile), BF16)],
        cols // tile,
        32,
    )


def pair_kernel(own, other, out):
    rank = own.shape[0]
    a, b = own[...], other[...]
    aa, ab, bb = dot_nt(a, a), dot_nt(a, b), dot_nt(b, b)
    diag = eye_mask(rank)
    trace = jnp.sum(jnp.where(diag, aa + bb, 0.0), axis=(0, 1), keepdims=True)
    mean = trace / (2 * rank)
    aa = aa - jnp.where(diag, mean, 0.0)
    bb = bb - jnp.where(diag, mean, 0.0)
    row = lax.broadcasted_iota(jnp.int32, (rank, rank), 0)
    col = lax.broadcasted_iota(jnp.int32, (rank, rank), 1)
    out[0:rank, :] = jnp.where(row <= col, aa, bb).astype(BF16)
    out[rank : 2 * rank, :] = ab.astype(BF16)
    bottom = jnp.sum(jnp.where(diag, bb, 0.0), axis=0, keepdims=True)
    full = jnp.broadcast_to(mean, (EXTRA, rank))
    high = full.astype(BF16).astype(F32)
    mid = (full - high).astype(BF16).astype(F32)
    low = full - high - mid
    line = lax.broadcasted_iota(jnp.int32, (EXTRA, rank), 0)
    extra = jnp.where(line == 0, high, jnp.where(line == 1, mid, jnp.where(line == 2, low, 0.0)))
    out[2 * rank :, :] = jnp.where(line == 3, jnp.broadcast_to(bottom, (EXTRA, rank)), extra).astype(
        BF16
    )


def pair_gram(own, other):
    rank = own.shape[0]
    return pl.pallas_call(
        pair_kernel,
        out_shape=jax.ShapeDtypeStruct((2 * rank + EXTRA, rank), BF16),
        compiler_params=PARAMS,
        name="pair_gram",
    )(own, other)


def ahead_kernel(width, own, sibling, partner, *refs):
    out = refs[-1]
    rank = own.shape[0]
    there = partner[:, :width]
    out[0:rank, :] = dot_nt(own[:, :width], there).astype(out.dtype)
    out[rank:, :] = dot_nt(sibling[:, :width], there).astype(out.dtype)


def ahead_gram(own, sibling, partner, width, *after):
    rank = own.shape[0]
    return pl.pallas_call(
        functools.partial(ahead_kernel, width),
        in_specs=[VMEM] * 3 + [ANY] * len(after),
        out_shape=jax.ShapeDtypeStruct((2 * rank, rank), BF16),
        compiler_params=PARAMS,
        name="ahead_gram",
    )(own, sibling, partner, *after)


def summed(parts):
    total = parts[0][...].astype(F32)
    for part in parts[1:]:
        total = total + part[...].astype(F32)
    return total


def hold_kernel(*refs):
    pass


def hold(value, *until):
    return pl.pallas_call(
        hold_kernel,
        in_specs=[ANY] * (1 + len(until)),
        out_specs=ANY,
        out_shape=jax.ShapeDtypeStruct(value.shape, value.dtype),
        input_output_aliases={0: 0},
        compiler_params=pltpu.CompilerParams(vmem_limit_bytes=16 * 2**20),
        name="hold",
    )(value, *until)


def add_kernel(one, two, _, out):
    out[...] = (one[...].astype(F32) + two[...].astype(F32)).astype(BF16)


def add_after(one, two, after):
    return pl.pallas_call(
        add_kernel,
        in_specs=[VMEM, VMEM, ANY],
        out_shape=jax.ShapeDtypeStruct(one.shape, BF16),
        compiler_params=pltpu.CompilerParams(vmem_limit_bytes=16 * 2**20),
        name="add_after",
    )(one, two, after)


def square_of(aa, ab, bb):
    return jnp.concatenate(
        [jnp.concatenate([aa, ab], 1), jnp.concatenate([ab.T, bb], 1)], 0
    )


def first_gram(parts):
    total = summed(parts)
    rank = total.shape[1]
    both = total[0:rank]
    ab = total[rank : 2 * rank]
    extra = total[2 * rank :]
    mean = extra[0:1, 0:1] + extra[1:2, 0:1] + extra[2:3, 0:1]
    row = lax.broadcasted_iota(jnp.int32, (rank, rank), 0)
    col = lax.broadcasted_iota(jnp.int32, (rank, rank), 1)
    turned = both.T
    aa = jnp.where(row <= col, both, turned)
    bb = jnp.where(row > col, both, jnp.where(row < col, turned, extra[3:4, :]))
    return square_of(aa, ab, bb), mean


def later_gram(own_mix, own_level, ahead, sibling_ahead, other):
    rank = own_mix.shape[0]
    mine, theirs = ahead[...], sibling_ahead[...]
    cross = jnp.concatenate(
        [
            jnp.concatenate([mine[:rank], theirs[rank:]], 1),
            jnp.concatenate([mine[rank:], theirs[:rank]], 1),
        ],
        0,
    )
    high, low = split(own_mix[...])
    half = dot(high, cross) + dot(low, cross)
    high, low = split(half)
    place = other.shape[1] - 4 * rank
    other_mix = other[:, place : place + 2 * rank]
    ab = dot_nt(high, other_mix) + dot_nt(low, other_mix)
    place += 2 * rank
    other_level = other[:, place : place + rank].astype(F32) + other[:, place + rank :].astype(F32)
    gram = square_of(own_level[...], ab, other_level)
    diag = eye_mask(gram.shape[0])
    mean = jnp.sum(jnp.where(diag, gram, 0.0), axis=(0, 1), keepdims=True) / gram.shape[0]
    return gram - jnp.where(diag, mean, 0.0), mean


def filter_kernel(count, first, kind, used, base, *refs):
    grams, refs = refs[:count], refs[count:]
    compress, places, refs = refs[0], refs[1], refs[2:]
    last = kind == "last"
    rank = compress.shape[1]
    if last:
        mix_out, turned = refs
        share = mix_out.shape[0] // used
    elif kind == "level":
        mix_out, packed, level, turned = refs
    else:
        own, other, mix_out, sketch, whole, pair, turned, sems = refs
        width = pair.shape[1]
        if width < used:
            span = pl.ds(pl.multiple_of(places[base], 128), width)
        else:
            span = slice(0, width)
        copies = [
            pltpu.make_async_copy(
                source.at[:, span], pair.at[slice(i * rank, (i + 1) * rank)], sems.at[i]
            )
            for i, source in enumerate((own, other))
        ]
        for copy in copies:
            copy.start()
    flip = places[base + 1]
    for i in range(2):
        half = compress[pl.ds(pl.multiple_of((flip + i) % 2 * rank, 128), rank), :]
        turned[:, i * rank : (i + 1) * rank] = half.T
    if last:
        parts = [
            turned[pl.ds(pl.multiple_of(places[base + 2 + i] * share, 8), share), :]
            for i in range(used)
        ]
        compress_t = jnp.concatenate(parts, 0) if used > 1 else parts[0]
    else:
        compress_t = turned[...]
    gram, mean = first_gram(grams) if first else later_gram(*grams)
    size = gram.shape[0]
    eye = jnp.where(eye_mask(size), 1.0, 0.0)
    z = gram * lax.rsqrt(jnp.sum(gram * gram, axis=(0, 1), keepdims=True) + 1e-6)
    for step in range(K_ITERS):
        zh, zl = split(z)
        square = dot3_split(zh, zl, zh, zl)
        factor = split(1.5 * eye - 0.5 * square)
        if step < K_ITERS - 1:
            z = dot3_split(zh, zl, *factor)
        else:
            turn = dot3_split(*split(compress_t), zh, zl)
            mixing = 0.5 * (compress_t + dot3_split(*split(turn), *factor))
    mix_out[...] = mixing
    if last:
        return
    full = gram + mean * eye
    if kind == "level":
        pack_level(mixing, full, packed, level)
        return
    whole[...] = full
    for copy in copies:
        copy.wait()
    both = jnp.concatenate(split(mixing), 0)
    tile = next((t for t in (640, 512, 256, 128) if width % t == 0), width)
    for c in range(0, width, tile):
        part = dot(both, pair[:, c : c + tile])
        sketch[:, c : c + tile] = (part[:rank] + part[rank:]).astype(BF16)


def pack_level(mixing, full, packed, level):
    rank = mixing.shape[0]
    block = dot3_nt(dot3(mixing, full), mixing)
    level[...] = block
    packed[:, : 2 * rank] = mixing.astype(BF16)
    high, low = split(block)
    packed[:, 2 * rank : 3 * rank] = high
    packed[:, 3 * rank :] = low


def level_kernel(mixing, full, packed, level):
    pack_level(mixing[...], full[...], packed, level)


def level_shapes(rank):
    return [
        jax.ShapeDtypeStruct((rank, 4 * rank), BF16),
        jax.ShapeDtypeStruct((rank, rank), F32),
    ]


def level_call(mixing, full):
    return pl.pallas_call(
        level_kernel,
        out_shape=level_shapes(mixing.shape[0]),
        compiler_params=pltpu.CompilerParams(vmem_limit_bytes=16 * 2**20),
        name="level",
    )(mixing, full)


def level_filter_call(grams, compress, places, base, first):
    rank = compress.shape[1]
    args = [*grams, compress]
    return pl.pallas_call(
        functools.partial(filter_kernel, len(grams), first, "level", 0, base),
        in_specs=[VMEM] * len(args) + [SMEM],
        out_shape=[jax.ShapeDtypeStruct((rank, 2 * rank), F32), *level_shapes(rank)],
        scratch_shapes=[pltpu.VMEM((rank, 2 * rank), F32)],
        compiler_params=PARAMS,
        name="sign_filter",
    )(*args, places)


def filter_call(grams, compress, places, base, own, other, used, width, first):
    rank = own.shape[0]
    args = [*grams, compress]
    return pl.pallas_call(
        functools.partial(filter_kernel, len(grams), first, "sketch", used, base),
        in_specs=[VMEM] * len(args) + [SMEM, ANY, ANY],
        out_shape=[
            jax.ShapeDtypeStruct((rank, 2 * rank), F32),
            jax.ShapeDtypeStruct((rank, width), BF16),
            jax.ShapeDtypeStruct((2 * rank, 2 * rank), F32),
        ],
        scratch_shapes=[
            pltpu.VMEM((2 * rank, width), BF16),
            pltpu.VMEM((rank, 2 * rank), F32),
            pltpu.SemaphoreType.DMA((2,)),
        ],
        compiler_params=PARAMS,
        name="sign_filter",
    )(*args, places, own, other)


def last_filter_call(grams, compress, places, base, first, share, pieces):
    rank = compress.shape[1]
    args = [*grams, compress]
    return pl.pallas_call(
        functools.partial(filter_kernel, len(grams), first, "last", pieces, base),
        in_specs=[VMEM] * len(args) + [SMEM],
        out_shape=jax.ShapeDtypeStruct((share * pieces, 2 * rank), F32),
        scratch_shapes=[pltpu.VMEM((rank, 2 * rank), F32)],
        compiler_params=PARAMS,
        cost_estimate=pl.CostEstimate(
            flops=50 * K_ITERS * (2 * rank) ** 3, bytes_accessed=0, transcendentals=0
        ),
        name="sign_filter",
    )(*args, places)


def mix_kernel(mixing, own, other, *out):
    rank = own.shape[0]
    rows, share = mixing.shape[0], out[0].shape[0]
    both = jnp.concatenate(split(mixing[...]), 0)
    width = own.shape[1]
    tile = next((t for t in (640, 512, 256, 128) if width % t == 0), width)
    for c in range(0, width, tile):
        span = slice(c, c + tile)
        part = dot(both, jnp.concatenate([own[:, span], other[:, span]], 0))
        part = part[:rows] + part[rows:]
        for i, piece in enumerate(out):
            piece[:, span] = part[i * share : (i + 1) * share].astype(piece.dtype)


def mix(mixing, own, other, pieces, dtype):
    shape = jax.ShapeDtypeStruct((mixing.shape[0] // pieces, own.shape[1]), dtype)
    return pl.pallas_call(
        mix_kernel,
        out_shape=[shape] * pieces,
        compiler_params=pltpu.CompilerParams(vmem_limit_bytes=16 * 2**20),
        name="mix",
    )(mixing, own, other)


def swap(value, axis, mask):
    count = lax.axis_size(axis)
    return lax.ppermute(value, axis, [(source, source ^ mask) for source in range(count)])


def gather_parts(value, axis):
    count = lax.axis_size(axis)
    if count > 4 or count & (count - 1):
        return [lax.psum(value.astype(F32), axis)]
    return [value] + [swap(value, axis, mask) for mask in range(1, count)]


def join_kernel(base, places, *refs):
    out = refs[-1]
    width = refs[0].shape[1]
    for i, piece in enumerate(refs[:-1]):
        out[:, pl.ds(pl.multiple_of(places[base + i], 128), width)] = piece[...]


def join(places, base, pieces):
    share, width = pieces[0].shape
    return pl.pallas_call(
        functools.partial(join_kernel, base),
        in_specs=[SMEM] + [VMEM] * len(pieces),
        out_shape=jax.ShapeDtypeStruct((share, width * len(pieces)), F32),
        compiler_params=pltpu.CompilerParams(vmem_limit_bytes=16 * 2**20),
        name="join",
    )(places, *pieces)


def on_device(record, fir_taps, gauge_lag, projector, compress):
    rows, cols = record.shape
    rank = projector.shape[1]
    count = lax.axis_size("tm")
    position = lax.axis_index("tm")
    depths = count.bit_length() - 1
    share = rank // count
    halo = lax.ppermute(
        record[rows - HALO :], "tm", [(source, source + 1) for source in range(count - 1)]
    )
    sketch = front(record, halo, gauge_lag, fir_taps[None, :], projector)

    widths = [cols]
    for depth in range(1, depths):
        widths.append(cols // 2 if cols % 256 == 0 else cols)
    narrowed = [depth for depth in range(depths - 1) if widths[depth + 1] < widths[depth]]
    assert narrowed == list(range(len(narrowed)))
    span = 2 ** len(narrowed)

    def bit_of(where, bit):
        return where // 2**bit % 2

    places = []
    for depth in range(depths):
        half = widths[depth] // 2 if depth in narrowed else 0
        flip = bit_of(position, depth)
        places += [flip * half, flip]
    places += [position ^ part for part in range(span)]
    joined = len(places)
    for part in range(span):
        places.append(sum([bit_of(position ^ part, bit) * (cols >> (bit + 1)) for bit in narrowed], 0))
    places = jnp.stack([position * 0 + place for place in places]).astype(jnp.int32)
    kept = ahead = None
    for depth in range(depths):
        first, last = depth == 0, depth == depths - 1
        mask = 2**depth
        here = widths[depth]
        if not last:
            other = swap(sketch, "tm", mask)
        if first:
            grams = gather_parts(pair_gram(sketch, other), "chan")
        else:
            packed, *kept = kept
            grams = [*kept, *ahead, swap(packed, "tm", mask)]
        if last:
            if not first:
                sketch = hold(sketch, *grams[-2:])
            other = swap(sketch, "tm", mask)
            mixing = last_filter_call(grams, compress, places, 2 * depth, first, share, span)
            pieces = mix(mixing, sketch, other, span, F32)
            break
        after = [] if first else [packed]
        part = ahead_gram(sketch, other, swap(sketch, "tm", 2 * mask), here, *after)
        if widths[depth + 1] == here and depth + 2 == depths:
            mixing, packed, level = level_filter_call(grams, compress, places, 2 * depth, first)
            (merged,) = mix(mixing, sketch, other, 1, BF16)
        else:
            mixing, merged, full = filter_call(
                grams, compress, places, 2 * depth, sketch, other, here, widths[depth + 1], first
            )
            packed, level = level_call(mixing, full)
        kept = packed, mixing, level
        for bit in [b for b in narrowed if b < depth]:
            part = add_after(part, swap(part, "tm", 2**bit), grams[-1])
        parts = gather_parts(part, "chan")
        total = sum(piece.astype(F32) for piece in parts).astype(BF16)
        ahead = [total, swap(total, "tm", mask)]
        sketch = merged
    if span == 1:
        return pieces[0]
    pieces = [pieces[0]] + [swap(piece, "tm", part) for part, piece in enumerate(pieces[1:], 1)]
    return join(places, joined, pieces)


def solution(mesh):
    return jax.shard_map(
        on_device,
        mesh=mesh,
        in_specs=(P("tm", "chan"), P(), P("chan"), P("tm", None), P()),
        out_specs=P("tm", "chan"),
        check_vma=False,
    )
```
